32 devices in a mesh: groups: 2 (over y), space: 8 (over z, x), node: 2 (over core).
Axes of the slice: x: 2, y: 2, z: 4, core: 2. Of those that a mesh axis runs over, the one named last changes fastest.
Arguments:
- concentration: float32 [2, 64, 64, 512], P('node', ('groups', 'space')), parts along dimension 1, may hold values from -6 to 6
- adjoint_next: bfloat16 [2, 64, 64, 512], P('node', ('groups', 'space')), parts along dimension 1, may hold values from -6 to 6
- speed: bfloat16 [3, 64, 64, 512], P(None, ('groups', 'space')), parts along dimension 1, may hold values from 0.099609375 to 0.29882812
- direction_mask: int32 [3, 64, 64, 64], P(None, ('groups', 'space')), parts along dimension 1, may hold values 0 or 1
- decay_rate: bfloat16 [64, 64, 512], P(('groups', 'space')), parts along dimension 0, may hold values from 0.019897461 to 0.29882812
- control: float32 [64, 64, 512], P(('groups', 'space')), parts along dimension 0, may hold values from -6 to 6
- goal_weight: bfloat16 [64, 64, 512], P(('groups', 'space')), parts along dimension 0, may hold values from 0.25 to 5.25, as said below
- node_index: int32 [2, 8], P('node'), may hold values from 0 to 8
- weight_num: int32 [2], P('node'), may hold values from -8 to 24
- step_index: int32 [2], P('groups'), parts along dimension 0, may hold values from 0 to 63
Outputs:
- adjoint: float32 [2, 64, 64, 512], P('node', ('groups', 'space')), parts along dimension 1
- gradient: float32 [64, 64, 512], P(('groups', 'space'), None, 'node'), parts along dimension 0
- objective: float32 [2], P('groups'), parts along dimension 0
The draws below stay inside these ranges and needn't reach their ends.
There are 2 independent parts, one for each index of `groups`. The reference program is written for one: setup_inputs(seed, part) draws one part's arguments, and reference() takes and returns one part's arrays. A program takes and returns all parts, laid end to end along the dimension named above; an argument that names none is the same for every part. Nothing has to cross between parts.
Inputs may be any that keep to these rules, and one draw needn't show every extreme that they name: `node_index`: level indices of the nested rule. `weight_num`: signed weight numerators. `goal_weight`: positive weights.
All inputs are finite; a program needn't handle non-finite values. No bound on the sum of `direction_mask` on one device may be relied on, other than what follows from the above.
Results may differ from the reference program's by a relative error of at most 0.0003.
Values sent between devices are 32-bit elements; how exact they have to be, the bound alone decides.
No kernel may reach another device: no remote copies, remote signals or barrier semaphores. Data moves between devices by JAX's collectives and lax.ppermute only.
A program may use at most 64 MiB of HBM per device.

```python
import math
import jax
import jax.numpy as jnp
from jax import lax

NZ = 64
NY = 512
NPAR = 8
NX = 32
NODES = 2


def draw_goal_weight(key, part):
    key = jax.random.fold_in(key, 11)
    rising = 1.0 + 2.0 * jnp.arange(NX, dtype=jnp.float32) / max(NX - 1, 1)
    values = jax.random.uniform(key, (NX, NZ, NY), jnp.float32, 0.5, 1.5)
    return (rising[:, None, None] * values).astype(jnp.bfloat16)


def set_ends(result, rng, least, top_value):
    longest = result.shape.index(max(result.shape))
    spots = []
    for shift in (0, 1):
        where = [jax.random.randint(jax.random.fold_in(rng, axis), (), 0, length) for axis, length in enumerate(result.shape)]
        where[longest] = (where[longest] + shift) % result.shape[longest]
        spots.append(tuple(where))
    return result.at[spots[0]].set(least).at[spots[1]].set(top_value)


def steps_of(own_key, dims, cuts, least, high):
    loudness, own = 1.0, jax.random.fold_in(own_key, 6)
    for dim, parts in cuts:
        draws = jnp.exp(jax.random.uniform(jax.random.fold_in(own, dim), (parts,), jnp.float32, least / len(cuts), high / len(cuts)))
        loudness = loudness * jnp.repeat(draws, dims[dim] // parts).reshape([-1 if axis == dim else 1 for axis in range(len(dims))])
    return loudness


def scatter_about(rng, shape, deviation, reach, split=(), kind=jnp.bfloat16):
    array = deviation * jax.random.normal(rng, shape, jnp.float32)
    if split:
        array = array * steps_of(rng, shape, split, -0.22, 0.18)
    return jnp.clip(array, -reach, reach).astype(kind)


def setup_inputs(seed: int = 0, part: int = 0) -> dict:
    seeds = jax.random.split(jax.random.key(seed), 11)
    part_keys = jax.random.split(jax.random.fold_in(seeds[10], part), 11)
    concentration = scatter_about(part_keys[0], (NODES, NX, NZ, NY), 1.0, 6.0, ((0, 2), (1, 8)), jnp.float32)
    adjoint_next = scatter_about(part_keys[1], (NODES, NX, NZ, NY), 1.0, 6.0, ((0, 2), (1, 8)))
    speed = jnp.clip(0.099609375 + 0.19921875 * jax.random.uniform(part_keys[2], (3, NX, NZ, NY), jnp.float32) ** steps_of(part_keys[2], (3, NX, NZ, NY), ((1, 8),), -0.2, 0.2), 0.099609375, 0.29882812).astype(jnp.bfloat16)
    direction_mask = set_ends((jax.random.randint(part_keys[3], (3, NX, NZ, NY // 8), 0, 2) < 1).astype(jnp.int32), jax.random.fold_in(part_keys[3], 1), 0, 1)
    decay_rate = jnp.clip(jnp.exp(math.log(0.29882812) - 2.7092764 * jax.random.uniform(part_keys[4], (NX, NZ, NY), jnp.float32) ** steps_of(part_keys[4], (NX, NZ, NY), ((0, 8),), -0.2, 0.2)), 0.019897461, 0.29882812).astype(jnp.bfloat16)
    control = scatter_about(part_keys[5], (NX, NZ, NY), 1.0, 6.0, ((0, 8),), jnp.float32)
    goal_weight = draw_goal_weight(jax.random.fold_in(jax.random.fold_in(seeds[10], part), 71), part)
    node_index = set_ends(jax.random.randint(seeds[7], (NODES, NPAR), 0, 9), jax.random.fold_in(seeds[7], 1), 0, 8).astype(jnp.int32)
    weight_num = jax.random.randint(seeds[8], (NODES,), -8, 25).astype(jnp.int32)
    step_index = jax.random.randint(part_keys[9], (1,), 0, 64).astype(jnp.int32)
    return {"concentration": concentration, "adjoint_next": adjoint_next, "speed": speed, "direction_mask": direction_mask, "decay_rate": decay_rate, "control": control, "goal_weight": goal_weight, "node_index": node_index, "weight_num": weight_num, "step_index": step_index}


time_step = 0.6
variance_gain = 0.5
penalty = 0.1
weight_denominator = 16.0

def node_scales(node_index, step_index):
    points = -jnp.cos(math.pi * node_index.astype(jnp.float32) / 8.0)
    source_phase = 1.0 + 0.5 * jnp.sin(2.0 * math.pi * step_index.astype(jnp.float32)[0] / 64.0)
    first_axis = 1.0 + 0.3 * points[:, 0]
    second_axis = 1.0 + 0.3 * points[:, 1]
    third_axis = (1.0 + 0.3 * points[:, 2]) * (1.0 + 0.2 * points[:, 7])
    kappa = jnp.exp(0.5 * (points[:, 3] + 0.5 * points[:, 5]))
    source = (1.0 + 0.3 * points[:, 4] + 0.2 * points[:, 6]) * source_phase
    return jnp.stack([first_axis, second_axis, third_axis, kappa, source], axis=1)

def expand_sign(direction_mask):
    signs = direction_mask.astype(jnp.float32) * 2.0 - 1.0
    extent = signs.shape
    return jnp.broadcast_to(signs[..., None], extent + (8,)).reshape(extent[:-1] + (extent[-1] * 8,))

def tendency(extended, fields, scales):
    center = extended[:, 1:-1]
    padded = jnp.pad(center, ((0, 0), (0, 0), (1, 1), (1, 1)))
    lower = (extended[:, :-2], padded[:, :, :-2, 1:-1], padded[:, :, 1:-1, :-2])
    higher = (extended[:, 2:], padded[:, :, 2:, 1:-1], padded[:, :, 1:-1, 2:])
    advection = jnp.zeros_like(center)
    for component in range(3):
        velocity = fields[component][None] * scales[:, component, None, None, None]
        upwind = jnp.where(fields[3 + component][None] > 0, center - lower[component], center - higher[component])
        advection = advection + velocity * upwind
    reaction = fields[6][None] * scales[:, 3, None, None, None] * center
    return -advection - reaction + fields[7][None] * scales[:, 4, None, None, None]

def reference(concentration, adjoint_next, speed, direction_mask, decay_rate, control, goal_weight, node_index, weight_num, step_index):
    fixed = jnp.concatenate([speed.astype(jnp.float32), expand_sign(direction_mask), decay_rate.astype(jnp.float32)[None]], 0)
    scales = node_scales(node_index, step_index)
    weights = weight_num.astype(jnp.float32) / weight_denominator
    goal = goal_weight.astype(jnp.float32)

    def step(state, source_field, scale_row):
        fields = jnp.concatenate([fixed, source_field[None]], 0)

        def advance(value):
            extended = jnp.pad(value[None], ((0, 0), (1, 1), (0, 0), (0, 0)))
            return value + time_step * tendency(extended, fields, scale_row[None])[0]
        first_section = advance(state)
        second_section = 0.75 * state + 0.25 * advance(first_section)
        return state / 3.0 + 2.0 / 3.0 * advance(second_section)
    finals = lax.map(lambda pair: step(pair[0], control, pair[1]), (concentration, scales))
    weighted = weights[:, None, None, None] * finals
    first = lax.optimization_barrier(jnp.sum(weighted, 0))
    second = lax.optimization_barrier(jnp.sum(weighted * finals, 0))
    objective = jnp.reshape(jnp.mean(goal * (first + variance_gain * (second - first * first))), (1,))

    def backward(items):
        state, after, scale_row, weight, final_state = items
        terminal = after.astype(jnp.float32) + goal * weight * (1.0 + 2.0 * variance_gain * (final_state - first))
        _, pullback = jax.vjp(lambda value, source_field: step(value, source_field, scale_row), state, control)
        return pullback(terminal)
    adjoint, source_terms = lax.map(backward, (concentration, adjoint_next, scales, weights, finals))
    gradient = lax.optimization_barrier(jnp.sum(source_terms, 0)) + penalty * control
    return (adjoint, gradient, objective)
```

```python
import functools
import math

import jax
import jax.numpy as jnp
from jax import lax
from jax.experimental import pallas as pl
from jax.experimental.pallas import tpu as pltpu
from jax.sharding import PartitionSpec as P

time_step = 0.6
variance_gain = 0.5
penalty = 0.1
weight_denominator = 16.0

VMEM_LIMIT = 24 * 1024 * 1024
AXES = ("space", "node")


def node_scales(node_index, step_index):
    points = -jnp.cos(math.pi * node_index.astype(jnp.float32) / 8.0)
    source_phase = 1.0 + 0.5 * jnp.sin(2.0 * math.pi * step_index.astype(jnp.float32)[0] / 64.0)
    first_axis = 1.0 + 0.3 * points[:, 0]
    second_axis = 1.0 + 0.3 * points[:, 1]
    third_axis = (1.0 + 0.3 * points[:, 2]) * (1.0 + 0.2 * points[:, 7])
    kappa = jnp.exp(0.5 * (points[:, 3] + 0.5 * points[:, 5]))
    source = (1.0 + 0.3 * points[:, 4] + 0.2 * points[:, 6]) * source_phase
    return jnp.stack([first_axis, second_axis, third_axis, kappa, source], axis=1)


def roll(value, steps, axis):
    return pltpu.roll(value, steps % value.shape[axis], axis)


def in_plane(value, a, cy, cz, k):
    return a[1] * (cy[0, k] * roll(value, 1, 0) + cy[1, k] * roll(value, -1, 0)) + a[2] * (
        cz[0, k] * roll(value, 1, 1) + cz[1, k] * roll(value, -1, 1)
    )


def in_plane_back(value, a, cy, cz, k):
    return a[1] * (roll(cy[0, k] * value, -1, 0) + roll(cy[1, k] * value, 1, 0)) + a[2] * (
        roll(cz[0, k] * value, -1, 1) + roll(cz[1, k] * value, 1, 1)
    )


def rows_of(scal, j):
    return [scal[j, k] for k in range(6)]


def prepare(core, scal, speed, mask, decay, control, goal, own_adj, far_adj, cx, cy, cz, dg, edge, ctl, goals, adj, adj_out):
    me = core[0]
    rows, columns = speed.shape[2:]
    blocks = mask.shape[3]
    spread = (
        lax.broadcasted_iota(jnp.int32, (blocks, columns), 1) // (columns // blocks)
        == lax.broadcasted_iota(jnp.int32, (blocks, columns), 0)
    ).astype(jnp.bfloat16)
    row = lax.broadcasted_iota(jnp.int32, (rows, columns), 0)
    column = lax.broadcasted_iota(jnp.int32, (rows, columns), 1)
    flip = (me == 1).astype(jnp.float32)
    for k in range(2):
        at = me if k == 0 else 1 - me
        s, up = [], []
        for d in range(3):
            bits = mask[d, at].astype(jnp.float32).astype(jnp.bfloat16)
            up.append(jnp.dot(bits, spread, preferred_element_type=jnp.float32))
            s.append(speed[d, at].astype(jnp.float32))
        toward_outer = up[0] + flip - 2.0 * flip * up[0]
        outer = s[0] * toward_outer
        cx[0, k] = outer
        cx[1, k] = s[0] - outer
        if k == 0:
            edge[...] = outer
        lower = s[1] * up[1]
        cy[0, k] = jnp.where(row == 0, 0.0, lower)
        cy[1, k] = jnp.where(row == rows - 1, 0.0, s[1] - lower)
        lower = s[2] * up[2]
        cz[0, k] = jnp.where(column == 0, 0.0, lower)
        cz[1, k] = jnp.where(column == columns - 1, 0.0, s[2] - lower)
        rate = decay[at].astype(jnp.float32)
        for j in range(2):
            a = rows_of(scal, j)
            dg[j, k] = a[0] * s[0] + a[1] * s[1] + a[2] * s[2] + a[3] * rate
        ctl[k] = control[at]
        goals[k] = goal[at].astype(jnp.float32)
        adj[k] = own_adj[0, at].astype(jnp.float32)
        adj_out[k] = far_adj[0, 1 - at].astype(jnp.float32)


def first_stage(core, scal, own, far, own_halo, far_halo, cx, cy, cz, dg, ctl, msg, s1_in):
    me = core[0]
    outer, inner, beyond = 3 * me, 1 + me, 2 - me
    for j, (c, halo) in enumerate(((own, own_halo), (far, far_halo))):
        a = rows_of(scal, j)
        c_o, c_i = c[0, outer], c[0, inner]
        push_o, push_i = a[4] * ctl[0], a[4] * ctl[1]
        l_o = a[0] * (cx[0, 0] * halo[0] + cx[1, 0] * c_i) + in_plane(c_o, a, cy, cz, 0) - dg[j, 0] * c_o
        l_i = a[0] * (cx[0, 1] * c_o + cx[1, 1] * c[0, beyond]) + in_plane(c_i, a, cy, cz, 1) - dg[j, 1] * c_i
        s1_o = c_o + time_step * (l_o + push_o)
        s1_i = c_i + time_step * (l_i + push_i)
        s1_in[j] = s1_i
        msg[j, 0] = s1_o
        l_o = a[0] * (cx[1, 0] * s1_i) + in_plane(s1_o, a, cy, cz, 0) - dg[j, 0] * s1_o
        msg[j, 1] = 0.75 * c_o + 0.25 * (s1_o + time_step * (l_o + push_o))


def second_stage_inner(core, scal, own, far, msg, s1_in, s1_far, cx, cy, cz, dg, ctl, s2_in):
    inner = 1 + core[0]
    for j, c in enumerate((own, far)):
        a = rows_of(scal, j)
        s1_i = s1_in[j]
        l_i = a[0] * (cx[0, 1] * msg[j, 0] + cx[1, 1] * s1_far[1 - j]) + in_plane(s1_i, a, cy, cz, 1) - dg[j, 1] * s1_i
        s2_in[j] = 0.75 * c[0, inner] + 0.25 * (s1_i + time_step * (l_i + a[4] * ctl[1]))


def middle(core, scal, own, far, msg, halo, s2_in, s2_far, near_edge, cx, cy, cz, dg, ctl, goals, adj, adj_far, cost, term, msg3, pin):
    me = core[0]
    place = (3 * me, 1 + me)
    ahead, first, second = [], [0.0, 0.0], [0.0, 0.0]
    for j, c in enumerate((own, far)):
        a = rows_of(scal, j)
        s1_o = msg[j, 0]
        s2_o = msg[j, 1] + (0.25 * time_step * a[0]) * (cx[0, 0] * halo[1 - j, 0])
        s2_h = halo[1 - j, 1] + (0.25 * time_step * a[0]) * (near_edge[...] * s1_o)
        s2_i = s2_in[j]
        l_o = a[0] * (cx[0, 0] * s2_h + cx[1, 0] * s2_i) + in_plane(s2_o, a, cy, cz, 0) - dg[j, 0] * s2_o
        l_i = a[0] * (cx[0, 1] * s2_o + cx[1, 1] * s2_far[1 - j]) + in_plane(s2_i, a, cy, cz, 1) - dg[j, 1] * s2_i
        final = []
        for k, (s2, l) in enumerate(((s2_o, l_o), (s2_i, l_i))):
            f = c[0, place[k]] / 3.0 + 2.0 / 3.0 * (s2 + time_step * (l + a[4] * ctl[k]))
            final.append(f)
            weighted = a[5] * f
            first[k] = first[k] + weighted
            second[k] = second[k] + weighted * f
        ahead.append(final)
    total = sum(
        goals[k] * (first[k] + variance_gain * (second[k] - first[k] * first[k])) for k in range(2)
    )
    rows, columns = total.shape
    total = sum(total[8 * r : 8 * r + 8] for r in range(rows // 8))
    cost[...] = sum(total[:, 128 * k : 128 * k + 128] for k in range(columns // 128))
    for j in range(2):
        a = rows_of(scal, j)
        u = []
        for k in range(2):
            after = adj[k] if j == 0 else adj_far[k]
            t = after + goals[k] * a[5] * (1.0 + 2.0 * variance_gain * (ahead[j][k] - first[k]))
            term[j, k] = t
            u.append(2.0 / 3.0 * t)
        pin[j] = a[0] * (cx[1, 1] * u[1])
        msg3[j, 0] = a[0] * (cx[0, 0] * u[0])
        spread = a[0] * (cx[0, 1] * u[1]) + in_plane_back(u[0], a, cy, cz, 0) - dg[j, 0] * u[0]
        msg3[j, 1] = a[0] * cx[0, 0] * (u[0] + time_step * spread)


def back_inner(scal, term, pin_far, cx, cy, cz, dg, a2, a2_part, pin2):
    for j in range(2):
        a = rows_of(scal, j)
        u = [2.0 / 3.0 * term[j, k] for k in range(2)]
        spread = a[0] * (cx[0, 1] * u[1]) + in_plane_back(u[0], a, cy, cz, 0) - dg[j, 0] * u[0]
        a2_part[j] = u[0] + time_step * spread
        spread = a[0] * (cx[1, 0] * u[0]) + in_plane_back(u[1], a, cy, cz, 1) - dg[j, 1] * u[1] + pin_far[1 - j]
        a2_i = u[1] + time_step * spread
        a2[j] = a2_i
        pin2[j] = (0.25 * a[0]) * (cx[1, 1] * a2_i)


def back_outer(core, scal, term, msg3, halo, near_edge, a2, a2_part, pin_far, cx, cy, cz, dg, ctl, a2_o, a1, msg4, pin3, keep, give):
    sources = [0.0, 0.0]
    for j in range(2):
        a = rows_of(scal, j)
        second = [a2_part[j] + time_step * halo[1 - j, 0], a2[j]]
        a2_o[j] = second[0]
        u2 = [0.25 * second[k] for k in range(2)]
        arrived = 0.25 * (halo[1 - j, 1] + (time_step * a[0]) * (near_edge[...] * msg3[j, 0]))
        spread = a[0] * (cx[0, 1] * u2[1]) + in_plane_back(u2[0], a, cy, cz, 0) - dg[j, 0] * u2[0] + arrived
        a1_o = u2[0] + time_step * spread
        spread = a[0] * (cx[1, 0] * u2[0]) + in_plane_back(u2[1], a, cy, cz, 1) - dg[j, 1] * u2[1] + pin_far[1 - j]
        a1_i = u2[1] + time_step * spread
        a1[j, 0] = a1_o
        a1[j, 1] = a1_i
        msg4[j] = a[0] * (cx[0, 0] * a1_o)
        pin3[j] = a[0] * (cx[1, 1] * a1_i)
        for k, last in enumerate((a1_o, a1_i)):
            sources[k] = sources[k] + a[4] * (2.0 / 3.0 * term[j, k] + u2[k] + last)
    half = ctl.shape[2] // 2
    zero = core[0] == 0
    for k in range(2):
        gradient = time_step * sources[k] + penalty * ctl[k]
        low, high = gradient[:, :half], gradient[:, half:]
        keep[k] = jnp.where(zero, low, high)
        give[k] = jnp.where(zero, high, low)


def last_inner(core, scal, term, a2, a2_o, a1, pin_far, keep, taken, cx, cy, cz, dg, part, adj_in, adj_out, gradient):
    me = core[0]
    for j in range(2):
        a = rows_of(scal, j)
        x = [a1[j, 0], a1[j, 1]]
        spread = a[0] * (cx[0, 1] * x[1]) + in_plane_back(x[0], a, cy, cz, 0) - dg[j, 0] * x[0]
        part[j] = term[j, 0] / 3.0 + 0.75 * a2_o[j] + (x[0] + time_step * spread)
        spread = a[0] * (cx[1, 0] * x[0]) + in_plane_back(x[1], a, cy, cz, 1) - dg[j, 1] * x[1] + pin_far[1 - j]
        inner = term[j, 1] / 3.0 + 0.75 * a2[j] + (x[1] + time_step * spread)
        if j == 0:
            adj_in[...] = inner
        else:
            adj_out[...] = inner
    gradient[3 * me] = keep[0]
    gradient[1 + me] = keep[1]
    gradient[3 - 3 * me] = taken[0]
    gradient[2 - me] = taken[1]


def last_outer(part, halo, mine, give):
    mine[...] = part[0] + time_step * halo[1]
    give[...] = part[1] + time_step * halo[0]


def assemble(core, mine, taken, adj_in, adj_taken, out):
    me = core[0]
    out[0, 3 * me] = mine[...]
    out[0, 1 + me] = adj_in[...]
    out[0, 3 - 3 * me] = taken[...]
    out[0, 2 - me] = adj_taken[...]


def on_core(body, outs, scalars, arrays, hbm_out=(), name=None):
    out_shape = [
        jax.ShapeDtypeStruct(s, jnp.float32) if i in hbm_out else pltpu.VMEM(s, jnp.float32)
        for i, s in enumerate(outs)
    ]
    held = [pltpu.with_memory_space_constraint(x, pltpu.VMEM) for x in arrays]
    return pl.pallas_call(
        body,
        out_shape=out_shape,
        in_specs=[pl.BlockSpec(memory_space=pltpu.SMEM)] * len(scalars)
        + [pl.BlockSpec(memory_space=pltpu.VMEM)] * len(arrays),
        out_specs=[pl.BlockSpec(memory_space=pltpu.VMEM)] * len(outs),
        compiler_params=pltpu.CompilerParams(vmem_limit_bytes=VMEM_LIMIT),
        name=name or body.__name__,
    )(*scalars, *held)


def sum_everywhere(value, ranks):
    if ranks & (ranks - 1):
        return lax.psum(value, AXES)
    step = 1
    while step < ranks:
        value = value + lax.ppermute(value, AXES, [(i, i ^ step) for i in range(ranks)])
        step *= 2
    return value


def shards(
    concentration,
    adjoint_next,
    speed,
    direction_mask,
    decay_rate,
    control,
    goal_weight,
    node_index,
    weight_num,
    step_index,
):
    sections = lax.axis_size("space")
    ranks = sections * lax.axis_size("node")
    within = [(i, i ^ 1) for i in range(ranks)]
    across = [p for i in range(1, ranks - 1, 2) for p in ((i, i + 1), (i + 1, i))]
    swap = lambda x: lax.ppermute(x, AXES, within)
    pass_on = lambda x: lax.ppermute(x, AXES, across)

    _, layers, rows, columns = concentration.shape
    me = lax.axis_index("node").astype(jnp.int32)
    core = jnp.reshape(me, (1,))
    scales = node_scales(node_index, step_index)
    weights = weight_num.astype(jnp.float32)[:, None] / weight_denominator
    scal = jnp.concatenate([scales, weights, jnp.zeros((1, 2), jnp.float32)], 1)
    scal = jnp.concatenate([scal, swap(scal)], 0)

    far = swap(concentration)
    take = lambda x: lax.dynamic_slice_in_dim(x, 3 * me, 1, axis=1)[0]
    far_halo = pass_on(take(concentration))
    own_halo = pass_on(take(far))

    plane = (rows, columns)
    pair = (2,) + plane
    four = (2,) + pair
    specs = [
        pl.BlockSpec((3, 2, rows, columns), lambda g, c: (0, c[0], 0, 0)),
        pl.BlockSpec((3, 2, rows, direction_mask.shape[3]), lambda g, c: (0, c[0], 0, 0)),
        pl.BlockSpec((2, rows, columns), lambda g, c: (c[0], 0, 0)),
        pl.BlockSpec((2, rows, columns), lambda g, c: (c[0], 0, 0)),
        pl.BlockSpec((2, rows, columns), lambda g, c: (c[0], 0, 0)),
        pl.BlockSpec((1, 2, rows, columns), lambda g, c: (0, c[0], 0, 0)),
        pl.BlockSpec((1, 2, rows, columns), lambda g, c: (0, 1 - c[0], 0, 0)),
    ]
    shapes = [four, four, four, four, plane, pair, pair, pair, pair]
    cx, cy, cz, dg, edge, ctl, goals, adj, adj_out = pl.pallas_call(
        prepare,
        out_shape=[pltpu.VMEM(s, jnp.float32) for s in shapes],
        grid_spec=pltpu.PrefetchScalarGridSpec(
            num_scalar_prefetch=1,
            grid=(1,),
            in_specs=[pl.BlockSpec(memory_space=pltpu.SMEM)] + specs,
            out_specs=[pl.BlockSpec(memory_space=pltpu.VMEM)] * len(shapes),
        ),
        compiler_params=pltpu.CompilerParams(vmem_limit_bytes=VMEM_LIMIT),
        name="prepare",
    )(core, scal, speed, direction_mask, decay_rate, control, goal_weight, adjoint_next, adjoint_next)
    adj_far = swap(adj_out)
    near_edge = pass_on(edge)

    fields = [cx, cy, cz, dg]
    msg, s1_in = on_core(
        first_stage, [four, pair], [core, scal], [concentration, far, own_halo, far_halo] + fields + [ctl]
    )
    halo2 = pass_on(msg)
    s1_far = swap(s1_in)
    (s2_in,) = on_core(
        second_stage_inner, [pair], [core, scal], [concentration, far, msg, s1_in, s1_far] + fields + [ctl]
    )
    s2_far = swap(s2_in)
    cost, term, msg3, pin = on_core(
        middle,
        [(8, 128), four, four, pair],
        [core, scal],
        [concentration, far, msg, halo2, s2_in, s2_far, near_edge] + fields + [ctl, goals, adj, adj_far],
    )
    halo3 = pass_on(msg3)
    pin_far = swap(pin)
    a2, a2_part, pin2 = on_core(back_inner, [pair, pair, pair], [scal], [term, pin_far] + fields)
    pin2_far = swap(pin2)
    half = (2, rows, columns // 2)
    a2_o, a1, msg4, pin3, keep, give = on_core(
        back_outer,
        [pair, four, pair, pair, half, half],
        [core, scal],
        [term, msg3, halo3, near_edge, a2, a2_part, pin2_far] + fields + [ctl],
    )
    halo4 = pass_on(msg4)
    pin3_far = swap(pin3)
    taken = swap(give)
    part, adj_in, adj_give, gradient = on_core(
        last_inner,
        [pair, plane, plane, (layers, rows, columns // 2)],
        [core, scal],
        [term, a2, a2_o, a1, pin3_far, keep, taken] + fields,
        hbm_out=(3,),
    )
    adj_taken = swap(adj_give)
    mine, edge_give = on_core(last_outer, [plane, plane], [], [part, halo4])
    edge_taken = swap(edge_give)
    (adjoint,) = on_core(
        assemble, [(1, layers, rows, columns)], [core], [mine, edge_taken, adj_in, adj_taken], hbm_out=(0,)
    )
    cells = sections * layers * rows * columns
    objective = jnp.reshape(jnp.sum(sum_everywhere(cost, ranks)) / cells, (1,))
    return (adjoint, gradient, objective)


def solution(mesh):
    return jax.shard_map(
        shards,
        mesh=mesh,
        in_specs=(
            P("node", ("groups", "space"), None, None),
            P("node", ("groups", "space"), None, None),
            P(None, ("groups", "space"), None, None),
            P(None, ("groups", "space"), None, None),
            P(("groups", "space"), None, None),
            P(("groups", "space"), None, None),
            P(("groups", "space"), None, None),
            P("node", None),
            P("node"),
            P("groups"),
        ),
        out_specs=(
            P("node", ("groups", "space"), None, None),
            P(("groups", "space"), None, "node"),
            P("groups"),
        ),
        check_vma=False,
    )
```

```python
import functools
import math

import jax
import jax.numpy as jnp
from jax import lax
from jax.experimental import pallas as pl
from jax.experimental.pallas import tpu as pltpu
from jax.sharding import PartitionSpec as P

time_step = 0.6
variance_gain = 0.5
penalty = 0.1
weight_denominator = 16.0

VMEM_LIMIT = 24 * 1024 * 1024
AXES = ("space", "node")


def roll(value, steps, axis):
    return pltpu.roll(value, steps % value.shape[axis], axis)


def in_plane(value, a, cy, cz, k):
    return a[1] * (cy[0, k] * roll(value, 1, 0) + cy[1, k] * roll(value, -1, 0)) + a[2] * (
        cz[0, k] * roll(value, 1, 1) + cz[1, k] * roll(value, -1, 1)
    )


def in_plane_back(value, a, cy, cz, k):
    return a[1] * (roll(cy[0, k] * value, -1, 0) + roll(cy[1, k] * value, 1, 0)) + a[2] * (
        roll(cz[0, k] * value, -1, 1) + roll(cz[1, k] * value, 1, 1)
    )


def rows_of(scal, j):
    return [scal[j, k] for k in range(6)]


def node_scales(own_raw, far_raw, scal):
    lanes = own_raw.shape[1]
    lane = lax.broadcasted_iota(jnp.int32, (8, lanes), 1)
    row = lax.broadcasted_iota(jnp.int32, (8, lanes), 0)
    raw = jnp.where(row == 0, own_raw[...], far_raw[...])
    points = -jnp.cos(math.pi * raw / 8.0)
    phase = 1.0 + 0.5 * jnp.sin(2.0 * math.pi * raw / 64.0)
    factor = 1.0 + 0.3 * points
    third = factor * (1.0 + 0.2 * roll(points, -5, 1))
    kappa = jnp.exp(0.5 * (points + 0.5 * roll(points, -2, 1)))
    source = (factor + 0.2 * roll(points, -2, 1)) * roll(phase, -5, 1)
    weight = roll(raw, -3, 1) / weight_denominator
    for j in range(2):
        for k, value in enumerate((factor, factor, third, kappa, source, weight)):
            scal[j, k] = jnp.sum(jnp.where((lane == k) & (row == j), value, 0.0))


def prepare(core, own_raw, far_raw, speed, mask, decay, control, goal, own_adj, far_adj, scal, cx, cy, cz, dg, edge, ctl, goals, adj, adj_out):
    me = core[0]
    node_scales(own_raw, far_raw, scal)
    rows, columns = speed.shape[2:]
    blocks = mask.shape[3]
    spread = (
        lax.broadcasted_iota(jnp.int32, (blocks, columns), 1) // (columns // blocks)
        == lax.broadcasted_iota(jnp.int32, (blocks, columns), 0)
    ).astype(jnp.bfloat16)
    row = lax.broadcasted_iota(jnp.int32, (rows, columns), 0)
    column = lax.broadcasted_iota(jnp.int32, (rows, columns), 1)
    flip = (me == 1).astype(jnp.float32)
    for k in range(2):
        at = me if k == 0 else 1 - me
        s, up = [], []
        for d in range(3):
            bits = mask[d, at].astype(jnp.float32).astype(jnp.bfloat16)
            up.append(jnp.dot(bits, spread, preferred_element_type=jnp.float32))
            s.append(speed[d, at].astype(jnp.float32))
        toward_outer = up[0] + flip - 2.0 * flip * up[0]
        outer = s[0] * toward_outer
        cx[0, k] = outer
        cx[1, k] = s[0] - outer
        if k == 0:
            edge[...] = outer
        lower = s[1] * up[1]
        cy[0, k] = jnp.where(row == 0, 0.0, lower)
        cy[1, k] = jnp.where(row == rows - 1, 0.0, s[1] - lower)
        lower = s[2] * up[2]
        cz[0, k] = jnp.where(column == 0, 0.0, lower)
        cz[1, k] = jnp.where(column == columns - 1, 0.0, s[2] - lower)
        rate = decay[at].astype(jnp.float32)
        for j in range(2):
            a = rows_of(scal, j)
            dg[j, k] = a[0] * s[0] + a[1] * s[1] + a[2] * s[2] + a[3] * rate
        ctl[k] = control[at]
        goals[k] = goal[at].astype(jnp.float32)
        adj[k] = own_adj[0, at].astype(jnp.float32)
        adj_out[k] = far_adj[0, 1 - at].astype(jnp.float32)


def first_stage(core, scal, own, far, cx, cy, cz, dg, ctl, base, base_q, s1_in):
    me = core[0]
    for j, c in enumerate((own, far)):
        a = rows_of(scal, j)
        c_o, c_i = c[0, 3 * me], c[0, 1 + me]
        push_o, push_i = a[4] * ctl[0], a[4] * ctl[1]
        l_i = a[0] * (cx[0, 1] * c_o + cx[1, 1] * c[0, 2 - me]) + in_plane(c_i, a, cy, cz, 1) - dg[j, 1] * c_i
        s1_i = c_i + time_step * (l_i + push_i)
        s1_in[j] = s1_i
        l_o = a[0] * (cx[1, 0] * c_i) + in_plane(c_o, a, cy, cz, 0) - dg[j, 0] * c_o
        base[j] = c_o + time_step * (l_o + push_o)
        base_q[j] = 0.75 * c_o + (0.25 * time_step) * (a[0] * (cx[1, 0] * s1_i) + push_o)


def first_edge(j, scal, halo, base, base_q, cx, cy, cz, dg, msg):
    a = rows_of(scal, j)
    s1_o = base[j] + (time_step * a[0]) * (cx[0, 0] * halo[0])
    msg[0] = s1_o
    msg[1] = base_q[j] + 0.25 * (s1_o + time_step * (in_plane(s1_o, a, cy, cz, 0) - dg[j, 0] * s1_o))


def second_inner(core, scal, own, far, msg_own, msg_far, s1_in, s1_far, cx, cy, cz, dg, ctl, s2_in):
    for j, (c, msg) in enumerate(((own, msg_own), (far, msg_far))):
        a = rows_of(scal, j)
        s1_i = s1_in[j]
        l_i = a[0] * (cx[0, 1] * msg[0] + cx[1, 1] * s1_far[1 - j]) + in_plane(s1_i, a, cy, cz, 1) - dg[j, 1] * s1_i
        s2_in[j] = 0.75 * c[0, 1 + core[0]] + 0.25 * (s1_i + time_step * (l_i + a[4] * ctl[1]))


def third_stage(core, scal, own, far, msg_own, msg_far, s2_in, s2_far, near_edge, cx, cy, cz, dg, ctl, base):
    me = core[0]
    for j, (c, msg) in enumerate(((own, msg_own), (far, msg_far))):
        a = rows_of(scal, j)
        q, s2_i = msg[1], s2_in[j]
        back = (0.25 * time_step * a[0]) * (near_edge[...] * msg[0])
        l_o = a[0] * (cx[0, 0] * back + cx[1, 0] * s2_i) + in_plane(q, a, cy, cz, 0) - dg[j, 0] * q
        l_i = a[0] * (cx[0, 1] * q + cx[1, 1] * s2_far[1 - j]) + in_plane(s2_i, a, cy, cz, 1) - dg[j, 1] * s2_i
        base[j, 0] = c[0, 3 * me] / 3.0 + 2.0 / 3.0 * (q + time_step * (l_o + a[4] * ctl[0]))
        base[j, 1] = c[0, 1 + me] / 3.0 + 2.0 / 3.0 * (s2_i + time_step * (l_i + a[4] * ctl[1]))


def finals(j, scal, halo, base, cx, cy, cz, dg):
    a = rows_of(scal, j)
    step = (0.25 * time_step * a[0]) * (cx[0, 0] * halo[0])
    change = in_plane(step, a, cy, cz, 0) - dg[j, 0] * step + a[0] * (cx[0, 0] * halo[1])
    outer = base[j, 0] + 2.0 / 3.0 * (step + time_step * change)
    inner = base[j, 1] + (2.0 / 3.0 * time_step * a[0]) * (cx[0, 1] * step)
    return outer, inner


def third_edge(scal, halo, base, cx, cy, cz, dg, final):
    final[0], final[1] = finals(0, scal, halo, base, cx, cy, cz, dg)


def back_edge(j, final, first, after, scal, cx, cy, cz, dg, goals, term, msg, partial):
    a = rows_of(scal, j)
    u = []
    for k in range(2):
        t = after[k] + goals[k] * a[5] * (1.0 + 2.0 * variance_gain * (final[k] - first[k]))
        term[k] = t
        u.append(2.0 / 3.0 * t)
    msg[0] = a[0] * (cx[0, 0] * u[0])
    spread = a[0] * (cx[0, 1] * u[1]) + in_plane_back(u[0], a, cy, cz, 0) - dg[j, 0] * u[0]
    value = u[0] + time_step * spread
    partial[...] = value
    msg[1] = a[0] * (cx[0, 0] * value)
    return u


def turn_far(scal, halo, base, final_own, cx, cy, cz, dg, goals, after, final, term, msg, partial):
    final[0], final[1] = finals(1, scal, halo, base, cx, cy, cz, dg)
    first = [scal[0, 5] * final_own[k] + scal[1, 5] * final[k] for k in range(2)]
    back_edge(1, final, first, after, scal, cx, cy, cz, dg, goals, term, msg, partial)


def turn_own(scal, final_own, final_far, cx, cy, cz, dg, goals, after, term_far, term, msg, partial, cost, pin):
    first, total = [], 0.0
    for k in range(2):
        own, far = scal[0, 5] * final_own[k], scal[1, 5] * final_far[k]
        first.append(own + far)
        second = own * final_own[k] + far * final_far[k]
        total = total + goals[k] * (first[k] + variance_gain * (second - first[k] * first[k]))
    u = back_edge(0, final_own, first, after, scal, cx, cy, cz, dg, goals, term, msg, partial)
    rows, columns = total.shape
    total = sum(total[8 * r : 8 * r + 8] for r in range(rows // 8))
    cost[...] = sum(total[:, 128 * k : 128 * k + 128] for k in range(columns // 128))
    pin[0] = scal[0, 0] * (cx[1, 1] * u[1])
    pin[1] = scal[1, 0] * (cx[1, 1] * (2.0 / 3.0 * term_far[1]))


def back_inner(scal, term_own, term_far, pin_far, cx, cy, cz, dg, a2, pin2):
    for j, term in enumerate((term_own, term_far)):
        a = rows_of(scal, j)
        u = [2.0 / 3.0 * term[k] for k in range(2)]
        spread = a[0] * (cx[1, 0] * u[0]) + in_plane_back(u[1], a, cy, cz, 1) - dg[j, 1] * u[1] + pin_far[1 - j]
        a2_i = u[1] + time_step * spread
        a2[j] = a2_i
        pin2[j] = (0.25 * a[0]) * (cx[1, 1] * a2_i)


def back_second(scal, msg_own, msg_far, partial_own, partial_far, a2, pin_far, near_edge, cx, cy, cz, dg, base):
    for j, (msg, partial) in enumerate(((msg_own, partial_own), (msg_far, partial_far))):
        a = rows_of(scal, j)
        u_o, u_i = 0.25 * partial[...], 0.25 * a2[j]
        back = (0.25 * time_step * a[0]) * (near_edge[...] * msg[0])
        spread = a[0] * (cx[0, 1] * u_i) + in_plane_back(u_o, a, cy, cz, 0) - dg[j, 0] * u_o + back
        base[j, 0] = u_o + time_step * spread
        spread = a[0] * (cx[1, 0] * u_o) + in_plane_back(u_i, a, cy, cz, 1) - dg[j, 1] * u_i + pin_far[1 - j]
        base[j, 1] = u_i + time_step * spread


def second_back_edge(j, scal, halo, base, cx, cy, cz, dg, a1_o, msg):
    a = rows_of(scal, j)
    step = (0.25 * time_step) * halo[0]
    value = base[j, 0] + step + time_step * (in_plane_back(step, a, cy, cz, 0) - dg[j, 0] * step + 0.25 * halo[1])
    a1_o[...] = value
    msg[0] = a[0] * (cx[0, 0] * value)


def close(core, scal, terms, partials, halos, a1s, a2, base, cx, cy, cz, dg, ctl, pin3, keep, give, part, a1_in):
    sources = [0.0, 0.0]
    for j in range(2):
        a = rows_of(scal, j)
        term, halo, a1_o = terms[j], halos[j], a1s[j][...]
        a1_i = base[j, 1] + (0.25 * time_step * time_step * a[0]) * (cx[1, 0] * halo[0])
        a2_o = partials[j][...] + time_step * halo[0]
        a1_in[j] = a1_i
        pin3[j] = a[0] * (cx[1, 1] * a1_i)
        for k, (u2, last) in enumerate(((0.25 * a2_o, a1_o), (0.25 * a2[j], a1_i))):
            sources[k] = sources[k] + a[4] * (2.0 / 3.0 * term[k] + u2 + last)
        spread = a[0] * (cx[0, 1] * a1_i) + in_plane_back(a1_o, a, cy, cz, 0) - dg[j, 0] * a1_o
        part[j] = term[0] / 3.0 + 0.75 * a2_o + (a1_o + time_step * spread)
    half = ctl.shape[2] // 2
    zero = core[0] == 0
    for k in range(2):
        gradient = time_step * sources[k] + penalty * ctl[k]
        low, high = gradient[:, :half], gradient[:, half:]
        keep[k] = jnp.where(zero, low, high)
        give[k] = jnp.where(zero, high, low)


def close_all(core, scal, term_own, term_far, partial_own, partial_far, halo_own, halo_far, a1_own, a1_far, *rest):
    close(core, scal, (term_own, term_far), (partial_own, partial_far), (halo_own, halo_far), (a1_own, a1_far), *rest)


def last_inner(core, scal, term_own, term_far, a2, a1_own, a1_far, a1_in, pin_far, keep, taken, cx, cy, cz, dg, adj_in, adj_out, gradient):
    me = core[0]
    for j, (term, a1_o, out) in enumerate(((term_own, a1_own, adj_in), (term_far, a1_far, adj_out))):
        a = rows_of(scal, j)
        x = a1_in[j]
        spread = a[0] * (cx[1, 0] * a1_o[...]) + in_plane_back(x, a, cy, cz, 1) - dg[j, 1] * x + pin_far[1 - j]
        out[...] = term[1] / 3.0 + 0.75 * a2[j] + (x + time_step * spread)
    gradient[3 * me] = keep[0]
    gradient[1 + me] = keep[1]
    gradient[3 - 3 * me] = taken[0]
    gradient[2 - me] = taken[1]


def last_outer(part, halo, give):
    give[...] = part[1] + time_step * halo[0]


def assemble(core, part, halo, taken, adj_in, adj_taken, out):
    me = core[0]
    out[0, 3 * me] = part[0] + time_step * halo[0]
    out[0, 1 + me] = adj_in[...]
    out[0, 3 - 3 * me] = taken[...]
    out[0, 2 - me] = adj_taken[...]


def on_core(body, outs, scalars, arrays, hbm_out=(), after=(), name=None):
    out_shape = [
        jax.ShapeDtypeStruct(s, jnp.float32) if i in hbm_out else pltpu.VMEM(s, jnp.float32)
        for i, s in enumerate(outs)
    ]
    held = [pltpu.with_memory_space_constraint(x, pltpu.SMEM) for x in scalars]
    held += [pltpu.with_memory_space_constraint(x, pltpu.VMEM) for x in arrays]
    count, waits = len(held), len(after)

    def run(*refs):
        body(*refs[:count], *refs[count + waits :])

    return pl.pallas_call(
        run,
        out_shape=out_shape,
        in_specs=[pl.BlockSpec(memory_space=pltpu.SMEM)] * len(scalars)
        + [pl.BlockSpec(memory_space=pltpu.VMEM)] * len(arrays)
        + [pl.BlockSpec(memory_space=pl.ANY)] * waits,
        out_specs=[pl.BlockSpec(memory_space=pltpu.VMEM)] * len(outs),
        compiler_params=pltpu.CompilerParams(vmem_limit_bytes=VMEM_LIMIT),
        name=name or body.__name__,
    )(*held, *after)


def shards(
    concentration,
    adjoint_next,
    speed,
    direction_mask,
    decay_rate,
    control,
    goal_weight,
    node_index,
    weight_num,
    step_index,
):
    sections = lax.axis_size("space")
    ranks = sections * lax.axis_size("node")
    within = [(i, i ^ 1) for i in range(ranks)]
    across = [p for i in range(1, ranks - 1, 2) for p in ((i, i + 1), (i + 1, i))]
    swap = lambda x: lax.ppermute(x, AXES, within)
    pass_on = lambda x: lax.ppermute(x, AXES, across)

    _, layers, rows, columns = concentration.shape
    me = lax.axis_index("node").astype(jnp.int32)
    core = jnp.reshape(me, (1,))
    raw = jnp.concatenate(
        [
            node_index.astype(jnp.float32),
            weight_num.astype(jnp.float32)[:, None],
            step_index.astype(jnp.float32)[:, None],
            jnp.zeros((1, 118), jnp.float32),
        ],
        1,
    )
    far_raw = swap(raw)

    far = swap(concentration)
    take = lambda x: lax.dynamic_slice_in_dim(x, 3 * me, 1, axis=1)[0]
    far_halo = pass_on(take(concentration))
    own_halo = pass_on(take(far))

    plane = (rows, columns)
    pair = (2,) + plane
    four = (2,) + pair
    specs = [
        pl.BlockSpec(memory_space=pltpu.VMEM),
        pl.BlockSpec(memory_space=pltpu.VMEM),
        pl.BlockSpec((3, 2, rows, columns), lambda g, c: (0, c[0], 0, 0)),
        pl.BlockSpec((3, 2, rows, direction_mask.shape[3]), lambda g, c: (0, c[0], 0, 0)),
        pl.BlockSpec((2, rows, columns), lambda g, c: (c[0], 0, 0)),
        pl.BlockSpec((2, rows, columns), lambda g, c: (c[0], 0, 0)),
        pl.BlockSpec((2, rows, columns), lambda g, c: (c[0], 0, 0)),
        pl.BlockSpec((1, 2, rows, columns), lambda g, c: (0, c[0], 0, 0)),
        pl.BlockSpec((1, 2, rows, columns), lambda g, c: (0, 1 - c[0], 0, 0)),
    ]
    shapes = [four, four, four, four, plane, pair, pair, pair, pair]
    far_off = [
        pltpu.with_memory_space_constraint(x, pltpu.HBM)
        for x in (speed, direction_mask, decay_rate, control, goal_weight, adjoint_next, adjoint_next)
    ]
    scal, cx, cy, cz, dg, edge, ctl, goals, adj, adj_out = pl.pallas_call(
        prepare,
        out_shape=[pltpu.SMEM((2, 8), jnp.float32)] + [pltpu.VMEM(s, jnp.float32) for s in shapes],
        grid_spec=pltpu.PrefetchScalarGridSpec(
            num_scalar_prefetch=1,
            grid=(1,),
            in_specs=specs,
            out_specs=[pl.BlockSpec(memory_space=pltpu.SMEM)]
            + [pl.BlockSpec(memory_space=pltpu.VMEM)] * len(shapes),
        ),
        compiler_params=pltpu.CompilerParams(vmem_limit_bytes=VMEM_LIMIT),
        name="prepare",
    )(core, raw, far_raw, *far_off)
    near_edge = pass_on(edge)
    adj_far = swap(adj_out)

    fields = [cx, cy, cz, dg]
    both = [core, scal]
    states = [concentration, far]
    base, base_q, s1_in = on_core(first_stage, [pair, pair, pair], both, states + fields + [ctl])
    s1_far = swap(s1_in)
    edge_of = lambda j, halo: on_core(
        functools.partial(first_edge, j), [pair], [scal], [halo, base, base_q] + fields, name="first_edge"
    )[0]
    msg_far = edge_of(1, far_halo)
    halo2_own = pass_on(msg_far)
    msg_own = edge_of(0, own_halo)
    halo2_far = pass_on(msg_own)

    msgs = [msg_own, msg_far]
    (s2_in,) = on_core(second_inner, [pair], both, states + msgs + [s1_in, s1_far] + fields + [ctl])
    s2_far = swap(s2_in)
    (base,) = on_core(third_stage, [four], both, states + msgs + [s2_in, s2_far, near_edge] + fields + [ctl])
    (final_own,) = on_core(third_edge, [pair], [scal], [halo2_own, base] + fields)
    final_far, term_far, msg3_far, partial_far = on_core(
        turn_far, [pair, pair, pair, plane], [scal], [halo2_far, base, final_own] + fields + [goals, adj_far]
    )
    halo3_own = pass_on(msg3_far)
    term_own, msg3_own, partial_own, cost, pin = on_core(
        turn_own,
        [pair, pair, plane, (8, 128), pair],
        [scal],
        [final_own, final_far] + fields + [goals, adj, term_far],
    )
    halo3_far = pass_on(msg3_own)
    pin_far = swap(pin)
    terms, partials = [term_own, term_far], [partial_own, partial_far]
    a2, pin2 = on_core(back_inner, [pair, pair], [scal], terms + [pin_far] + fields)
    pin2_far = swap(pin2)
    (base,) = on_core(
        back_second, [four], [scal], [msg3_own, msg3_far] + partials + [a2, pin2_far, near_edge] + fields
    )
    edge_of = lambda j, halo: on_core(
        functools.partial(second_back_edge, j),
        [plane, (1,) + plane],
        [scal],
        [halo, base] + fields,
        name="second_back_edge",
    )
    a1_own, msg4_own = edge_of(0, halo3_own)
    halo4_far = pass_on(msg4_own)
    a1_far, msg4_far = edge_of(1, halo3_far)
    halo4_own = pass_on(msg4_far)
    half = (2, rows, columns // 2)
    pin3, keep, give, part, a1_in = on_core(
        close_all,
        [pair, half, half, pair, pair],
        both,
        terms + partials + [halo3_own, halo3_far, a1_own, a1_far, a2, base] + fields + [ctl],
    )
    pin3_far = swap(pin3)
    taken = swap(give)
    adj_in, adj_give, gradient = on_core(
        last_inner,
        [plane, plane, (layers, rows, columns // 2)],
        both,
        terms + [a2, a1_own, a1_far, a1_in, pin3_far, keep, taken] + fields,
        hbm_out=(2,),
    )
    adj_taken = swap(adj_give)
    (edge_give,) = on_core(last_outer, [plane], [], [part, halo4_far])
    edge_taken = swap(edge_give)
    (adjoint,) = on_core(
        assemble,
        [(1, layers, rows, columns)],
        [core],
        [part, halo4_own, edge_taken, adj_in, adj_taken],
        hbm_out=(0,),
    )

    if ranks & (ranks - 1):
        cost = lax.psum(cost, AXES)
    else:
        steps = [1 << k for k in range(ranks.bit_length() - 1)]
        for step in steps[:1] + steps[2:] + steps[1:2]:
            cost = cost + lax.ppermute(cost, AXES, [(i, i ^ step) for i in range(ranks)])
    cells = sections * layers * rows * columns
    objective = jnp.reshape(jnp.sum(cost) / cells, (1,))
    return (adjoint, gradient, objective)


def solution(mesh):
    return jax.shard_map(
        shards,
        mesh=mesh,
        in_specs=(
            P("node", ("groups", "space"), None, None),
            P("node", ("groups", "space"), None, None),
            P(None, ("groups", "space"), None, None),
            P(None, ("groups", "space"), None, None),
            P(("groups", "space"), None, None),
            P(("groups", "space"), None, None),
            P(("groups", "space"), None, None),
            P("node", None),
            P("node"),
            P("groups"),
        ),
        out_specs=(
            P("node", ("groups", "space"), None, None),
            P(("groups", "space"), None, "node"),
            P("groups"),
        ),
        check_vma=False,
    )
```

```python
import functools
import math

import jax
import jax.numpy as jnp
from jax import lax
from jax.experimental import pallas as pl
from jax.experimental.pallas import tpu as pltpu
from jax.sharding import PartitionSpec as P

time_step = 0.6
variance_gain = 0.5
penalty = 0.1
weight_denominator = 16.0

VMEM_LIMIT = 24 * 1024 * 1024
AXES = ("space", "node")
LONG = 40


def roll(value, steps, axis):
    return pltpu.roll(value, steps % value.shape[axis], axis)


def in_plane(value, a, cy, cz, k):
    return a[1] * (cy[0, k] * roll(value, 1, 0) + cy[1, k] * roll(value, -1, 0)) + a[2] * (
        cz[0, k] * roll(value, 1, 1) + cz[1, k] * roll(value, -1, 1)
    )


def in_plane_back(value, a, cy, cz, k):
    return a[1] * (roll(cy[0, k] * value, -1, 0) + roll(cy[1, k] * value, 1, 0)) + a[2] * (
        roll(cz[0, k] * value, -1, 1) + roll(cz[1, k] * value, 1, 1)
    )


def rows_of(scal, j):
    return [scal[j, k] for k in range(6)]


def node_scales(own_index, far_index, own_weight, far_weight, step_index, scal):
    lane = lax.broadcasted_iota(jnp.int32, (8, 128), 1)
    row = lax.broadcasted_iota(jnp.int32, (8, 128), 0)
    raw = jnp.zeros((8, 128), jnp.int32)
    for j, (index, weight) in enumerate(((own_index, own_weight), (far_index, far_weight))):
        for k, number in enumerate([index[0, k] for k in range(8)] + [weight[0], step_index[0]]):
            raw = jnp.where((lane == k) & (row == j), number, raw)
    raw = raw.astype(jnp.float32)
    points = -jnp.cos(math.pi * raw / 8.0)
    phase = 1.0 + 0.5 * jnp.sin(2.0 * math.pi * raw / 64.0)
    factor = 1.0 + 0.3 * points
    third = factor * (1.0 + 0.2 * roll(points, -5, 1))
    kappa = jnp.exp(0.5 * (points + 0.5 * roll(points, -2, 1)))
    source = (factor + 0.2 * roll(points, -2, 1)) * roll(phase, -5, 1)
    weight = roll(raw, -3, 1) / weight_denominator
    for j in range(2):
        for k, value in enumerate((factor, factor, third, kappa, source, weight)):
            scal[j, k] = jnp.sum(jnp.where((lane == k) & (row == j), value, 0.0))


def prepare(core, own_index, far_index, own_weight, far_weight, step_index, speed, mask, decay, control, goal, adjoint, scal, cx, cy, cz, dg, edge, ctl, goals, adj, adj_out_o, adj_out_i):
    me = core[0]
    node_scales(own_index, far_index, own_weight, far_weight, step_index, scal)
    rows, columns = speed.shape[2:]
    blocks = mask.shape[3]
    spread = (
        lax.broadcasted_iota(jnp.int32, (blocks, columns), 1) // (columns // blocks)
        == lax.broadcasted_iota(jnp.int32, (blocks, columns), 0)
    ).astype(jnp.bfloat16)
    row = lax.broadcasted_iota(jnp.int32, (rows, columns), 0)
    column = lax.broadcasted_iota(jnp.int32, (rows, columns), 1)
    flip = (me == 1).astype(jnp.float32)
    for k, at in enumerate((3 * me, 1 + me, 2 - me)):
        s, up = [], []
        for d in range(3):
            bits = mask[d, at].astype(jnp.float32).astype(jnp.bfloat16)
            up.append(jnp.dot(bits, spread, preferred_element_type=jnp.float32))
            s.append(speed[d, at].astype(jnp.float32))
        toward_outer = up[0] + flip - 2.0 * flip * up[0]
        outer = s[0] * toward_outer
        cx[0, k] = outer
        cx[1, k] = s[0] - outer
        if k == 0:
            edge[...] = outer
        lower = s[1] * up[1]
        cy[0, k] = jnp.where(row == 0, 0.0, lower)
        cy[1, k] = jnp.where(row == rows - 1, 0.0, s[1] - lower)
        lower = s[2] * up[2]
        cz[0, k] = jnp.where(column == 0, 0.0, lower)
        cz[1, k] = jnp.where(column == columns - 1, 0.0, s[2] - lower)
        rate = decay[at].astype(jnp.float32)
        for j in range(2):
            a = rows_of(scal, j)
            dg[j, k] = a[0] * s[0] + a[1] * s[1] + a[2] * s[2] + a[3] * rate
        ctl[k] = control[at]
        if k < 2:
            goals[k] = goal[at].astype(jnp.float32)
            adj[k] = adjoint[0, at].astype(jnp.float32)
    adj_out_o[...] = adjoint[0, 3 - 3 * me].astype(jnp.float32)
    adj_out_i[...] = adjoint[0, 2 - me].astype(jnp.float32)


def first_stage(core, scal, own, far, cx, cy, cz, dg, ctl, base, base_q, s1_in, s1_next):
    me = core[0]
    for j, c in enumerate((own, far)):
        a = rows_of(scal, j)
        c_o, c_i, c_n, c_f = c[0, 3 * me], c[0, 1 + me], c[0, 2 - me], c[0, 3 - 3 * me]
        push = [a[4] * ctl[k] for k in range(3)]
        l_i = a[0] * (cx[0, 1] * c_o + cx[1, 1] * c_n) + in_plane(c_i, a, cy, cz, 1) - dg[j, 1] * c_i
        s1_i = c_i + time_step * (l_i + push[1])
        s1_in[j] = s1_i
        l_o = a[0] * (cx[1, 0] * c_i) + in_plane(c_o, a, cy, cz, 0) - dg[j, 0] * c_o
        base[j] = c_o + time_step * (l_o + push[0])
        base_q[j] = 0.75 * c_o + (0.25 * time_step) * (a[0] * (cx[1, 0] * s1_i) + push[0])
        l_n = a[0] * (cx[0, 2] * c_i + cx[1, 2] * c_f) + in_plane(c_n, a, cy, cz, 2) - dg[j, 2] * c_n
        s1_next[j] = c_n + time_step * (l_n + push[2])


def first_edge(j, scal, halo, base, base_q, cx, cy, cz, dg, msg):
    a = rows_of(scal, j)
    s1_o = base[j] + (time_step * a[0]) * (cx[0, 0] * halo[0])
    msg[0] = s1_o
    msg[1] = base_q[j] + 0.25 * (s1_o + time_step * (in_plane(s1_o, a, cy, cz, 0) - dg[j, 0] * s1_o))


def second_inner(core, scal, own, far, msg_own, msg_far, s1_in, s1_next, cx, cy, cz, dg, ctl, s2_own, s2_far):
    for j, (c, msg, out) in enumerate(((own, msg_own, s2_own), (far, msg_far, s2_far))):
        a = rows_of(scal, j)
        s1_i = s1_in[j]
        l_i = a[0] * (cx[0, 1] * msg[0] + cx[1, 1] * s1_next[j]) + in_plane(s1_i, a, cy, cz, 1) - dg[j, 1] * s1_i
        out[...] = 0.75 * c[0, 1 + core[0]] + 0.25 * (s1_i + time_step * (l_i + a[4] * ctl[1]))


def third_stage(core, scal, own, far, msg_own, msg_far, s2_own, s2_far, next_own, next_far, near_edge, cx, cy, cz, dg, ctl, base):
    me = core[0]
    parts = ((own, msg_own, s2_own, next_own), (far, msg_far, s2_far, next_far))
    for j, (c, msg, s2, s2_next) in enumerate(parts):
        a = rows_of(scal, j)
        q, s2_i = msg[1], s2[...]
        back = (0.25 * time_step * a[0]) * (near_edge[...] * msg[0])
        l_o = a[0] * (cx[0, 0] * back + cx[1, 0] * s2_i) + in_plane(q, a, cy, cz, 0) - dg[j, 0] * q
        l_i = a[0] * (cx[0, 1] * q + cx[1, 1] * s2_next[...]) + in_plane(s2_i, a, cy, cz, 1) - dg[j, 1] * s2_i
        base[j, 0] = c[0, 3 * me] / 3.0 + 2.0 / 3.0 * (q + time_step * (l_o + a[4] * ctl[0]))
        base[j, 1] = c[0, 1 + me] / 3.0 + 2.0 / 3.0 * (s2_i + time_step * (l_i + a[4] * ctl[1]))


def finals(j, scal, halo, base, cx, cy, cz, dg):
    a = rows_of(scal, j)
    step = (0.25 * time_step * a[0]) * (cx[0, 0] * halo[0])
    change = in_plane(step, a, cy, cz, 0) - dg[j, 0] * step + a[0] * (cx[0, 0] * halo[1])
    outer = base[j, 0] + 2.0 / 3.0 * (step + time_step * change)
    inner = base[j, 1] + (2.0 / 3.0 * time_step * a[0]) * (cx[0, 1] * step)
    return outer, inner


def third_edge(scal, halo, base, cx, cy, cz, dg, final):
    final[0], final[1] = finals(0, scal, halo, base, cx, cy, cz, dg)


def back_edge(j, final, first, after, scal, cx, cy, cz, dg, goals, term, msg, partial):
    a = rows_of(scal, j)
    u = []
    for k in range(2):
        t = after[k] + goals[k] * a[5] * (1.0 + 2.0 * variance_gain * (final[k] - first[k]))
        term[k] = t
        u.append(2.0 / 3.0 * t)
    msg[0] = a[0] * (cx[0, 0] * u[0])
    spread = a[0] * (cx[0, 1] * u[1]) + in_plane_back(u[0], a, cy, cz, 0) - dg[j, 0] * u[0]
    value = u[0] + time_step * spread
    partial[...] = value
    msg[1] = a[0] * (cx[0, 0] * value)


def turn_far(scal, halo, base, final_own, cx, cy, cz, dg, goals, after_o, after_i, final, term, msg, partial):
    final[0], final[1] = finals(1, scal, halo, base, cx, cy, cz, dg)
    first = [scal[0, 5] * final_own[k] + scal[1, 5] * final[k] for k in range(2)]
    after = (after_o[...], after_i[...])
    back_edge(1, final, first, after, scal, cx, cy, cz, dg, goals, term, msg, partial)


def turn_own(scal, final_own, final_far, cx, cy, cz, dg, goals, after, term, msg, partial):
    first = [scal[0, 5] * final_own[k] + scal[1, 5] * final_far[k] for k in range(2)]
    back_edge(0, final_own, first, after, scal, cx, cy, cz, dg, goals, term, msg, partial)


def put(refs, values):
    start, whole = 0, jnp.concatenate(values, 0)
    for ref in refs:
        ref[...] = whole[start : start + ref.shape[0]]
        start += ref.shape[0]


def get(refs, count):
    whole = jnp.concatenate([ref[...] for ref in refs], 0)
    rows = whole.shape[0] // count
    return [whole[rows * k : rows * k + rows] for k in range(count)]


def cut(rows, pieces):
    tiles = rows // 8
    return [8 * (tiles // pieces + (k < tiles % pieces)) for k in range(pieces)]


def turn_inner(scal, final_own, final_far, term_own, term_far, cx, cy, cz, dg, goals, cost, part, *pins):
    total = 0.0
    for k in range(2):
        own, far = scal[0, 5] * final_own[k], scal[1, 5] * final_far[k]
        first = own + far
        second = own * final_own[k] + far * final_far[k]
        total = total + goals[k] * (first + variance_gain * (second - first * first))
    rows, columns = total.shape
    total = sum(total[8 * r : 8 * r + 8] for r in range(rows // 8))
    cost[...] = sum(total[:, 128 * k : 128 * k + 128] for k in range(columns // 128))
    products = []
    for j, term in enumerate((term_own, term_far)):
        a = rows_of(scal, j)
        u = [2.0 / 3.0 * term[k] for k in range(2)]
        spread = a[0] * (cx[1, 0] * u[0]) + in_plane_back(u[1], a, cy, cz, 1) - dg[j, 1] * u[1]
        value = u[1] + time_step * spread
        part[j] = value
        products += [a[0] * (cx[1, 1] * u[1]), a[0] * (cx[1, 1] * value)]
    put(pins, products)


def back_second(scal, msg_own, msg_far, partial_own, partial_far, part, near_edge, cx, cy, cz, dg, *rest):
    (cost, cost_far), (base, a2, total) = rest[:2], rest[-3:]
    count = (len(rest) - 5) // 2
    mine, theirs = get(rest[2 : 2 + count], 4), get(rest[2 + count : -3], 4)
    total[...] = cost[...] + cost_far[...]
    for j, (msg, partial) in enumerate(((msg_own, partial_own), (msg_far, partial_far))):
        a = rows_of(scal, j)
        pin, pin2 = theirs[2 - 2 * j], theirs[3 - 2 * j]
        pin2 = 0.25 * (pin2 + (time_step * a[0]) * (cx[0, 2] * mine[2 * j]))
        a2_i = part[j] + time_step * pin
        a2[j] = a2_i
        u_o, u_i = 0.25 * partial[...], 0.25 * a2_i
        back = (0.25 * time_step * a[0]) * (near_edge[...] * msg[0])
        spread = a[0] * (cx[0, 1] * u_i) + in_plane_back(u_o, a, cy, cz, 0) - dg[j, 0] * u_o + back
        base[j, 0] = u_o + time_step * spread
        spread = a[0] * (cx[1, 0] * u_o) + in_plane_back(u_i, a, cy, cz, 1) - dg[j, 1] * u_i + pin2
        base[j, 1] = u_i + time_step * spread


def second_back_edge(j, scal, halo, base, cx, cy, cz, dg, a1_o, msg):
    a = rows_of(scal, j)
    step = (0.25 * time_step) * halo[0]
    value = base[j, 0] + step + time_step * (in_plane_back(step, a, cy, cz, 0) - dg[j, 0] * step + 0.25 * halo[1])
    a1_o[...] = value
    msg[...] = a[0] * (cx[0, 0] * value)


def close(core, scal, term_own, term_far, partial_own, partial_far, halo_own, halo_far, a1_own, a1_far, a2, base, cx, cy, cz, dg, ctl, keep, part, *out):
    give, send = out[0], out[1:]
    sources = [0.0, 0.0]
    parts = ((term_own, partial_own, halo_own, a1_own), (term_far, partial_far, halo_far, a1_far))
    for j, (term, partial, halo, a1) in enumerate(parts):
        a = rows_of(scal, j)
        x = [a1[...], base[j, 1] + (0.25 * time_step * time_step * a[0]) * (cx[1, 0] * halo[0])]
        a2_o = partial[...] + time_step * halo[0]
        for k, second in enumerate((a2_o, a2[j])):
            sources[k] = sources[k] + a[4] * (2.0 / 3.0 * term[k] + 0.25 * second + x[k])
        spread = a[0] * (cx[0, 1] * x[1]) + in_plane_back(x[0], a, cy, cz, 0) - dg[j, 0] * x[0]
        outer = term[0] / 3.0 + 0.75 * a2_o + (x[0] + time_step * spread)
        spread = a[0] * (cx[1, 0] * x[0]) + in_plane_back(x[1], a, cy, cz, 1) - dg[j, 1] * x[1]
        inner = term[1] / 3.0 + 0.75 * a2[j] + (x[1] + time_step * spread)
        pin = a[0] * (cx[1, 1] * x[1])
        if j == 0:
            part[0], part[1], part[2] = outer, inner, pin
        else:
            put(send, [outer, inner, pin])
    half = ctl.shape[2] // 2
    zero = core[0] == 0
    for k in range(2):
        gradient = time_step * sources[k] + penalty * ctl[k]
        low, high = gradient[:, :half], gradient[:, half:]
        keep[k] = jnp.where(zero, low, high)
        give[k] = jnp.where(zero, high, low)


def place_gradient(core, keep, taken, gradient):
    me = core[0]
    gradient[3 * me] = keep[0]
    gradient[1 + me] = keep[1]
    gradient[3 - 3 * me] = taken[0]
    gradient[2 - me] = taken[1]


def last_edge(halo, halo_far, part, outer, add):
    outer[...] = part[0] + time_step * halo[...]
    add[...] = time_step * halo_far[...]


def assemble(cells, core, part, outer, add, cost, *rest):
    taken, (out, objective) = get(rest[:-2], 3), rest[-2:]
    me = core[0]
    out[0, 3 * me] = outer[...]
    out[0, 1 + me] = part[1] + time_step * taken[2]
    out[0, 3 - 3 * me] = taken[0] + add[...]
    out[0, 2 - me] = taken[1] + time_step * part[2]
    objective[0] = jnp.sum(cost[...]) / cells


def on_core(body, outs, scalars, arrays, hbm_out=(), smem_out=(), after=(), cost=0, name=None):
    hbm_out = tuple(hbm_out) + tuple(smem_out)
    out_shape = [
        jax.ShapeDtypeStruct(s, jnp.float32) if i in hbm_out else pltpu.VMEM(s, jnp.float32)
        for i, s in enumerate(outs)
    ]
    held = [pltpu.with_memory_space_constraint(x, pltpu.SMEM) for x in scalars]
    held += [pltpu.with_memory_space_constraint(x, pltpu.VMEM) for x in arrays]
    count, waits = len(held), len(after)

    def run(*refs):
        body(*refs[:count], *refs[count + waits :])

    return pl.pallas_call(
        run,
        out_shape=out_shape,
        in_specs=[pl.BlockSpec(memory_space=pltpu.SMEM)] * len(scalars)
        + [pl.BlockSpec(memory_space=pltpu.VMEM)] * len(arrays)
        + [pl.BlockSpec(memory_space=pl.ANY)] * waits,
        out_specs=[
            pl.BlockSpec(memory_space=pltpu.SMEM if i in smem_out else pltpu.VMEM) for i in range(len(outs))
        ],
        compiler_params=pltpu.CompilerParams(vmem_limit_bytes=VMEM_LIMIT),
        cost_estimate=pl.CostEstimate(flops=cost * 1_000_000_000, bytes_accessed=cost * 3_000_000, transcendentals=0) if cost else None,
        name=name or body.__name__,
    )(*held, *after)


def shards(
    concentration,
    adjoint_next,
    speed,
    direction_mask,
    decay_rate,
    control,
    goal_weight,
    node_index,
    weight_num,
    step_index,
):
    sections = lax.axis_size("space")
    ranks = sections * lax.axis_size("node")
    within = [(i, i ^ 1) for i in range(ranks)]
    across = [p for i in range(1, ranks - 1, 2) for p in ((i, i + 1), (i + 1, i))]
    along = [p for i in range(0, ranks - 2, 2) for p in ((i + 1, i + 3), (i + 2, i))]

    def swap(x, what):
        with jax.named_scope("swap_" + what):
            return lax.ppermute(x, AXES, within)

    def pass_on(x, what, pairs=across):
        with jax.named_scope("pass_" + what):
            return lax.ppermute(x, AXES, pairs)

    _, layers, rows, columns = concentration.shape
    me = lax.axis_index("node").astype(jnp.int32)
    core = jnp.reshape(me, (1,))
    far_index, far_weight = swap(node_index, "node_index"), swap(weight_num, "weight_num")

    far = swap(concentration, "state")
    take = lambda x: lax.dynamic_slice_in_dim(x, 3 * me, 1, axis=1)[0]
    far_halo = pass_on(take(concentration), "state_own")
    own_halo = pass_on(take(far), "state_far")

    plane = (rows, columns)
    pair, three = (2,) + plane, (3,) + plane
    four, six = (2,) + pair, (2,) + three
    sides = (2, rows, columns // 2)
    shapes = [six, six, six, six, plane, three, pair, pair, plane, plane]
    far_off = [
        pltpu.with_memory_space_constraint(x, pltpu.HBM)
        for x in (speed, direction_mask, decay_rate, control, goal_weight, adjoint_next)
    ]
    scal, cx, cy, cz, dg, edge, ctl, goals, adj, adj_out_o, adj_out_i = pl.pallas_call(
        prepare,
        out_shape=[pltpu.SMEM((2, 8), jnp.float32)] + [pltpu.VMEM(s, jnp.float32) for s in shapes],
        in_specs=[pl.BlockSpec(memory_space=pltpu.SMEM)] * 6 + [pl.BlockSpec(memory_space=pltpu.VMEM)] * 6,
        out_specs=[pl.BlockSpec(memory_space=pltpu.SMEM)] + [pl.BlockSpec(memory_space=pltpu.VMEM)] * len(shapes),
        compiler_params=pltpu.CompilerParams(vmem_limit_bytes=VMEM_LIMIT),
        name="prepare",
    )(core, node_index, far_index, weight_num, far_weight, step_index, *far_off)
    near_edge = pass_on(edge, "edge")
    after_o, after_i = swap(adj_out_o, "after_o"), swap(adj_out_i, "after_i")

    fields = [cx, cy, cz, dg]
    both = [core, scal]
    states = [concentration, far]
    base, base_q, s1_in, s1_next = on_core(first_stage, [pair] * 4, both, states + fields + [ctl])
    edge_of = lambda j, halo, after=(): on_core(
        functools.partial(first_edge, j), [pair], [scal], [halo, base, base_q] + fields, after=after, cost=LONG, name="first_edge"
    )[0]
    msg_far = edge_of(1, far_halo)
    halo2_own = pass_on(msg_far, "stage2_far")
    msg_own = edge_of(0, own_halo)
    halo2_far = pass_on(msg_own, "stage2_own")

    msgs = [msg_own, msg_far]
    s2 = list(on_core(second_inner, [plane] * 2, both, states + msgs + [s1_in, s1_next] + fields + [ctl], after=[near_edge, after_o, after_i]))
    s2_next = [swap(s2[1], "s2_far"), swap(s2[0], "s2_own")]
    (base,) = on_core(third_stage, [four], both, states + msgs + s2 + s2_next + [near_edge] + fields + [ctl])
    (final_own,) = on_core(third_edge, [pair], [scal], [halo2_own, base] + fields)
    final_far, term_far, msg3_far, partial_far = on_core(
        turn_far, [pair, pair, pair, plane], [scal], [halo2_far, base, final_own] + fields + [goals, after_o, after_i]
    )
    halo3_own = pass_on(msg3_far, "back2_far")
    term_own, msg3_own, partial_own = on_core(
        turn_own, [pair, pair, plane], [scal], [final_own, final_far] + fields + [goals, adj]
    )
    halo3_far = pass_on(msg3_own, "back2_own")
    terms, partials = [term_own, term_far], [partial_own, partial_far]
    cost, part, *pins = on_core(
        turn_inner, [(8, 128), pair] + [(r, columns) for r in cut(4 * rows, 3)], [scal], [final_own, final_far] + terms + fields + [goals]
    )
    theirs = [swap(x, "pin") for x in pins]
    base, a2, cost = on_core(
        back_second,
        [four, pair, (8, 128)],
        [scal],
        [msg3_own, msg3_far] + partials + [part, near_edge] + fields + [cost, swap(cost, "goal_sum")] + pins + theirs,
    )
    sums = [cost]
    if sections & (sections - 1):
        sums.append(lax.psum(cost, "space"))
    else:
        steps = [1 << k for k in range(sections.bit_length() - 1)]
        for step in steps[1:] + steps[:1]:
            with jax.named_scope("goal_sum"):
                sums.append(sums[-1] + lax.ppermute(sums[-1], "space", [(i, i ^ step) for i in range(sections)]))
    sum_at = lambda k: sums[min(k, len(sums) - 1)]

    edge_of = lambda j, halo, last: on_core(
        functools.partial(second_back_edge, j),
        [plane, plane],
        [scal],
        [halo, base] + fields,
        after=[last],
        cost=LONG,
        name="second_back_edge",
    )
    a1_own, msg4_own = edge_of(0, halo3_own, sum_at(1))
    halo4_far = pass_on(msg4_own, "back1_own", along)
    a1_far, msg4_far = edge_of(1, halo3_far, a1_own)
    halo4_own = pass_on(msg4_far, "back1_far")
    keep, part, *out = on_core(
        close,
        [sides, three, sides] + [(r, columns) for r in cut(3 * rows, 2)],
        both,
        terms + partials + [halo3_own, halo3_far, a1_own, a1_far, a2, base] + fields + [ctl],
        after=[sum_at(2)],
        cost=LONG,
    )
    parts = [swap(x, "adjoint") for x in out[1:]]
    taken = swap(out[0], "gradient")
    (gradient,) = on_core(
        place_gradient, [(layers, rows, columns // 2)], [core], [keep, taken], hbm_out=(0,)
    )
    outer, add = on_core(last_edge, [plane] * 2, [], [halo4_own, halo4_far, part], after=[sums[-1]], cost=LONG)
    adjoint, objective = on_core(
        functools.partial(assemble, sections * layers * rows * columns),
        [(1, layers, rows, columns), (1,)],
        [core],
        [part, outer, add, sums[-1]] + parts,
        hbm_out=(0,),
        smem_out=(1,),
        name="assemble",
    )
    return (adjoint, gradient, objective)


def solution(mesh):
    return jax.shard_map(
        shards,
        mesh=mesh,
        in_specs=(
            P("node", ("groups", "space"), None, None),
            P("node", ("groups", "space"), None, None),
            P(None, ("groups", "space"), None, None),
            P(None, ("groups", "space"), None, None),
            P(("groups", "space"), None, None),
            P(("groups", "space"), None, None),
            P(("groups", "space"), None, None),
            P("node", None),
            P("node"),
            P("groups"),
        ),
        out_specs=(
            P("node", ("groups", "space"), None, None),
            P(("groups", "space"), None, "node"),
            P("groups"),
        ),
        check_vma=False,
    )
```

```python
import functools
import math

import jax
import jax.numpy as jnp
from jax import lax
from jax.experimental import pallas as pl
from jax.experimental.pallas import tpu as pltpu
from jax.sharding import PartitionSpec as P

time_step = 0.6
variance_gain = 0.5
penalty = 0.1
weight_denominator = 16.0

VMEM_LIMIT = 24 * 1024 * 1024
AXES = ("space", "node")
LONG = 40


def cost_of(us):
    return pl.CostEstimate(flops=us * 1_000_000_000, bytes_accessed=us * 3_000_000, transcendentals=0)


def roll(value, steps, axis):
    return pltpu.roll(value, steps % value.shape[axis], axis)


def in_plane(value, a, cy, cz, k):
    return a[1] * (cy[0, k] * roll(value, 1, 0) + cy[1, k] * roll(value, -1, 0)) + a[2] * (
        cz[0, k] * roll(value, 1, 1) + cz[1, k] * roll(value, -1, 1)
    )


def in_plane_back(value, a, cy, cz, k):
    return a[1] * (roll(cy[0, k] * value, -1, 0) + roll(cy[1, k] * value, 1, 0)) + a[2] * (
        roll(cz[0, k] * value, -1, 1) + roll(cz[1, k] * value, 1, 1)
    )


def rows_of(scal, j):
    return [scal[j, k] for k in range(5)]


def pick(values, index):
    result = jnp.float32(values[-1])
    for k, value in enumerate(values[:-1]):
        result = jnp.where(index == k, jnp.float32(value), result)
    return result


def node_scales(indices, step, scal):
    levels = [-math.cos(math.pi * k / 8.0) for k in range(9)]
    half = step[0] & 31
    wave = pick([math.sin(2.0 * math.pi * k / 64.0) for k in range(17)], jnp.minimum(half, 32 - half))
    phase = 1.0 + jnp.where(step[0] < 32, 0.5, -0.5) * wave
    for j, index in enumerate(indices):
        p = {k: pick(levels, index[0, k]) for k in (0, 1, 2, 4, 6, 7)}
        scal[j, 0] = 1.0 + 0.3 * p[0]
        scal[j, 1] = 1.0 + 0.3 * p[1]
        scal[j, 2] = (1.0 + 0.3 * p[2]) * (1.0 + 0.2 * p[7])
        scal[j, 3] = pick([math.exp(0.5 * p) for p in levels], index[0, 3]) * pick(
            [math.exp(0.25 * p) for p in levels], index[0, 5]
        )
        scal[j, 4] = (1.0 + 0.3 * p[4] + 0.2 * p[6]) * phase


def expand(bits, columns):
    blocks = bits.shape[1]
    spread = (
        lax.broadcasted_iota(jnp.int32, (blocks, columns), 1) // (columns // blocks)
        == lax.broadcasted_iota(jnp.int32, (blocks, columns), 0)
    ).astype(jnp.bfloat16)
    return jnp.dot(bits.astype(jnp.float32).astype(jnp.bfloat16), spread, preferred_element_type=jnp.float32)


def toward_outer(up, me):
    flip = (me == 1).astype(jnp.float32)
    return up + flip - 2.0 * flip * up


def pack(core, own, far, out):
    out[0] = own[0, 0]
    out[1] = far[0, 3 * core[0]]


def fields_of(k, at, me, speeds, masks, cx, cy, cz):
    rows, columns = speeds.shape[2:]
    row = lax.broadcasted_iota(jnp.int32, (rows, columns), 0)
    column = lax.broadcasted_iota(jnp.int32, (rows, columns), 1)
    up = [expand(masks[d, at], columns) for d in range(3)]
    s = [speeds[d, at].astype(jnp.float32) for d in range(3)]
    outer = s[0] * toward_outer(up[0], me)
    cx[0, k] = outer
    cx[1, k] = s[0] - outer
    lower = s[1] * up[1]
    cy[0, k] = jnp.where(row == 0, 0.0, lower)
    cy[1, k] = jnp.where(row == rows - 1, 0.0, s[1] - lower)
    lower = s[2] * up[2]
    cz[0, k] = jnp.where(column == 0, 0.0, lower)
    cz[1, k] = jnp.where(column == columns - 1, 0.0, s[2] - lower)


def own_of(k, at, rates, speeds, scal, dg):
    s = [speeds[d, at].astype(jnp.float32) for d in range(3)] + [rates[at].astype(jnp.float32)]
    for j in range(2):
        dg[j, k] = sum(scal[j, d] * s[d] for d in range(4))


def prepare(core, own_index, far_index, step_index, speed, mask, decay, control, scal, cx, cy, cz, dg, ctl, edge, own_ids, far_ids, step, few):
    me = core[0]
    small = [(own_index, own_ids), (far_index, far_ids), (step_index, step)]
    small = [pltpu.make_async_copy(source, target, few.at[n]) for n, (source, target) in enumerate(small)]
    for copy in small:
        copy.start()
    for k, at in enumerate((3 * me, 1 + me)):
        fields_of(k, at, me, speed, mask, cx, cy, cz)
        ctl[k] = control[at]
    edge[...] = cx[0, 0]
    for copy in small:
        copy.wait()
    node_scales((own_ids, far_ids), step, scal)
    for k, at in enumerate((3 * me, 1 + me)):
        own_of(k, at, decay, speed, scal, dg)


def prepare_next(core, scal, speed, mask, decay, control, own, far, _, __, s1_next, near, cx, cy, cz, dg):
    me = core[0]
    at = 2 - me
    fields_of(0, at, me, speed, mask, cx, cy, cz)
    own_of(0, at, decay, speed, scal, dg)
    near[...] = cx[0, 0]
    for j, c in enumerate((own, far)):
        a = rows_of(scal, j)
        value = c[0, at]
        l = a[0] * (cx[0, 0] * c[0, 1 + me] + cx[1, 0] * c[0, 3 - 3 * me]) + in_plane(value, a, cy, cz, 0) - dg[j, 0] * value
        s1_next[j] = value + time_step * (l + a[4] * control[at])


def prepare_back(core, own_weight, far_weight, goal, adjoint, weights, goals, adj, adj_out_o, adj_out_i):
    me = core[0]
    weights[0] = own_weight[0].astype(jnp.float32) * (1.0 / weight_denominator)
    weights[1] = far_weight[0].astype(jnp.float32) * (1.0 / weight_denominator)
    for k, at in enumerate((3 * me, 1 + me)):
        goals[k] = goal[at].astype(jnp.float32)
        adj[k] = adjoint[0, at].astype(jnp.float32)
    adj_out_o[...] = adjoint[0, 3 - 3 * me].astype(jnp.float32)
    adj_out_i[...] = adjoint[0, 2 - me].astype(jnp.float32)


def first_stage(core, scal, own, far, cx, cy, cz, dg, ctl, base, base_q, s1_in):
    me = core[0]
    for j, c in enumerate((own, far)):
        a = rows_of(scal, j)
        c_o, c_i = c[0, 3 * me], c[0, 1 + me]
        push = [a[4] * ctl[k] for k in range(2)]
        l_i = a[0] * (cx[0, 1] * c_o + cx[1, 1] * c[0, 2 - me]) + in_plane(c_i, a, cy, cz, 1) - dg[j, 1] * c_i
        s1_i = c_i + time_step * (l_i + push[1])
        s1_in[j] = s1_i
        l_o = a[0] * (cx[1, 0] * c_i) + in_plane(c_o, a, cy, cz, 0) - dg[j, 0] * c_o
        base[j] = c_o + time_step * (l_o + push[0])
        base_q[j] = 0.75 * c_o + (0.25 * time_step) * (a[0] * (cx[1, 0] * s1_i) + push[0])


def first_edge(scal, halo, base, base_q, cx, cy, cz, dg, msg):
    for j in range(2):
        a = rows_of(scal, j)
        s1_o = base[j] + (time_step * a[0]) * (cx[0, 0] * halo[1 - j])
        msg[j, 0] = s1_o
        msg[j, 1] = base_q[j] + 0.25 * (s1_o + time_step * (in_plane(s1_o, a, cy, cz, 0) - dg[j, 0] * s1_o))


def second_inner(core, scal, own, far, msg, s1_in, s1_next, cx, cy, cz, dg, ctl, s2_own, s2_far):
    for j, (c, out) in enumerate(((own, s2_own), (far, s2_far))):
        a = rows_of(scal, j)
        s1_i = s1_in[j]
        l_i = a[0] * (cx[0, 1] * msg[j, 0] + cx[1, 1] * s1_next[j]) + in_plane(s1_i, a, cy, cz, 1) - dg[j, 1] * s1_i
        out[...] = 0.75 * c[0, 1 + core[0]] + 0.25 * (s1_i + time_step * (l_i + a[4] * ctl[1]))


def third_stage(core, scal, own, far, msg, s2_own, s2_far, next_own, next_far, near_edge, cx, cy, cz, dg, ctl, base):
    me = core[0]
    parts = ((own, s2_own, next_own), (far, s2_far, next_far))
    for j, (c, s2, s2_next) in enumerate(parts):
        a = rows_of(scal, j)
        q, s2_i = msg[j, 1], s2[...]
        back = (0.25 * time_step * a[0]) * (near_edge[...] * msg[j, 0])
        l_o = a[0] * (cx[0, 0] * back + cx[1, 0] * s2_i) + in_plane(q, a, cy, cz, 0) - dg[j, 0] * q
        l_i = a[0] * (cx[0, 1] * q + cx[1, 1] * s2_next[...]) + in_plane(s2_i, a, cy, cz, 1) - dg[j, 1] * s2_i
        base[j, 0] = c[0, 3 * me] / 3.0 + 2.0 / 3.0 * (q + time_step * (l_o + a[4] * ctl[0]))
        base[j, 1] = c[0, 1 + me] / 3.0 + 2.0 / 3.0 * (s2_i + time_step * (l_i + a[4] * ctl[1]))


def finals(j, scal, halo, base, cx, cy, cz, dg):
    a = rows_of(scal, j)
    step = (0.25 * time_step * a[0]) * (cx[0, 0] * halo[1 - j, 0])
    change = in_plane(step, a, cy, cz, 0) - dg[j, 0] * step + a[0] * (cx[0, 0] * halo[1 - j, 1])
    outer = base[j, 0] + 2.0 / 3.0 * (step + time_step * change)
    inner = base[j, 1] + (2.0 / 3.0 * time_step * a[0]) * (cx[0, 1] * step)
    return outer, inner


def turn(scal, weights, halo, base, cx, cy, cz, dg, goals, adj, after_o, after_i, final_own, final_far, term, msg, partial):
    final_own[0], final_own[1] = finals(0, scal, halo, base, cx, cy, cz, dg)
    final_far[0], final_far[1] = finals(1, scal, halo, base, cx, cy, cz, dg)
    first = [weights[0] * final_own[k] + weights[1] * final_far[k] for k in range(2)]
    for j, (final, after) in enumerate(((final_own, (adj[0], adj[1])), (final_far, (after_o[...], after_i[...])))):
        a = rows_of(scal, j)
        u = []
        for k in range(2):
            t = after[k] + goals[k] * weights[j] * (1.0 + 2.0 * variance_gain * (final[k] - first[k]))
            term[j, k] = t
            u.append(2.0 / 3.0 * t)
        msg[j, 0] = a[0] * (cx[0, 0] * u[0])
        spread = a[0] * (cx[0, 1] * u[1]) + in_plane_back(u[0], a, cy, cz, 0) - dg[j, 0] * u[0]
        value = u[0] + time_step * spread
        partial[j] = value
        msg[j, 1] = a[0] * (cx[0, 0] * value)


class Laid:
    def __init__(self, refs):
        self.left = [(ref, start) for ref in refs for start in range(0, ref.shape[0], 8)]

    def put(self, value):
        for start in range(0, value.shape[0], 8):
            ref, at = self.left.pop(0)
            ref[at : at + 8] = value[start : start + 8]


def get(refs, count, rows):
    whole = jnp.concatenate([ref[...] for ref in refs], 0)
    return [whole[rows * k : rows * k + rows] for k in range(count)] + [whole[rows * count :]]


def cut(rows, pieces):
    tiles = rows // 8
    return [8 * (tiles // pieces + (k < tiles % pieces)) for k in range(pieces)]


def turn_inner(scal, weights, final_own, final_far, terms, cx, cy, cz, dg, goals, part, cost, *pins):
    laid = Laid(pins)
    for j in range(2):
        a = rows_of(scal, j)
        u = [2.0 / 3.0 * terms[j, k] for k in range(2)]
        laid.put(a[0] * (cx[1, 1] * u[1]))
        spread = a[0] * (cx[1, 0] * u[0]) + in_plane_back(u[1], a, cy, cz, 1) - dg[j, 1] * u[1]
        value = u[1] + time_step * spread
        part[j] = value
        laid.put(a[0] * (cx[1, 1] * value))
    total = 0.0
    for k in range(2):
        own, far = weights[0] * final_own[k], weights[1] * final_far[k]
        first = own + far
        second = own * final_own[k] + far * final_far[k]
        total = total + goals[k] * (first + variance_gain * (second - first * first))
    rows = total.shape[0]
    total = sum(total[8 * r : 8 * r + 8] for r in range(rows // 8))
    cost[...] = total
    laid.put(total)


def back_second(scal, msgs, partials, part, near_edge, near, cx, cy, cz, dg, cost_own, *rest):
    base, a2, total = rest[-3:]
    count, rows = (len(rest) - 3) // 2, msgs.shape[2]
    mine, theirs = get(rest[:count], 4, rows), get(rest[count:-3], 4, rows)
    cost = cost_own[...] + theirs[4]
    total[...] = sum(cost[:, 128 * k : 128 * k + 128] for k in range(cost.shape[1] // 128))
    for j in range(2):
        a = rows_of(scal, j)
        pin, pin2 = theirs[2 - 2 * j], theirs[3 - 2 * j]
        pin2 = 0.25 * (pin2 + (time_step * a[0]) * (near[...] * mine[2 * j]))
        a2_i = part[j] + time_step * pin
        a2[j] = a2_i
        u_o, u_i = 0.25 * partials[j], 0.25 * a2_i
        back = (0.25 * time_step * a[0]) * (near_edge[...] * msgs[j, 0])
        spread = a[0] * (cx[0, 1] * u_i) + in_plane_back(u_o, a, cy, cz, 0) - dg[j, 0] * u_o + back
        base[j, 0] = u_o + time_step * spread
        spread = a[0] * (cx[1, 0] * u_o) + in_plane_back(u_i, a, cy, cz, 1) - dg[j, 1] * u_i + pin2
        base[j, 1] = u_i + time_step * spread


def second_back_edge(scal, halo, base, cx, cy, cz, dg, cost, cost_far, a1, msg_far, msg_own, total):
    total[...] = cost[...] + cost_far[...]
    for j, msg in ((1, msg_far), (0, msg_own)):
        a = rows_of(scal, j)
        step = (0.25 * time_step) * halo[1 - j, 0]
        spread = in_plane_back(step, a, cy, cz, 0) - dg[j, 0] * step + 0.25 * halo[1 - j, 1]
        value = base[j, 0] + step + time_step * spread
        a1[j] = value
        msg[...] = a[0] * (cx[0, 0] * value)


def close(core, scal, terms, partials, halo, a1, a2, base, cx, cy, cz, dg, ctl, keep, part, give, *send):
    laid = Laid(send)
    sources = [0.0, 0.0]
    for j in range(2):
        a = rows_of(scal, j)
        first = halo[1 - j, 0]
        x = [a1[j], base[j, 1] + (0.25 * time_step * time_step * a[0]) * (cx[1, 0] * first)]
        a2_o = partials[j] + time_step * first
        for k, second in enumerate((a2_o, a2[j])):
            sources[k] = sources[k] + a[4] * (2.0 / 3.0 * terms[j, k] + 0.25 * second + x[k])
        spread = a[0] * (cx[0, 1] * x[1]) + in_plane_back(x[0], a, cy, cz, 0) - dg[j, 0] * x[0]
        outer = terms[j, 0] / 3.0 + 0.75 * a2_o + (x[0] + time_step * spread)
        spread = a[0] * (cx[1, 0] * x[0]) + in_plane_back(x[1], a, cy, cz, 1) - dg[j, 1] * x[1]
        inner = terms[j, 1] / 3.0 + 0.75 * a2[j] + (x[1] + time_step * spread)
        for k, value in enumerate((outer, inner, a[0] * (cx[1, 1] * x[1]))):
            if j == 0:
                part[k] = value
            else:
                laid.put(value)
    half = ctl.shape[2] // 2
    zero = core[0] == 0
    for k in range(2):
        gradient = time_step * sources[k] + penalty * ctl[k]
        low, high = gradient[:, :half], gradient[:, half:]
        keep[k] = jnp.where(zero, low, high)
        give[k] = jnp.where(zero, high, low)


def last_edge(halo_own, halo_far, part, cost, cost_far, outer, add, total):
    total[...] = cost[...] + cost_far[...]
    outer[...] = part[0] + time_step * halo_own[...]
    add[...] = time_step * halo_far[...]


def assemble(cells, core, part, outer, add, cost, keep, taken, *rest):
    theirs, (out, gradient, objective) = get(rest[:-3], 3, part.shape[1]), rest[-3:]
    me = core[0]
    out[0, 3 * me] = outer[...]
    out[0, 1 + me] = part[1] + time_step * theirs[2]
    out[0, 3 - 3 * me] = theirs[0] + add[...]
    out[0, 2 - me] = theirs[1] + time_step * part[2]
    gradient[3 * me] = keep[0]
    gradient[1 + me] = keep[1]
    gradient[3 - 3 * me] = taken[0]
    gradient[2 - me] = taken[1]
    objective[0] = jnp.sum(cost[...]) / cells


def on_core(body, outs, scalars, arrays, hbm_out=(), smem_out=(), after=(), cost=0, name=None):
    hbm_out = tuple(hbm_out) + tuple(smem_out)
    out_shape = [
        jax.ShapeDtypeStruct(s, jnp.float32) if i in hbm_out else pltpu.VMEM(s, jnp.float32)
        for i, s in enumerate(outs)
    ]
    held = [pltpu.with_memory_space_constraint(x, pltpu.SMEM) for x in scalars]
    held += [pltpu.with_memory_space_constraint(x, pltpu.VMEM) for x in arrays]
    count, waits = len(held), len(after)

    def run(*refs):
        body(*refs[:count], *refs[count + waits :])

    return pl.pallas_call(
        run,
        out_shape=out_shape,
        in_specs=[pl.BlockSpec(memory_space=pltpu.SMEM)] * len(scalars)
        + [pl.BlockSpec(memory_space=pltpu.VMEM)] * len(arrays)
        + [pl.BlockSpec(memory_space=pl.ANY)] * waits,
        out_specs=[
            pl.BlockSpec(memory_space=pltpu.SMEM if i in smem_out else pltpu.VMEM) for i in range(len(outs))
        ],
        compiler_params=pltpu.CompilerParams(vmem_limit_bytes=VMEM_LIMIT),
        cost_estimate=cost_of(cost) if cost else None,
        name=name or body.__name__,
    )(*held, *after)


def shards(
    concentration,
    adjoint_next,
    speed,
    direction_mask,
    decay_rate,
    control,
    goal_weight,
    node_index,
    weight_num,
    step_index,
):
    sections = lax.axis_size("space")
    ranks = sections * lax.axis_size("node")
    within = [(i, i ^ 1) for i in range(ranks)]
    across = [p for i in range(1, ranks - 1, 2) for p in ((i, i + 1), (i + 1, i))]
    along = [p for i in range(0, ranks - 2, 2) for p in ((i + 1, i + 3), (i + 2, i))]

    def swap(x, what):
        with jax.named_scope("swap_" + what):
            return lax.ppermute(x, AXES, within)

    def pass_on(x, what, pairs=across):
        with jax.named_scope("pass_" + what):
            return lax.ppermute(x, AXES, pairs)

    _, layers, rows, columns = concentration.shape
    me = lax.axis_index("node").astype(jnp.int32)
    core = jnp.reshape(me, (1,))
    far_index, far_weight, step = swap(node_index, "node_index"), swap(weight_num, "weight_num"), swap(step_index, "step")

    far = swap(concentration, "state")
    plane = (rows, columns)
    pair, three = (2,) + plane, (3,) + plane
    four = (2,) + pair
    sides = (2, rows, columns // 2)
    held = lambda x, space: pltpu.with_memory_space_constraint(x, space)
    packed = pl.pallas_call(
        pack,
        out_shape=pltpu.VMEM(pair, jnp.float32),
        grid_spec=pltpu.PrefetchScalarGridSpec(
            num_scalar_prefetch=1,
            grid=(1,),
            in_specs=[
                pl.BlockSpec((1, 1) + plane, lambda g, c: (0, 3 * c[0], 0, 0)),
                pl.BlockSpec(memory_space=pltpu.VMEM),
            ],
            out_specs=pl.BlockSpec(memory_space=pltpu.VMEM),
        ),
        compiler_params=pltpu.CompilerParams(vmem_limit_bytes=VMEM_LIMIT),
        cost_estimate=cost_of(LONG),
        name="pack",
    )(core, held(concentration, pltpu.HBM), held(far, pltpu.VMEM))
    halo = pass_on(packed, "state")

    shapes = [four, four, four, four, pair, plane]
    scal, cx, cy, cz, dg, ctl, edge = pl.pallas_call(
        prepare,
        out_shape=[pltpu.SMEM((2, 8), jnp.float32)] + [pltpu.VMEM(s, jnp.float32) for s in shapes],
        in_specs=[pl.BlockSpec(memory_space=pltpu.SMEM)]
        + [pl.BlockSpec(memory_space=pl.ANY)] * 3
        + [pl.BlockSpec(memory_space=pltpu.VMEM)] * 4,
        out_specs=[pl.BlockSpec(memory_space=pltpu.SMEM)] + [pl.BlockSpec(memory_space=pltpu.VMEM)] * len(shapes),
        scratch_shapes=[
            pltpu.SMEM(node_index.shape, jnp.int32),
            pltpu.SMEM(node_index.shape, jnp.int32),
            pltpu.SMEM((1,), jnp.int32),
            pltpu.SemaphoreType.DMA((3,)),
        ],
        compiler_params=pltpu.CompilerParams(vmem_limit_bytes=VMEM_LIMIT),
        cost_estimate=cost_of(LONG),
        name="prepare",
    )(
        core,
        held(node_index, pltpu.HBM),
        *(far_index, step),
        *[held(x, pltpu.VMEM) for x in (speed, direction_mask, decay_rate, control)],
    )
    near_edge = pass_on(edge, "edge")
    fields = [cx, cy, cz, dg]
    both = [core, scal]
    states = [concentration, far]
    base, base_q, s1_in = on_core(first_stage, [pair] * 3, both, states + fields + [ctl])
    (msg,) = on_core(first_edge, [four], [scal], [halo, base, base_q] + fields, cost=LONG)
    halo2 = pass_on(msg, "stage2")

    weights, goals, adj, adj_out_o, adj_out_i = pl.pallas_call(
        lambda *refs: prepare_back(*refs[:5], *refs[6:]),
        out_shape=[pltpu.SMEM((2,), jnp.float32)]
        + [pltpu.VMEM(s, jnp.float32) for s in (pair, pair, plane, plane)],
        in_specs=[pl.BlockSpec(memory_space=pltpu.SMEM)] * 3
        + [pl.BlockSpec(memory_space=pltpu.VMEM)] * 2
        + [pl.BlockSpec(memory_space=pl.ANY)],
        out_specs=[pl.BlockSpec(memory_space=pltpu.SMEM)] + [pl.BlockSpec(memory_space=pltpu.VMEM)] * 4,
        compiler_params=pltpu.CompilerParams(vmem_limit_bytes=VMEM_LIMIT),
        name="prepare_back",
    )(core, swap(far_weight, "weight_num"), far_weight, held(goal_weight, pltpu.HBM), held(adjoint_next, pltpu.HBM), msg)
    after_o, after_i = swap(adj_out_o, "after_o"), swap(adj_out_i, "after_i")

    s1_next, near = pl.pallas_call(
        prepare_next,
        out_shape=[pltpu.VMEM(pair, jnp.float32), pltpu.VMEM(plane, jnp.float32)],
        in_specs=[pl.BlockSpec(memory_space=pltpu.SMEM)] * 2
        + [pl.BlockSpec(memory_space=pltpu.VMEM)] * 6
        + [pl.BlockSpec(memory_space=pl.ANY)] * 2,
        out_specs=[pl.BlockSpec(memory_space=pltpu.VMEM)] * 2,
        scratch_shapes=[pltpu.VMEM((2, 1) + plane, jnp.float32)] * 4,
        compiler_params=pltpu.CompilerParams(vmem_limit_bytes=VMEM_LIMIT),
        cost_estimate=cost_of(LONG),
        name="prepare_next",
    )(
        core,
        held(scal, pltpu.SMEM),
        *[held(x, pltpu.VMEM) for x in (speed, direction_mask, decay_rate, control)],
        *[held(x, pltpu.VMEM) for x in states],
        msg,
        near_edge,
    )

    s2 = list(on_core(second_inner, [plane] * 2, both, states + [msg, s1_in, s1_next] + fields + [ctl]))
    s2_next = [swap(s2[1], "s2_far"), swap(s2[0], "s2_own")]
    (base,) = on_core(third_stage, [four], both, states + [msg] + s2 + s2_next + [near_edge] + fields + [ctl])
    final_own, final_far, terms, msg3, partials = on_core(
        turn,
        [pair, pair, four, four, pair],
        [scal, weights],
        [halo2, base] + fields + [goals, adj, after_o, after_i],
    )
    halo3 = pass_on(msg3, "back2")
    part, cost, *pins = on_core(
        turn_inner,
        [pair, (8, columns)] + [(r, columns) for r in cut(4 * rows + 8, 3)],
        [scal, weights],
        [final_own, final_far, terms] + fields + [goals],
    )
    theirs = [swap(x, "pin") for x in pins]
    base, a2, cost = on_core(
        back_second,
        [four, pair, (8, 128)],
        [scal],
        [msg3, partials, part, near_edge, near] + fields + [cost] + pins + theirs,
    )
    whole = sections & (sections - 1) == 0
    steps = [1 << k for k in range(sections.bit_length() - 1)] if whole else []
    steps = steps[1:] + steps[:1]

    def from_pair(x, k):
        with jax.named_scope("goal_sum"):
            if k >= len(steps):
                return jnp.zeros_like(x)
            return lax.ppermute(x, "space", [(i, i ^ steps[k]) for i in range(sections)])

    for k in range(len(steps) - 2):
        cost = cost + from_pair(cost, k)
    a1, msg4_far, msg4_own, cost = on_core(
        second_back_edge,
        [pair, plane, plane, (8, 128)],
        [scal],
        [halo3, base] + fields + [cost, from_pair(cost, max(0, len(steps) - 2))],
    )
    halo4_own = pass_on(msg4_far, "back1_far")
    halo4_far = pass_on(msg4_own, "back1_own", along)
    keep, part, *out = on_core(
        close,
        [sides, three, sides] + [(r, columns) for r in cut(3 * rows, 2)],
        both,
        [terms, partials, halo3, a1, a2, base] + fields + [ctl],
    )
    parts = [swap(x, "adjoint") for x in out[1:]]
    taken = swap(out[0], "gradient")
    outer, add, cost = on_core(
        last_edge,
        [plane, plane, (8, 128)],
        [],
        [halo4_own, halo4_far, part, cost, from_pair(cost, max(1, len(steps) - 1))],
        cost=LONG,
    )
    if not whole:
        cost = lax.psum(cost, "space")
    adjoint, gradient, objective = on_core(
        functools.partial(assemble, sections * layers * rows * columns),
        [(1, layers, rows, columns), (layers, rows, columns // 2), (1,)],
        [core],
        [part, outer, add, cost, keep, taken] + parts,
        hbm_out=(0, 1),
        smem_out=(2,),
        name="assemble",
    )
    return (adjoint, gradient, objective)


def solution(mesh):
    return jax.shard_map(
        shards,
        mesh=mesh,
        in_specs=(
            P("node", ("groups", "space"), None, None),
            P("node", ("groups", "space"), None, None),
            P(None, ("groups", "space"), None, None),
            P(None, ("groups", "space"), None, None),
            P(("groups", "space"), None, None),
            P(("groups", "space"), None, None),
            P(("groups", "space"), None, None),
            P("node", None),
            P("node"),
            P("groups"),
        ),
        out_specs=(
            P("node", ("groups", "space"), None, None),
            P(("groups", "space"), None, "node"),
            P("groups"),
        ),
        check_vma=False,
    )
```

```python
import functools
import math

import jax
import jax.numpy as jnp
from jax import lax
from jax.experimental import pallas as pl
from jax.experimental.pallas import tpu as pltpu
from jax.sharding import PartitionSpec as P

time_step = 0.6
variance_gain = 0.5
penalty = 0.1
weight_denominator = 16.0

VMEM_LIMIT = 24 * 1024 * 1024
AXES = ("space", "node")
LONG = 40


def cost_of(us):
    return pl.CostEstimate(flops=us * 1_000_000_000, bytes_accessed=us * 3_000_000, transcendentals=0)


def roll(value, steps, axis):
    return pltpu.roll(value, steps % value.shape[axis], axis)


def in_plane(value, a, cy, cz, k):
    return a[1] * (cy[0, k] * roll(value, 1, 0) + cy[1, k] * roll(value, -1, 0)) + a[2] * (
        cz[0, k] * roll(value, 1, 1) + cz[1, k] * roll(value, -1, 1)
    )


def in_plane_back(value, a, cy, cz, k):
    return a[1] * (roll(cy[0, k] * value, -1, 0) + roll(cy[1, k] * value, 1, 0)) + a[2] * (
        roll(cz[0, k] * value, -1, 1) + roll(cz[1, k] * value, 1, 1)
    )


def rows_of(scal, j):
    return [scal[j, k] for k in range(5)]


def pick(values, index):
    result = jnp.float32(values[-1])
    for k, value in enumerate(values[:-1]):
        result = jnp.where(index == k, jnp.float32(value), result)
    return result


def node_scales(tiles, scal):
    levels = [-math.cos(math.pi * k / 8.0) for k in range(9)]
    step = tiles[0][0, 9].astype(jnp.int32)
    half = step & 31
    wave = pick([math.sin(2.0 * math.pi * k / 64.0) for k in range(17)], jnp.minimum(half, 32 - half))
    phase = 1.0 + jnp.where(step < 32, 0.5, -0.5) * wave
    for j, tile in enumerate(tiles):
        p = {k: pick(levels, tile[0, k]) for k in (0, 1, 2, 4, 6, 7)}
        scal[j, 0] = 1.0 + 0.3 * p[0]
        scal[j, 1] = 1.0 + 0.3 * p[1]
        scal[j, 2] = (1.0 + 0.3 * p[2]) * (1.0 + 0.2 * p[7])
        scal[j, 3] = pick([math.exp(0.5 * p) for p in levels], tile[0, 3]) * pick(
            [math.exp(0.25 * p) for p in levels], tile[0, 5]
        )
        scal[j, 4] = (1.0 + 0.3 * p[4] + 0.2 * p[6]) * phase


def expand(bits, columns):
    blocks = bits.shape[1]
    spread = (
        lax.broadcasted_iota(jnp.int32, (blocks, columns), 1) // (columns // blocks)
        == lax.broadcasted_iota(jnp.int32, (blocks, columns), 0)
    ).astype(jnp.bfloat16)
    return jnp.dot(bits.astype(jnp.float32).astype(jnp.bfloat16), spread, preferred_element_type=jnp.float32)


def toward_outer(up, me):
    flip = (me == 1).astype(jnp.float32)
    return up + flip - 2.0 * flip * up


def begin(out):
    out[...] = jnp.zeros_like(out)


def gather_numbers(index, weight, step, _, numbers):
    lane = lax.broadcasted_iota(jnp.int32, numbers.shape, 1)
    value = jnp.zeros(numbers.shape, jnp.int32)
    for k, number in enumerate([index[0, k] for k in range(index.shape[1])] + [weight[0], step[0]]):
        value = jnp.where(lane == k, number, value)
    numbers[...] = value.astype(jnp.float32)


def pack(core, own, far, speed, mask, out):
    at = 3 * core[0]
    out[0] = own[0, at]
    out[1] = far[0, at]
    out[2] = speed[0, at].astype(jnp.float32) * toward_outer(expand(mask[0, at], speed.shape[3]), core[0])


def fields_of(k, at, me, speeds, masks, cx, cy, cz):
    rows, columns = speeds.shape[2:]
    row = lax.broadcasted_iota(jnp.int32, (rows, columns), 0)
    column = lax.broadcasted_iota(jnp.int32, (rows, columns), 1)
    up = [expand(masks[d, at], columns) for d in range(3)]
    s = [speeds[d, at].astype(jnp.float32) for d in range(3)]
    outer = s[0] * toward_outer(up[0], me)
    cx[0, k] = outer
    cx[1, k] = s[0] - outer
    lower = s[1] * up[1]
    cy[0, k] = jnp.where(row == 0, 0.0, lower)
    cy[1, k] = jnp.where(row == rows - 1, 0.0, s[1] - lower)
    lower = s[2] * up[2]
    cz[0, k] = jnp.where(column == 0, 0.0, lower)
    cz[1, k] = jnp.where(column == columns - 1, 0.0, s[2] - lower)


def own_of(k, at, rates, speeds, scal, dg):
    s = [speeds[d, at].astype(jnp.float32) for d in range(3)] + [rates[at].astype(jnp.float32)]
    for j in range(2):
        dg[j, k] = sum(scal[j, d] * s[d] for d in range(4))


def prepare(core, own_numbers, far_numbers, speed, mask, decay, control, scal, cx, cy, cz, dg, ctl):
    me = core[0]
    for k, at in enumerate((3 * me, 1 + me)):
        fields_of(k, at, me, speed, mask, cx, cy, cz)
        ctl[k] = control[at]
    node_scales((own_numbers[...], far_numbers[...]), scal)
    for k, at in enumerate((3 * me, 1 + me)):
        own_of(k, at, decay, speed, scal, dg)


def prepare_next(core, scal, speed, mask, decay, control, own, far, _, s1_next, near, cx, cy, cz, dg):
    me = core[0]
    at = 2 - me
    fields_of(0, at, me, speed, mask, cx, cy, cz)
    own_of(0, at, decay, speed, scal, dg)
    near[...] = cx[0, 0]
    for j, c in enumerate((own, far)):
        a = rows_of(scal, j)
        value = c[0, at]
        l = a[0] * (cx[0, 0] * c[0, 1 + me] + cx[1, 0] * c[0, 3 - 3 * me]) + in_plane(value, a, cy, cz, 0) - dg[j, 0] * value
        s1_next[j] = value + time_step * (l + a[4] * control[at])


def prepare_back(core, goal, own_numbers, far_numbers, adjoint, _, weights, goals, adj, adj_out_o, adj_out_i):
    me = core[0]
    weights[0] = own_numbers[...][0, 8] * (1.0 / weight_denominator)
    weights[1] = far_numbers[...][0, 8] * (1.0 / weight_denominator)
    for k, at in enumerate((3 * me, 1 + me)):
        goals[k] = goal[at].astype(jnp.float32)
        adj[k] = adjoint[0, at].astype(jnp.float32)
    adj_out_o[...] = adjoint[0, 3 - 3 * me].astype(jnp.float32)
    adj_out_i[...] = adjoint[0, 2 - me].astype(jnp.float32)


def first_stage(core, scal, own, far, cx, cy, cz, dg, ctl, base, base_q, s1_in):
    me = core[0]
    for j, c in enumerate((own, far)):
        a = rows_of(scal, j)
        c_o, c_i = c[0, 3 * me], c[0, 1 + me]
        push = [a[4] * ctl[k] for k in range(2)]
        l_i = a[0] * (cx[0, 1] * c_o + cx[1, 1] * c[0, 2 - me]) + in_plane(c_i, a, cy, cz, 1) - dg[j, 1] * c_i
        s1_i = c_i + time_step * (l_i + push[1])
        s1_in[j] = s1_i
        l_o = a[0] * (cx[1, 0] * c_i) + in_plane(c_o, a, cy, cz, 0) - dg[j, 0] * c_o
        base[j] = c_o + time_step * (l_o + push[0])
        base_q[j] = 0.75 * c_o + (0.25 * time_step) * (a[0] * (cx[1, 0] * s1_i) + push[0])


def first_edge(scal, halo, base, base_q, cx, cy, cz, dg, msg):
    for j in range(2):
        a = rows_of(scal, j)
        s1_o = base[j] + (time_step * a[0]) * (cx[0, 0] * halo[1 - j])
        msg[j, 0] = s1_o
        msg[j, 1] = base_q[j] + 0.25 * (s1_o + time_step * (in_plane(s1_o, a, cy, cz, 0) - dg[j, 0] * s1_o))


def second_inner(core, scal, own, far, msg, s1_in, s1_next, cx, cy, cz, dg, ctl, s2_own, s2_far):
    for j, (c, out) in enumerate(((own, s2_own), (far, s2_far))):
        a = rows_of(scal, j)
        s1_i = s1_in[j]
        l_i = a[0] * (cx[0, 1] * msg[j, 0] + cx[1, 1] * s1_next[j]) + in_plane(s1_i, a, cy, cz, 1) - dg[j, 1] * s1_i
        out[...] = 0.75 * c[0, 1 + core[0]] + 0.25 * (s1_i + time_step * (l_i + a[4] * ctl[1]))


def third_stage(core, scal, own, far, msg, s2_own, s2_far, next_own, next_far, halo, cx, cy, cz, dg, ctl, base):
    me = core[0]
    parts = ((own, s2_own, next_own), (far, s2_far, next_far))
    for j, (c, s2, s2_next) in enumerate(parts):
        a = rows_of(scal, j)
        q, s2_i = msg[j, 1], s2[...]
        back = (0.25 * time_step * a[0]) * (halo[2] * msg[j, 0])
        l_o = a[0] * (cx[0, 0] * back + cx[1, 0] * s2_i) + in_plane(q, a, cy, cz, 0) - dg[j, 0] * q
        l_i = a[0] * (cx[0, 1] * q + cx[1, 1] * s2_next[...]) + in_plane(s2_i, a, cy, cz, 1) - dg[j, 1] * s2_i
        base[j, 0] = c[0, 3 * me] / 3.0 + 2.0 / 3.0 * (q + time_step * (l_o + a[4] * ctl[0]))
        base[j, 1] = c[0, 1 + me] / 3.0 + 2.0 / 3.0 * (s2_i + time_step * (l_i + a[4] * ctl[1]))


def finals(j, scal, halo, base, cx, cy, cz, dg):
    a = rows_of(scal, j)
    step = (0.25 * time_step * a[0]) * (cx[0, 0] * halo[1 - j, 0])
    change = in_plane(step, a, cy, cz, 0) - dg[j, 0] * step + a[0] * (cx[0, 0] * halo[1 - j, 1])
    outer = base[j, 0] + 2.0 / 3.0 * (step + time_step * change)
    inner = base[j, 1] + (2.0 / 3.0 * time_step * a[0]) * (cx[0, 1] * step)
    return outer, inner


def turn(scal, weights, halo, base, cx, cy, cz, dg, goals, adj, after_o, after_i, final_own, final_far, term, msg, partial):
    final_own[0], final_own[1] = finals(0, scal, halo, base, cx, cy, cz, dg)
    final_far[0], final_far[1] = finals(1, scal, halo, base, cx, cy, cz, dg)
    first = [weights[0] * final_own[k] + weights[1] * final_far[k] for k in range(2)]
    for j, (final, after) in enumerate(((final_own, (adj[0], adj[1])), (final_far, (after_o[...], after_i[...])))):
        a = rows_of(scal, j)
        u = []
        for k in range(2):
            t = after[k] + goals[k] * weights[j] * (1.0 + 2.0 * variance_gain * (final[k] - first[k]))
            term[j, k] = t
            u.append(2.0 / 3.0 * t)
        msg[j, 0] = a[0] * (cx[0, 0] * u[0])
        spread = a[0] * (cx[0, 1] * u[1]) + in_plane_back(u[0], a, cy, cz, 0) - dg[j, 0] * u[0]
        value = u[0] + time_step * spread
        partial[j] = value
        msg[j, 1] = a[0] * (cx[0, 0] * value)


class Laid:
    def __init__(self, refs):
        self.left = [(ref, start) for ref in refs for start in range(0, ref.shape[0], 8)]

    def put(self, value):
        for start in range(0, value.shape[0], 8):
            ref, at = self.left.pop(0)
            ref[at : at + 8] = value[start : start + 8]


def get(refs, count, rows):
    whole = jnp.concatenate([ref[...] for ref in refs], 0)
    return [whole[rows * k : rows * k + rows] for k in range(count)] + [whole[rows * count :]]


def cut(rows, pieces):
    tiles = rows // 8
    return [8 * (tiles // pieces + (k < tiles % pieces)) for k in range(pieces)]


def turn_inner(scal, weights, final_own, final_far, terms, cx, cy, cz, dg, goals, part, cost, *pins):
    laid = Laid(pins)
    for j in range(2):
        a = rows_of(scal, j)
        u = [2.0 / 3.0 * terms[j, k] for k in range(2)]
        laid.put(a[0] * (cx[1, 1] * u[1]))
        spread = a[0] * (cx[1, 0] * u[0]) + in_plane_back(u[1], a, cy, cz, 1) - dg[j, 1] * u[1]
        value = u[1] + time_step * spread
        part[j] = value
        laid.put(a[0] * (cx[1, 1] * value))
    total = 0.0
    for k in range(2):
        own, far = weights[0] * final_own[k], weights[1] * final_far[k]
        first = own + far
        second = own * final_own[k] + far * final_far[k]
        total = total + goals[k] * (first + variance_gain * (second - first * first))
    rows = total.shape[0]
    total = sum(total[8 * r : 8 * r + 8] for r in range(rows // 8))
    cost[...] = total
    laid.put(total)


def back_second(scal, msgs, partials, part, halo, near, cx, cy, cz, dg, cost_own, *rest):
    base, a2, total = rest[-3:]
    count, rows = (len(rest) - 3) // 2, msgs.shape[2]
    mine, theirs = get(rest[:count], 4, rows), get(rest[count:-3], 4, rows)
    cost = cost_own[...] + theirs[4]
    total[...] = sum(cost[:, 128 * k : 128 * k + 128] for k in range(cost.shape[1] // 128))
    for j in range(2):
        a = rows_of(scal, j)
        pin, pin2 = theirs[2 - 2 * j], theirs[3 - 2 * j]
        pin2 = 0.25 * (pin2 + (time_step * a[0]) * (near[...] * mine[2 * j]))
        a2_i = part[j] + time_step * pin
        a2[j] = a2_i
        u_o, u_i = 0.25 * partials[j], 0.25 * a2_i
        back = (0.25 * time_step * a[0]) * (halo[2] * msgs[j, 0])
        spread = a[0] * (cx[0, 1] * u_i) + in_plane_back(u_o, a, cy, cz, 0) - dg[j, 0] * u_o + back
        base[j, 0] = u_o + time_step * spread
        spread = a[0] * (cx[1, 0] * u_o) + in_plane_back(u_i, a, cy, cz, 1) - dg[j, 1] * u_i + pin2
        base[j, 1] = u_i + time_step * spread


def second_back_edge(scal, halo, base, cx, cy, cz, dg, a1, msg):
    for j in range(2):
        a = rows_of(scal, j)
        step = (0.25 * time_step) * halo[1 - j, 0]
        spread = in_plane_back(step, a, cy, cz, 0) - dg[j, 0] * step + 0.25 * halo[1 - j, 1]
        value = base[j, 0] + step + time_step * spread
        a1[j] = value
        msg[j] = a[0] * (cx[0, 0] * value)


def close(core, scal, terms, partials, halo, a1, a2, base, cx, cy, cz, dg, ctl, cost, cost_far, keep, part, give, total, *send):
    total[...] = cost[...] + cost_far[...]
    laid = Laid(send)
    sources = [0.0, 0.0]
    for j in range(2):
        a = rows_of(scal, j)
        first = halo[1 - j, 0]
        x = [a1[j], base[j, 1] + (0.25 * time_step * time_step * a[0]) * (cx[1, 0] * first)]
        a2_o = partials[j] + time_step * first
        for k, second in enumerate((a2_o, a2[j])):
            sources[k] = sources[k] + a[4] * (2.0 / 3.0 * terms[j, k] + 0.25 * second + x[k])
        spread = a[0] * (cx[0, 1] * x[1]) + in_plane_back(x[0], a, cy, cz, 0) - dg[j, 0] * x[0]
        outer = terms[j, 0] / 3.0 + 0.75 * a2_o + (x[0] + time_step * spread)
        spread = a[0] * (cx[1, 0] * x[0]) + in_plane_back(x[1], a, cy, cz, 1) - dg[j, 1] * x[1]
        inner = terms[j, 1] / 3.0 + 0.75 * a2[j] + (x[1] + time_step * spread)
        pin = a[0] * (cx[1, 1] * x[1])
        part[j] = outer
        if j == 0:
            part[2], part[3] = inner, pin
        else:
            laid.put(inner)
            laid.put(pin)
    half = ctl.shape[2] // 2
    zero = core[0] == 0
    for k in range(2):
        gradient = time_step * sources[k] + penalty * ctl[k]
        low, high = gradient[:, :half], gradient[:, half:]
        keep[k] = jnp.where(zero, low, high)
        give[k] = jnp.where(zero, high, low)


def last_edge(halo, part, cost, cost_far, outer, give, total):
    total[...] = cost[...] + cost_far[...]
    give[...] = part[1] + time_step * halo[0]
    outer[...] = part[0] + time_step * halo[1]


def write_inner(core, part, keep, taken, *rest):
    theirs, (out, gradient) = get(rest[:-2], 2, part.shape[1]), rest[-2:]
    me = core[0]
    out[0, 1 + me] = part[2] + time_step * theirs[1]
    out[0, 2 - me] = theirs[0] + time_step * part[3]
    gradient[3 * me] = keep[0]
    gradient[1 + me] = keep[1]
    gradient[3 - 3 * me] = taken[0]
    gradient[2 - me] = taken[1]


def write_outer(far, core, value, _, out, sem):
    at = 3 * core[0]
    copy = pltpu.make_async_copy(value, out.at[0, 3 - at if far else at], sem)
    copy.start()
    copy.wait()


def finish(cells, cost, objective):
    objective[0] = jnp.sum(cost[...]) / cells


def on_core(body, outs, scalars, arrays, hbm_out=(), smem_out=(), after=(), cost=0, name=None):
    hbm_out = tuple(hbm_out) + tuple(smem_out)
    out_shape = [
        jax.ShapeDtypeStruct(s, jnp.float32) if i in hbm_out else pltpu.VMEM(s, jnp.float32)
        for i, s in enumerate(outs)
    ]
    held = [pltpu.with_memory_space_constraint(x, pltpu.SMEM) for x in scalars]
    held += [pltpu.with_memory_space_constraint(x, pltpu.VMEM) for x in arrays]
    count, waits = len(held), len(after)

    def run(*refs):
        body(*refs[:count], *refs[count + waits :])

    return pl.pallas_call(
        run,
        out_shape=out_shape,
        in_specs=[pl.BlockSpec(memory_space=pltpu.SMEM)] * len(scalars)
        + [pl.BlockSpec(memory_space=pltpu.VMEM)] * len(arrays)
        + [pl.BlockSpec(memory_space=pl.ANY)] * waits,
        out_specs=[
            pl.BlockSpec(memory_space=pltpu.SMEM if i in smem_out else pltpu.VMEM) for i in range(len(outs))
        ],
        compiler_params=pltpu.CompilerParams(vmem_limit_bytes=VMEM_LIMIT),
        cost_estimate=cost_of(cost) if cost else None,
        name=name or body.__name__,
    )(*held, *after)


def shards(
    concentration,
    adjoint_next,
    speed,
    direction_mask,
    decay_rate,
    control,
    goal_weight,
    node_index,
    weight_num,
    step_index,
):
    sections = lax.axis_size("space")
    ranks = sections * lax.axis_size("node")
    within = [(i, i ^ 1) for i in range(ranks)]
    across = [p for i in range(1, ranks - 1, 2) for p in ((i, i + 1), (i + 1, i))]

    def swap(x, what):
        with jax.named_scope("swap_" + what):
            return lax.ppermute(x, AXES, within)

    def pass_on(x, what):
        with jax.named_scope("pass_" + what):
            return lax.ppermute(x, AXES, across)

    _, layers, rows, columns = concentration.shape
    me = lax.axis_index("node").astype(jnp.int32)
    core = jnp.reshape(me, (1,))
    far = swap(concentration, "state")
    plane = (rows, columns)
    pair, four_planes = (2,) + plane, (4,) + plane
    four = (2,) + pair
    sides = (2, rows, columns // 2)
    held = lambda x, space: pltpu.with_memory_space_constraint(x, space)
    (first,) = on_core(begin, [(8, 128)], [], [], cost=LONG)
    (packed,) = on_core(
        pack, [(3,) + plane], [core], [concentration, far, speed, direction_mask], after=[first]
    )
    halo = pass_on(packed, "state")
    numbers = pl.pallas_call(
        gather_numbers,
        out_shape=pltpu.VMEM((8, 128), jnp.float32),
        in_specs=[pl.BlockSpec(memory_space=pltpu.SMEM)] * 3 + [pl.BlockSpec(memory_space=pl.ANY)],
        out_specs=pl.BlockSpec(memory_space=pltpu.VMEM),
        name="gather_numbers",
    )(node_index, weight_num, step_index, packed)
    far_numbers = swap(numbers, "numbers")

    shapes = [four, four, four, four, pair]
    scal, cx, cy, cz, dg, ctl = pl.pallas_call(
        prepare,
        out_shape=[pltpu.SMEM((2, 8), jnp.float32)] + [pltpu.VMEM(s, jnp.float32) for s in shapes],
        in_specs=[pl.BlockSpec(memory_space=pltpu.SMEM)]
        + [pl.BlockSpec(memory_space=pltpu.VMEM)] * 6,
        out_specs=[pl.BlockSpec(memory_space=pltpu.SMEM)] + [pl.BlockSpec(memory_space=pltpu.VMEM)] * len(shapes),
        compiler_params=pltpu.CompilerParams(vmem_limit_bytes=VMEM_LIMIT),
        name="prepare",
    )(
        core,
        *[held(x, pltpu.VMEM) for x in (numbers, far_numbers, speed, direction_mask, decay_rate, control)],
    )
    fields = [cx, cy, cz, dg]
    both = [core, scal]
    states = [concentration, far]
    base, base_q, s1_in = on_core(first_stage, [pair] * 3, both, states + fields + [ctl])
    (msg,) = on_core(
        first_edge, [four], [scal], [halo, base, base_q] + fields, cost=LONG
    )
    halo2 = pass_on(msg, "stage2")
    weights, goals, adj, adj_out_o, adj_out_i = pl.pallas_call(
        prepare_back,
        out_shape=[pltpu.SMEM((2,), jnp.float32)]
        + [pltpu.VMEM(s, jnp.float32) for s in (pair, pair, plane, plane)],
        in_specs=[pl.BlockSpec(memory_space=pltpu.SMEM)]
        + [pl.BlockSpec(memory_space=pltpu.VMEM)] * 4
        + [pl.BlockSpec(memory_space=pl.ANY)],
        out_specs=[pl.BlockSpec(memory_space=pltpu.SMEM)] + [pl.BlockSpec(memory_space=pltpu.VMEM)] * 4,
        compiler_params=pltpu.CompilerParams(vmem_limit_bytes=VMEM_LIMIT),
        name="prepare_back",
    )(
        core,
        held(goal_weight, pltpu.HBM),
        *[held(x, pltpu.VMEM) for x in (numbers, far_numbers)],
        held(adjoint_next, pltpu.HBM),
        msg,
    )
    s1_next, near = pl.pallas_call(
        prepare_next,
        out_shape=[pltpu.VMEM(pair, jnp.float32), pltpu.VMEM(plane, jnp.float32)],
        in_specs=[pl.BlockSpec(memory_space=pltpu.SMEM)] * 2
        + [pl.BlockSpec(memory_space=pltpu.VMEM)] * 6
        + [pl.BlockSpec(memory_space=pl.ANY)],
        out_specs=[pl.BlockSpec(memory_space=pltpu.VMEM)] * 2,
        scratch_shapes=[pltpu.VMEM((2, 1) + plane, jnp.float32)] * 4,
        compiler_params=pltpu.CompilerParams(vmem_limit_bytes=VMEM_LIMIT),
        name="prepare_next",
    )(
        core,
        held(scal, pltpu.SMEM),
        *[held(x, pltpu.VMEM) for x in (speed, direction_mask, decay_rate, control)],
        *[held(x, pltpu.VMEM) for x in states],
        msg,
    )

    after_o, after_i = swap(adj_out_o, "after_o"), swap(adj_out_i, "after_i")

    s2 = list(on_core(second_inner, [plane] * 2, both, states + [msg, s1_in, s1_next] + fields + [ctl]))
    s2_next = [swap(s2[1], "s2_far"), swap(s2[0], "s2_own")]
    (base,) = on_core(third_stage, [four], both, states + [msg] + s2 + s2_next + [halo] + fields + [ctl])
    final_own, final_far, terms, msg3, partials = on_core(
        turn,
        [pair, pair, four, four, pair],
        [scal, weights],
        [halo2, base] + fields + [goals, adj, after_o, after_i],
    )
    halo3 = pass_on(msg3, "back2")
    part, cost, *pins = on_core(
        turn_inner,
        [pair, (8, columns)] + [(r, columns) for r in cut(4 * rows + 8, 3)],
        [scal, weights],
        [final_own, final_far, terms] + fields + [goals],
    )
    theirs = [swap(x, "pin") for x in pins]
    base, a2, cost = on_core(
        back_second,
        [four, pair, (8, 128)],
        [scal],
        [msg3, partials, part, halo, near] + fields + [cost] + pins + theirs,
    )
    whole = sections & (sections - 1) == 0
    steps = [1 << k for k in range(sections.bit_length() - 1)] if whole else []
    steps = steps[1:] + steps[:1]

    def from_pair(x, k):
        with jax.named_scope("goal_sum"):
            if k >= len(steps):
                return jnp.zeros_like(x)
            return lax.ppermute(x, "space", [(i, i ^ steps[k]) for i in range(sections)])

    cost = cost + from_pair(cost, 0)
    a1, msg4 = on_core(second_back_edge, [pair, pair], [scal], [halo3, base] + fields, after=[cost])
    halo4 = pass_on(msg4, "back1")
    keep, part, give, cost, *out = on_core(
        close,
        [sides, four_planes, sides, (8, 128)] + [(r, columns) for r in cut(2 * rows, 2)],
        both,
        [terms, partials, halo3, a1, a2, base] + fields + [ctl, cost, from_pair(cost, 1)],
        cost=2 * LONG,
    )
    parts = [swap(x, "adjoint") for x in out]
    taken = swap(give, "gradient")
    adjoint, gradient = on_core(
        write_inner,
        [(1, layers, rows, columns), (layers, rows, columns // 2)],
        [core],
        [part, keep, taken] + parts,
        hbm_out=(0, 1),
    )
    for k in range(2, len(steps) - 1):
        cost = cost + from_pair(cost, k)
    outer, give, cost = on_core(
        last_edge,
        [plane, plane, (8, 128)],
        [],
        [halo4, part, cost, from_pair(cost, max(2, len(steps) - 1))],
        after=[held(adjoint, pltpu.HBM)],
        cost=LONG,
    )
    if not whole:
        cost = lax.psum(cost, "space")
    cells = sections * layers * rows * columns
    (objective,) = on_core(functools.partial(finish, cells), [(1,)], [], [cost], smem_out=(0,), name="finish")
    for far, value in ((False, outer), (True, swap(give, "outer"))):
        adjoint = pl.pallas_call(
            functools.partial(write_outer, far),
            out_shape=jax.ShapeDtypeStruct(adjoint.shape, jnp.float32),
            in_specs=[
                pl.BlockSpec(memory_space=pltpu.SMEM),
                pl.BlockSpec(memory_space=pltpu.VMEM),
                pl.BlockSpec(memory_space=pl.ANY),
            ],
            out_specs=pl.BlockSpec(memory_space=pl.ANY),
            scratch_shapes=[pltpu.SemaphoreType.DMA],
            input_output_aliases={2: 0},
            compiler_params=pltpu.CompilerParams(vmem_limit_bytes=VMEM_LIMIT),
            name="write_outer",
        )(held(core, pltpu.SMEM), held(value, pltpu.VMEM), held(adjoint, pltpu.HBM))
    return (adjoint, gradient, objective)


def solution(mesh):
    return jax.shard_map(
        shards,
        mesh=mesh,
        in_specs=(
            P("node", ("groups", "space"), None, None),
            P("node", ("groups", "space"), None, None),
            P(None, ("groups", "space"), None, None),
            P(None, ("groups", "space"), None, None),
            P(("groups", "space"), None, None),
            P(("groups", "space"), None, None),
            P(("groups", "space"), None, None),
            P("node", None),
            P("node"),
            P("groups"),
        ),
        out_specs=(
            P("node", ("groups", "space"), None, None),
            P(("groups", "space"), None, "node"),
            P("groups"),
        ),
        check_vma=False,
    )
```

```python
import functools
import math

import jax
import jax.numpy as jnp
from jax import lax
from jax.experimental import pallas as pl
from jax.experimental.pallas import tpu as pltpu
from jax.sharding import PartitionSpec as P

time_step = 0.6
variance_gain = 0.5
penalty = 0.1
weight_denominator = 16.0

VMEM_LIMIT = 24 * 1024 * 1024
AXES = ("space", "node")
LONG = 8


def cost_of(us):
    return pl.CostEstimate(flops=us * 1_000_000_000, bytes_accessed=us * 3_000_000, transcendentals=0)


def roll(value, steps, axis):
    return pltpu.roll(value, steps % value.shape[axis], axis)


def in_plane(value, a, cy, cz, k):
    return a[1] * (cy[0, k] * roll(value, 1, 0) + cy[1, k] * roll(value, -1, 0)) + a[2] * (
        cz[0, k] * roll(value, 1, 1) + cz[1, k] * roll(value, -1, 1)
    )


def in_plane_back(value, a, cy, cz, k):
    return a[1] * (roll(cy[0, k] * value, -1, 0) + roll(cy[1, k] * value, 1, 0)) + a[2] * (
        roll(cz[0, k] * value, -1, 1) + roll(cz[1, k] * value, 1, 1)
    )


def rows_of(scal, j):
    return [scal[j, k] for k in range(5)]


def pick(values, index):
    result = jnp.float32(values[-1])
    for k, value in enumerate(values[:-1]):
        result = jnp.where(index == k, jnp.float32(value), result)
    return result


def node_scales(tiles, scal):
    levels = [-math.cos(math.pi * k / 8.0) for k in range(9)]
    step = tiles[0][0, 9].astype(jnp.int32)
    half = step & 31
    wave = pick([math.sin(2.0 * math.pi * k / 64.0) for k in range(17)], jnp.minimum(half, 32 - half))
    phase = 1.0 + jnp.where(step < 32, 0.5, -0.5) * wave
    for j, tile in enumerate(tiles):
        p = {k: pick(levels, tile[0, k]) for k in (0, 1, 2, 4, 6, 7)}
        scal[j, 0] = 1.0 + 0.3 * p[0]
        scal[j, 1] = 1.0 + 0.3 * p[1]
        scal[j, 2] = (1.0 + 0.3 * p[2]) * (1.0 + 0.2 * p[7])
        scal[j, 3] = pick([math.exp(0.5 * p) for p in levels], tile[0, 3]) * pick(
            [math.exp(0.25 * p) for p in levels], tile[0, 5]
        )
        scal[j, 4] = (1.0 + 0.3 * p[4] + 0.2 * p[6]) * phase


def expand(bits, columns):
    blocks = bits.shape[1]
    spread = (
        lax.broadcasted_iota(jnp.int32, (blocks, columns), 1) // (columns // blocks)
        == lax.broadcasted_iota(jnp.int32, (blocks, columns), 0)
    ).astype(jnp.bfloat16)
    return jnp.dot(bits.astype(jnp.float32).astype(jnp.bfloat16), spread, preferred_element_type=jnp.float32)


def toward_outer(up, me):
    flip = (me == 1).astype(jnp.float32)
    return up + flip - 2.0 * flip * up


def begin(out):
    out[...] = jnp.zeros_like(out)


def gather_numbers(index, weight, step, _, numbers):
    lane = lax.broadcasted_iota(jnp.int32, numbers.shape, 1)
    value = jnp.zeros(numbers.shape, jnp.int32)
    for k, number in enumerate([index[0, k] for k in range(index.shape[1])] + [weight[0], step[0]]):
        value = jnp.where(lane == k, number, value)
    numbers[...] = value.astype(jnp.float32)


def pack(core, own, far, speed, mask, out):
    at = 3 * core[0]
    out[0] = own[0, at]
    out[1] = far[0, at]
    out[2] = speed[0, at].astype(jnp.float32) * toward_outer(expand(mask[0, at], speed.shape[3]), core[0])


def fields_of(k, at, me, speeds, masks, cx, cy, cz):
    rows, columns = speeds.shape[2:]
    row = lax.broadcasted_iota(jnp.int32, (rows, columns), 0)
    column = lax.broadcasted_iota(jnp.int32, (rows, columns), 1)
    up = [expand(masks[d, at], columns) for d in range(3)]
    s = [speeds[d, at].astype(jnp.float32) for d in range(3)]
    outer = s[0] * toward_outer(up[0], me)
    cx[0, k] = outer
    cx[1, k] = s[0] - outer
    lower = s[1] * up[1]
    cy[0, k] = jnp.where(row == 0, 0.0, lower)
    cy[1, k] = jnp.where(row == rows - 1, 0.0, s[1] - lower)
    lower = s[2] * up[2]
    cz[0, k] = jnp.where(column == 0, 0.0, lower)
    cz[1, k] = jnp.where(column == columns - 1, 0.0, s[2] - lower)


def own_of(k, at, rates, speeds, scal, dg):
    s = [speeds[d, at].astype(jnp.float32) for d in range(3)] + [rates[at].astype(jnp.float32)]
    for j in range(2):
        dg[j, k] = sum(scal[j, d] * s[d] for d in range(4))


def prepare(core, own_numbers, far_numbers, speed, mask, decay, control, scal, cx, cy, cz, dg, ctl):
    me = core[0]
    for k, at in enumerate((3 * me, 1 + me)):
        fields_of(k, at, me, speed, mask, cx, cy, cz)
        ctl[k] = control[at]
    node_scales((own_numbers[...], far_numbers[...]), scal)
    for k, at in enumerate((3 * me, 1 + me)):
        own_of(k, at, decay, speed, scal, dg)


def prepare_next(core, scal, speed, mask, decay, control, own, far, _, s1_next, near, cx, cy, cz, dg):
    me = core[0]
    at = 2 - me
    fields_of(0, at, me, speed, mask, cx, cy, cz)
    own_of(0, at, decay, speed, scal, dg)
    near[...] = cx[0, 0]
    for j, c in enumerate((own, far)):
        a = rows_of(scal, j)
        value = c[0, at]
        l = a[0] * (cx[0, 0] * c[0, 1 + me] + cx[1, 0] * c[0, 3 - 3 * me]) + in_plane(value, a, cy, cz, 0) - dg[j, 0] * value
        s1_next[j] = value + time_step * (l + a[4] * control[at])


def prepare_back(core, goal, own_numbers, far_numbers, adjoint, _, weights, goals, adj, adj_out):
    me = core[0]
    weights[0] = own_numbers[...][0, 8] * (1.0 / weight_denominator)
    weights[1] = far_numbers[...][0, 8] * (1.0 / weight_denominator)
    for k, at in enumerate((3 * me, 1 + me)):
        goals[k] = goal[at].astype(jnp.float32)
        adj[k] = adjoint[0, at].astype(jnp.float32)
    adj_out[0] = adjoint[0, 3 - 3 * me].astype(jnp.float32)
    adj_out[1] = adjoint[0, 2 - me].astype(jnp.float32)


def first_stage(core, scal, own, far, cx, cy, cz, dg, ctl, base, base_q, s1_in):
    me = core[0]
    for j, c in enumerate((own, far)):
        a = rows_of(scal, j)
        c_o, c_i = c[0, 3 * me], c[0, 1 + me]
        push = [a[4] * ctl[k] for k in range(2)]
        l_i = a[0] * (cx[0, 1] * c_o + cx[1, 1] * c[0, 2 - me]) + in_plane(c_i, a, cy, cz, 1) - dg[j, 1] * c_i
        s1_i = c_i + time_step * (l_i + push[1])
        s1_in[j] = s1_i
        l_o = a[0] * (cx[1, 0] * c_i) + in_plane(c_o, a, cy, cz, 0) - dg[j, 0] * c_o
        base[j] = c_o + time_step * (l_o + push[0])
        base_q[j] = 0.75 * c_o + (0.25 * time_step) * (a[0] * (cx[1, 0] * s1_i) + push[0])


def first_edge(scal, halo, base, base_q, cx, cy, cz, dg, msg, s1_out):
    for j in range(2):
        a = rows_of(scal, j)
        s1_o = base[j] + (time_step * a[0]) * (cx[0, 0] * halo[1 - j])
        s1_out[j] = s1_o
        msg[j] = base_q[j] + 0.25 * (s1_o + time_step * (in_plane(s1_o, a, cy, cz, 0) - dg[j, 0] * s1_o))


def second_inner(core, scal, own, far, s1_out, s1_in, s1_next, cx, cy, cz, dg, ctl, s2_own, s2_far):
    for j, (c, out) in enumerate(((own, s2_own), (far, s2_far))):
        a = rows_of(scal, j)
        s1_i = s1_in[j]
        l_i = a[0] * (cx[0, 1] * s1_out[j] + cx[1, 1] * s1_next[j]) + in_plane(s1_i, a, cy, cz, 1) - dg[j, 1] * s1_i
        out[...] = 0.75 * c[0, 1 + core[0]] + 0.25 * (s1_i + time_step * (l_i + a[4] * ctl[1]))


def far_part(core, scal, own, far, halo, far_base, cx, step):
    for j, c in enumerate((own, far)):
        s1_h = far_base[1 - j] + (time_step * scal[j, 0]) * (halo[2] * c[0, 3 * core[0]])
        step[j] = (0.25 * time_step * scal[j, 0]) * (cx[0, 0] * s1_h)


def third_stage(core, scal, own, far, msg, s1_out, s2_own, s2_far, next_own, next_far, halo, step, cx, cy, cz, dg, ctl, base):
    me = core[0]
    parts = ((own, s2_own, next_own), (far, s2_far, next_far))
    for j, (c, s2, s2_next) in enumerate(parts):
        a = rows_of(scal, j)
        c_o, s2_i = c[0, 3 * me], s2[...]
        s2_o = msg[j] + step[j]
        back = (0.25 * time_step * a[0]) * (halo[2] * s1_out[j])
        l_o = a[0] * (cx[0, 0] * back + cx[1, 0] * s2_i) + in_plane(s2_o, a, cy, cz, 0) - dg[j, 0] * s2_o
        l_i = a[0] * (cx[0, 1] * s2_o + cx[1, 1] * s2_next[...]) + in_plane(s2_i, a, cy, cz, 1) - dg[j, 1] * s2_i
        base[j, 0] = c_o / 3.0 + 2.0 / 3.0 * (s2_o + time_step * (l_o + a[4] * ctl[0]))
        base[j, 1] = c[0, 1 + me] / 3.0 + 2.0 / 3.0 * (s2_i + time_step * (l_i + a[4] * ctl[1]))


def finals(j, scal, halo, base, cx):
    return base[j, 0] + (2.0 / 3.0 * time_step * scal[j, 0]) * (cx[0, 0] * halo[1 - j]), base[j, 1]


def turn(scal, weights, halo, base, cx, cy, cz, dg, goals, adj, after_far, final_own, final_far, term, msg, partial):
    final_own[0], final_own[1] = finals(0, scal, halo, base, cx)
    final_far[0], final_far[1] = finals(1, scal, halo, base, cx)
    first = [weights[0] * final_own[k] + weights[1] * final_far[k] for k in range(2)]
    for j, (final, after) in enumerate(((final_own, (adj[0], adj[1])), (final_far, (after_far[0], after_far[1])))):
        a = rows_of(scal, j)
        u = []
        for k in range(2):
            t = after[k] + goals[k] * weights[j] * (1.0 + 2.0 * variance_gain * (final[k] - first[k]))
            term[j, k] = t
            u.append(2.0 / 3.0 * t)
        msg[j, 0] = a[0] * (cx[0, 0] * u[0])
        spread = a[0] * (cx[0, 1] * u[1]) + in_plane_back(u[0], a, cy, cz, 0) - dg[j, 0] * u[0]
        value = u[0] + time_step * spread
        partial[j] = value
        msg[j, 1] = a[0] * (cx[0, 0] * value)


class Laid:
    def __init__(self, refs):
        self.left = [(ref, start) for ref in refs for start in range(0, ref.shape[0], 8)]

    def put(self, value):
        for start in range(0, value.shape[0], 8):
            ref, at = self.left.pop(0)
            ref[at : at + 8] = value[start : start + 8]


def get(refs, count, rows):
    whole = jnp.concatenate([ref[...] for ref in refs], 0)
    return [whole[rows * k : rows * k + rows] for k in range(count)] + [whole[rows * count :]]


def cut(rows, pieces):
    tiles = rows // 8
    return [8 * (tiles // pieces + (k < tiles % pieces)) for k in range(pieces)]


def turn_inner(scal, weights, final_own, final_far, terms, cx, cy, cz, dg, goals, part, cost, *pins):
    laid = Laid(pins)
    for j in range(2):
        a = rows_of(scal, j)
        u = [2.0 / 3.0 * terms[j, k] for k in range(2)]
        laid.put(a[0] * (cx[1, 1] * u[1]))
        spread = a[0] * (cx[1, 0] * u[0]) + in_plane_back(u[1], a, cy, cz, 1) - dg[j, 1] * u[1]
        value = u[1] + time_step * spread
        part[j] = value
        laid.put(a[0] * (cx[1, 1] * value))
    total = 0.0
    for k in range(2):
        own, far = weights[0] * final_own[k], weights[1] * final_far[k]
        first = own + far
        second = own * final_own[k] + far * final_far[k]
        total = total + goals[k] * (first + variance_gain * (second - first * first))
    rows = total.shape[0]
    total = sum(total[8 * r : 8 * r + 8] for r in range(rows // 8))
    cost[...] = total
    laid.put(total)


def back_second(scal, msgs, partials, part, halo, near, cx, cy, cz, dg, cost_own, *rest):
    base, a2, total = rest[-3:]
    count, rows = (len(rest) - 3) // 2, msgs.shape[2]
    mine, theirs = get(rest[:count], 4, rows), get(rest[count:-3], 4, rows)
    cost = cost_own[...] + theirs[4]
    total[...] = sum(cost[:, 128 * k : 128 * k + 128] for k in range(cost.shape[1] // 128))
    for j in range(2):
        a = rows_of(scal, j)
        pin, pin2 = theirs[2 - 2 * j], theirs[3 - 2 * j]
        pin2 = 0.25 * (pin2 + (time_step * a[0]) * (near[...] * mine[2 * j]))
        a2_i = part[j] + time_step * pin
        a2[j] = a2_i
        u_o, u_i = 0.25 * partials[j], 0.25 * a2_i
        back = (0.25 * time_step * a[0]) * (halo[2] * msgs[j, 0])
        spread = a[0] * (cx[0, 1] * u_i) + in_plane_back(u_o, a, cy, cz, 0) - dg[j, 0] * u_o + back
        base[j, 0] = u_o + time_step * spread
        spread = a[0] * (cx[1, 0] * u_o) + in_plane_back(u_i, a, cy, cz, 1) - dg[j, 1] * u_i + pin2
        base[j, 1] = u_i + time_step * spread


def second_back_edge(scal, halo, base, cx, cy, cz, dg, a1, msg):
    for j in range(2):
        a = rows_of(scal, j)
        step = (0.25 * time_step) * halo[1 - j, 0]
        spread = in_plane_back(step, a, cy, cz, 0) - dg[j, 0] * step + 0.25 * halo[1 - j, 1]
        value = base[j, 0] + step + time_step * spread
        a1[j] = value
        msg[j] = a[0] * (cx[0, 0] * value)


def close(core, scal, terms, partials, halo, a1, a2, base, cx, cy, cz, dg, ctl, cost, cost_far, keep, part, give, total, *send):
    total[...] = cost[...] + cost_far[...]
    laid = Laid(send)
    sources = [0.0, 0.0]
    for j in range(2):
        a = rows_of(scal, j)
        first = halo[1 - j, 0]
        x = [a1[j], base[j, 1] + (0.25 * time_step * time_step * a[0]) * (cx[1, 0] * first)]
        a2_o = partials[j] + time_step * first
        for k, second in enumerate((a2_o, a2[j])):
            sources[k] = sources[k] + a[4] * (2.0 / 3.0 * terms[j, k] + 0.25 * second + x[k])
        spread = a[0] * (cx[0, 1] * x[1]) + in_plane_back(x[0], a, cy, cz, 0) - dg[j, 0] * x[0]
        outer = terms[j, 0] / 3.0 + 0.75 * a2_o + (x[0] + time_step * spread)
        spread = a[0] * (cx[1, 0] * x[0]) + in_plane_back(x[1], a, cy, cz, 1) - dg[j, 1] * x[1]
        inner = terms[j, 1] / 3.0 + 0.75 * a2[j] + (x[1] + time_step * spread)
        pin = a[0] * (cx[1, 1] * x[1])
        part[j] = outer
        if j == 0:
            part[2], part[3] = inner, pin
        else:
            laid.put(inner)
            laid.put(pin)
    half = ctl.shape[2] // 2
    zero = core[0] == 0
    for k in range(2):
        gradient = time_step * sources[k] + penalty * ctl[k]
        low, high = gradient[:, :half], gradient[:, half:]
        keep[k] = jnp.where(zero, low, high)
        give[k] = jnp.where(zero, high, low)


def last_edge(halo, part, cost, cost_far, outer, give, total):
    total[...] = cost[...] + cost_far[...]
    give[...] = part[1] + time_step * halo[0]
    outer[...] = part[0] + time_step * halo[1]


def write_inner(core, part, keep, taken, *rest):
    theirs, (out, gradient) = get(rest[:-2], 2, part.shape[1]), rest[-2:]
    me = core[0]
    out[0, 1 + me] = part[2] + time_step * theirs[1]
    out[0, 2 - me] = theirs[0] + time_step * part[3]
    gradient[3 * me] = keep[0]
    gradient[1 + me] = keep[1]
    gradient[3 - 3 * me] = taken[0]
    gradient[2 - me] = taken[1]


def write_outer(far, core, value, _, out, sem):
    at = 3 * core[0]
    copy = pltpu.make_async_copy(value, out.at[0, 3 - at if far else at], sem)
    copy.start()
    copy.wait()


def finish(cells, cost, objective):
    objective[0] = jnp.sum(cost[...]) / cells


def on_core(body, outs, scalars, arrays, hbm_out=(), smem_out=(), after=(), cost=0, name=None):
    hbm_out = tuple(hbm_out) + tuple(smem_out)
    out_shape = [
        jax.ShapeDtypeStruct(s, jnp.float32) if i in hbm_out else pltpu.VMEM(s, jnp.float32)
        for i, s in enumerate(outs)
    ]
    held = [pltpu.with_memory_space_constraint(x, pltpu.SMEM) for x in scalars]
    held += [pltpu.with_memory_space_constraint(x, pltpu.VMEM) for x in arrays]
    count, waits = len(held), len(after)

    def run(*refs):
        body(*refs[:count], *refs[count + waits :])

    return pl.pallas_call(
        run,
        out_shape=out_shape,
        in_specs=[pl.BlockSpec(memory_space=pltpu.SMEM)] * len(scalars)
        + [pl.BlockSpec(memory_space=pltpu.VMEM)] * len(arrays)
        + [pl.BlockSpec(memory_space=pl.ANY)] * waits,
        out_specs=[
            pl.BlockSpec(memory_space=pltpu.SMEM if i in smem_out else pltpu.VMEM) for i in range(len(outs))
        ],
        compiler_params=pltpu.CompilerParams(vmem_limit_bytes=VMEM_LIMIT),
        cost_estimate=cost_of(cost) if cost else None,
        name=name or body.__name__,
    )(*held, *after)


def shards(
    concentration,
    adjoint_next,
    speed,
    direction_mask,
    decay_rate,
    control,
    goal_weight,
    node_index,
    weight_num,
    step_index,
):
    sections = lax.axis_size("space")
    ranks = sections * lax.axis_size("node")
    within = [(i, i ^ 1) for i in range(ranks)]
    across = [p for i in range(1, ranks - 1, 2) for p in ((i, i + 1), (i + 1, i))]

    def swap(x, what):
        with jax.named_scope("swap_" + what):
            return lax.ppermute(x, AXES, within)

    def pass_on(x, what):
        with jax.named_scope("pass_" + what):
            return lax.ppermute(x, AXES, across)

    _, layers, rows, columns = concentration.shape
    me = lax.axis_index("node").astype(jnp.int32)
    core = jnp.reshape(me, (1,))
    far = swap(concentration, "state")
    plane = (rows, columns)
    pair, four_planes = (2,) + plane, (4,) + plane
    four = (2,) + pair
    sides = (2, rows, columns // 2)
    held = lambda x, space: pltpu.with_memory_space_constraint(x, space)
    (first,) = on_core(begin, [(8, 128)], [], [], cost=LONG)
    (packed,) = on_core(
        pack, [(3,) + plane], [core], [concentration, far, speed, direction_mask], after=[first]
    )
    halo = pass_on(packed, "state")
    numbers = pl.pallas_call(
        gather_numbers,
        out_shape=pltpu.VMEM((8, 128), jnp.float32),
        in_specs=[pl.BlockSpec(memory_space=pltpu.SMEM)] * 3 + [pl.BlockSpec(memory_space=pl.ANY)],
        out_specs=pl.BlockSpec(memory_space=pltpu.VMEM),
        name="gather_numbers",
    )(node_index, weight_num, step_index, packed)
    far_numbers = swap(numbers, "numbers")

    shapes = [four, four, four, four, pair]
    scal, cx, cy, cz, dg, ctl = pl.pallas_call(
        prepare,
        out_shape=[pltpu.SMEM((2, 8), jnp.float32)] + [pltpu.VMEM(s, jnp.float32) for s in shapes],
        in_specs=[pl.BlockSpec(memory_space=pltpu.SMEM)]
        + [pl.BlockSpec(memory_space=pltpu.VMEM)] * 6,
        out_specs=[pl.BlockSpec(memory_space=pltpu.SMEM)] + [pl.BlockSpec(memory_space=pltpu.VMEM)] * len(shapes),
        compiler_params=pltpu.CompilerParams(vmem_limit_bytes=VMEM_LIMIT),
        name="prepare",
    )(
        core,
        *[held(x, pltpu.VMEM) for x in (numbers, far_numbers, speed, direction_mask, decay_rate, control)],
    )
    fields = [cx, cy, cz, dg]
    both = [core, scal]
    states = [concentration, far]
    base, base_q, s1_in = on_core(first_stage, [pair] * 3, both, states + fields + [ctl])
    far_base = pass_on(base, "stage1")
    msg, s1_out = on_core(
        first_edge, [pair, pair], [scal], [halo, base, base_q] + fields, cost=LONG
    )
    halo2 = pass_on(msg, "stage2")
    weights, goals, adj, adj_out = pl.pallas_call(
        prepare_back,
        out_shape=[pltpu.SMEM((2,), jnp.float32)]
        + [pltpu.VMEM(s, jnp.float32) for s in (pair, pair, pair)],
        in_specs=[pl.BlockSpec(memory_space=pltpu.SMEM)]
        + [pl.BlockSpec(memory_space=pltpu.VMEM)] * 4
        + [pl.BlockSpec(memory_space=pl.ANY)],
        out_specs=[pl.BlockSpec(memory_space=pltpu.SMEM)] + [pl.BlockSpec(memory_space=pltpu.VMEM)] * 3,
        compiler_params=pltpu.CompilerParams(vmem_limit_bytes=VMEM_LIMIT),
        name="prepare_back",
    )(
        core,
        held(goal_weight, pltpu.HBM),
        *[held(x, pltpu.VMEM) for x in (numbers, far_numbers)],
        held(adjoint_next, pltpu.HBM),
        msg,
    )
    s1_next, near = pl.pallas_call(
        prepare_next,
        out_shape=[pltpu.VMEM(pair, jnp.float32), pltpu.VMEM(plane, jnp.float32)],
        in_specs=[pl.BlockSpec(memory_space=pltpu.SMEM)] * 2
        + [pl.BlockSpec(memory_space=pltpu.VMEM)] * 6
        + [pl.BlockSpec(memory_space=pl.ANY)],
        out_specs=[pl.BlockSpec(memory_space=pltpu.VMEM)] * 2,
        scratch_shapes=[pltpu.VMEM((2, 1) + plane, jnp.float32)] * 4,
        compiler_params=pltpu.CompilerParams(vmem_limit_bytes=VMEM_LIMIT),
        name="prepare_next",
    )(
        core,
        held(scal, pltpu.SMEM),
        *[held(x, pltpu.VMEM) for x in (speed, direction_mask, decay_rate, control)],
        *[held(x, pltpu.VMEM) for x in states],
        msg,
    )

    after = swap(adj_out, "after")

    (far_step,) = on_core(far_part, [pair], both, states + [halo, far_base, cx], cost=LONG)
    s2 = list(on_core(second_inner, [plane] * 2, both, states + [s1_out, s1_in, s1_next] + fields + [ctl]))
    s2_next = [swap(s2[1], "s2_far"), swap(s2[0], "s2_own")]
    (base,) = on_core(third_stage, [four], both, states + [msg, s1_out] + s2 + s2_next + [halo, far_step] + fields + [ctl])
    final_own, final_far, terms, msg3, partials = on_core(
        turn,
        [pair, pair, four, four, pair],
        [scal, weights],
        [halo2, base] + fields + [goals, adj, after],
    )
    halo3 = pass_on(msg3, "back2")
    part, cost, *pins = on_core(
        turn_inner,
        [pair, (8, columns)] + [(r, columns) for r in cut(4 * rows + 8, 3)],
        [scal, weights],
        [final_own, final_far, terms] + fields + [goals],
    )
    theirs = [swap(x, "pin") for x in pins]
    base, a2, cost = on_core(
        back_second,
        [four, pair, (8, 128)],
        [scal],
        [msg3, partials, part, halo, near] + fields + [cost] + pins + theirs,
    )
    whole = sections & (sections - 1) == 0
    steps = [1 << k for k in range(sections.bit_length() - 1)] if whole else []
    steps = steps[1:] + steps[:1]

    def from_pair(x, k):
        with jax.named_scope("goal_sum"):
            if k >= len(steps):
                return jnp.zeros_like(x)
            return lax.ppermute(x, "space", [(i, i ^ steps[k]) for i in range(sections)])

    cost = cost + from_pair(cost, 0)
    a1, msg4 = on_core(second_back_edge, [pair, pair], [scal], [halo3, base] + fields, after=[cost])
    halo4 = pass_on(msg4, "back1")
    keep, part, give, cost, *out = on_core(
        close,
        [sides, four_planes, sides, (8, 128)] + [(r, columns) for r in cut(2 * rows, 2)],
        both,
        [terms, partials, halo3, a1, a2, base] + fields + [ctl, cost, from_pair(cost, 1)],
        cost=2 * LONG,
    )
    parts = [swap(x, "adjoint") for x in out]
    taken = swap(give, "gradient")
    adjoint, gradient = on_core(
        write_inner,
        [(1, layers, rows, columns), (layers, rows, columns // 2)],
        [core],
        [part, keep, taken] + parts,
        hbm_out=(0, 1),
    )
    for k in range(2, len(steps) - 1):
        cost = cost + from_pair(cost, k)
    outer, give, cost = on_core(
        last_edge,
        [plane, plane, (8, 128)],
        [],
        [halo4, part, cost, from_pair(cost, max(2, len(steps) - 1))],
        after=[held(adjoint, pltpu.HBM)],
        cost=LONG,
    )
    if not whole:
        cost = lax.psum(cost, "space")
    cells = sections * layers * rows * columns
    (objective,) = on_core(functools.partial(finish, cells), [(1,)], [], [cost], smem_out=(0,), name="finish")
    for far, value in ((False, outer), (True, swap(give, "outer"))):
        adjoint = pl.pallas_call(
            functools.partial(write_outer, far),
            out_shape=jax.ShapeDtypeStruct(adjoint.shape, jnp.float32),
            in_specs=[
                pl.BlockSpec(memory_space=pltpu.SMEM),
                pl.BlockSpec(memory_space=pltpu.VMEM),
                pl.BlockSpec(memory_space=pl.ANY),
            ],
            out_specs=pl.BlockSpec(memory_space=pl.ANY),
            scratch_shapes=[pltpu.SemaphoreType.DMA],
            input_output_aliases={2: 0},
            compiler_params=pltpu.CompilerParams(vmem_limit_bytes=VMEM_LIMIT),
            name="write_outer",
        )(held(core, pltpu.SMEM), held(value, pltpu.VMEM), held(adjoint, pltpu.HBM))
    return (adjoint, gradient, objective)


def solution(mesh):
    return jax.shard_map(
        shards,
        mesh=mesh,
        in_specs=(
            P("node", ("groups", "space"), None, None),
            P("node", ("groups", "space"), None, None),
            P(None, ("groups", "space"), None, None),
            P(None, ("groups", "space"), None, None),
            P(("groups", "space"), None, None),
            P(("groups", "space"), None, None),
            P(("groups", "space"), None, None),
            P("node", None),
            P("node"),
            P("groups"),
        ),
        out_specs=(
            P("node", ("groups", "space"), None, None),
            P(("groups", "space"), None, "node"),
            P("groups"),
        ),
        check_vma=False,
    )
```

```python
import functools
import math

import jax
import jax.numpy as jnp
from jax import lax
from jax.experimental import pallas as pl
from jax.experimental.pallas import tpu as pltpu
from jax.sharding import PartitionSpec as P

time_step = 0.6
variance_gain = 0.5
penalty = 0.1
weight_denominator = 16.0

VMEM_LIMIT = 8 * 1024 * 1024
AXES = ("space", "node")
LONG = 8


def cost_of(us):
    return pl.CostEstimate(flops=us * 1_000_000_000, bytes_accessed=us * 3_000_000, transcendentals=0)


def roll(value, steps, axis):
    return pltpu.roll(value, steps % value.shape[axis], axis)


def in_plane(value, a, cy, cz, k):
    return a[1] * (cy[0, k] * roll(value, 1, 0) + cy[1, k] * roll(value, -1, 0)) + a[2] * (
        cz[0, k] * roll(value, 1, 1) + cz[1, k] * roll(value, -1, 1)
    )


def in_plane_back(value, a, cy, cz, k):
    return a[1] * (roll(cy[0, k] * value, -1, 0) + roll(cy[1, k] * value, 1, 0)) + a[2] * (
        roll(cz[0, k] * value, -1, 1) + roll(cz[1, k] * value, 1, 1)
    )


def rows_of(scal, j):
    return [scal[j, k] for k in range(5)]


def pick(values, index):
    result = jnp.float32(values[-1])
    for k, value in enumerate(values[:-1]):
        result = jnp.where(index == k, jnp.float32(value), result)
    return result


def node_scales(tiles, scal):
    levels = [-math.cos(math.pi * k / 8.0) for k in range(9)]
    step = tiles[0][0, 9].astype(jnp.int32)
    half = step & 31
    wave = pick([math.sin(2.0 * math.pi * k / 64.0) for k in range(17)], jnp.minimum(half, 32 - half))
    phase = 1.0 + jnp.where(step < 32, 0.5, -0.5) * wave
    for j, tile in enumerate(tiles):
        p = {k: pick(levels, tile[0, k]) for k in (0, 1, 2, 4, 6, 7)}
        scal[j, 0] = 1.0 + 0.3 * p[0]
        scal[j, 1] = 1.0 + 0.3 * p[1]
        scal[j, 2] = (1.0 + 0.3 * p[2]) * (1.0 + 0.2 * p[7])
        scal[j, 3] = pick([math.exp(0.5 * p) for p in levels], tile[0, 3]) * pick(
            [math.exp(0.25 * p) for p in levels], tile[0, 5]
        )
        scal[j, 4] = (1.0 + 0.3 * p[4] + 0.2 * p[6]) * phase


def expand(bits, columns):
    blocks = bits.shape[1]
    spread = (
        lax.broadcasted_iota(jnp.int32, (blocks, columns), 1) // (columns // blocks)
        == lax.broadcasted_iota(jnp.int32, (blocks, columns), 0)
    ).astype(jnp.bfloat16)
    return jnp.dot(bits.astype(jnp.float32).astype(jnp.bfloat16), spread, preferred_element_type=jnp.float32)


def toward_outer(up, me):
    flip = (me == 1).astype(jnp.float32)
    return up + flip - 2.0 * flip * up


def begin(out):
    out[...] = jnp.zeros_like(out)


def gather_numbers(index, weight, step, _, numbers):
    lane = lax.broadcasted_iota(jnp.int32, numbers.shape, 1)
    value = jnp.zeros(numbers.shape, jnp.int32)
    for k, number in enumerate([index[0, k] for k in range(index.shape[1])] + [weight[0], step[0]]):
        value = jnp.where(lane == k, number, value)
    numbers[...] = value.astype(jnp.float32)


def pack(core, own, far, speed, mask, out):
    at = 3 * core[0]
    out[0] = own[0, at]
    out[1] = far[0, at]
    out[2] = speed[0, at].astype(jnp.float32) * toward_outer(expand(mask[0, at], speed.shape[3]), core[0])


def fields_of(k, at, me, speeds, masks, cx, cy, cz):
    rows, columns = speeds.shape[2:]
    row = lax.broadcasted_iota(jnp.int32, (rows, columns), 0)
    column = lax.broadcasted_iota(jnp.int32, (rows, columns), 1)
    up = [expand(masks[d, at], columns) for d in range(3)]
    s = [speeds[d, at].astype(jnp.float32) for d in range(3)]
    outer = s[0] * toward_outer(up[0], me)
    cx[0, k] = outer
    cx[1, k] = s[0] - outer
    lower = s[1] * up[1]
    cy[0, k] = jnp.where(row == 0, 0.0, lower)
    cy[1, k] = jnp.where(row == rows - 1, 0.0, s[1] - lower)
    lower = s[2] * up[2]
    cz[0, k] = jnp.where(column == 0, 0.0, lower)
    cz[1, k] = jnp.where(column == columns - 1, 0.0, s[2] - lower)


def own_of(k, at, rates, speeds, scal, dg):
    s = [speeds[d, at].astype(jnp.float32) for d in range(3)] + [rates[at].astype(jnp.float32)]
    for j in range(2):
        dg[j, k] = sum(scal[j, d] * s[d] for d in range(4))


def prepare(core, own_numbers, far_numbers, speed, mask, decay, control, scal, cx, cy, cz, dg, ctl):
    me = core[0]
    for k, at in enumerate((3 * me, 1 + me)):
        fields_of(k, at, me, speed, mask, cx, cy, cz)
        ctl[k] = control[at]
    node_scales((own_numbers[...], far_numbers[...]), scal)
    for k, at in enumerate((3 * me, 1 + me)):
        own_of(k, at, decay, speed, scal, dg)


def prepare_next(core, scal, speed, mask, decay, control, own, far, _, s1_next, near, cx, cy, cz, dg):
    me = core[0]
    at = 2 - me
    fields_of(0, at, me, speed, mask, cx, cy, cz)
    own_of(0, at, decay, speed, scal, dg)
    near[...] = cx[0, 0]
    for j, c in enumerate((own, far)):
        a = rows_of(scal, j)
        value = c[0, at]
        l = a[0] * (cx[0, 0] * c[0, 1 + me] + cx[1, 0] * c[0, 3 - 3 * me]) + in_plane(value, a, cy, cz, 0) - dg[j, 0] * value
        s1_next[j] = value + time_step * (l + a[4] * control[at])


def prepare_back(core, goal, own_numbers, far_numbers, adjoint, _, weights, goals, adj, adj_out):
    me = core[0]
    weights[0] = own_numbers[...][0, 8] * (1.0 / weight_denominator)
    weights[1] = far_numbers[...][0, 8] * (1.0 / weight_denominator)
    for k, at in enumerate((3 * me, 1 + me)):
        goals[k] = goal[at].astype(jnp.float32)
        adj[k] = adjoint[0, at].astype(jnp.float32)
    adj_out[0] = adjoint[0, 3 - 3 * me].astype(jnp.float32)
    adj_out[1] = adjoint[0, 2 - me].astype(jnp.float32)


def first_stage(core, scal, own, far, cx, cy, cz, dg, ctl, base, base_q, s1_in):
    me = core[0]
    for j, c in enumerate((own, far)):
        a = rows_of(scal, j)
        c_o, c_i = c[0, 3 * me], c[0, 1 + me]
        push = [a[4] * ctl[k] for k in range(2)]
        l_i = a[0] * (cx[0, 1] * c_o + cx[1, 1] * c[0, 2 - me]) + in_plane(c_i, a, cy, cz, 1) - dg[j, 1] * c_i
        s1_i = c_i + time_step * (l_i + push[1])
        s1_in[j] = s1_i
        l_o = a[0] * (cx[1, 0] * c_i) + in_plane(c_o, a, cy, cz, 0) - dg[j, 0] * c_o
        base[j] = c_o + time_step * (l_o + push[0])
        base_q[j] = 0.75 * c_o + (0.25 * time_step) * (a[0] * (cx[1, 0] * s1_i) + push[0])


def first_edge(scal, halo, base, base_q, cx, cy, cz, dg, msg, s1_out):
    for j in range(2):
        a = rows_of(scal, j)
        s1_o = base[j] + (time_step * a[0]) * (cx[0, 0] * halo[1 - j])
        s1_out[j] = s1_o
        msg[j] = base_q[j] + 0.25 * (s1_o + time_step * (in_plane(s1_o, a, cy, cz, 0) - dg[j, 0] * s1_o))


def second_inner(core, scal, own, far, s1_out, s1_in, s1_next, cx, cy, cz, dg, ctl, s2_own, s2_far):
    for j, (c, out) in enumerate(((own, s2_own), (far, s2_far))):
        a = rows_of(scal, j)
        s1_i = s1_in[j]
        l_i = a[0] * (cx[0, 1] * s1_out[j] + cx[1, 1] * s1_next[j]) + in_plane(s1_i, a, cy, cz, 1) - dg[j, 1] * s1_i
        out[...] = 0.75 * c[0, 1 + core[0]] + 0.25 * (s1_i + time_step * (l_i + a[4] * ctl[1]))


def far_part(core, scal, own, far, halo, far_base, cx, step):
    for j, c in enumerate((own, far)):
        s1_h = far_base[1 - j] + (time_step * scal[j, 0]) * (halo[2] * c[0, 3 * core[0]])
        step[j] = (0.25 * time_step * scal[j, 0]) * (cx[0, 0] * s1_h)


def third_stage(core, scal, own, far, msg, s1_out, s2_own, s2_far, next_own, next_far, halo, step, cx, cy, cz, dg, ctl, base):
    me = core[0]
    parts = ((own, s2_own, next_own), (far, s2_far, next_far))
    for j, (c, s2, s2_next) in enumerate(parts):
        a = rows_of(scal, j)
        c_o, s2_i = c[0, 3 * me], s2[...]
        s2_o = msg[j] + step[j]
        back = (0.25 * time_step * a[0]) * (halo[2] * s1_out[j])
        l_o = a[0] * (cx[0, 0] * back + cx[1, 0] * s2_i) + in_plane(s2_o, a, cy, cz, 0) - dg[j, 0] * s2_o
        l_i = a[0] * (cx[0, 1] * s2_o + cx[1, 1] * s2_next[...]) + in_plane(s2_i, a, cy, cz, 1) - dg[j, 1] * s2_i
        base[j, 0] = c_o / 3.0 + 2.0 / 3.0 * (s2_o + time_step * (l_o + a[4] * ctl[0]))
        base[j, 1] = c[0, 1 + me] / 3.0 + 2.0 / 3.0 * (s2_i + time_step * (l_i + a[4] * ctl[1]))


def finals(j, scal, halo, base, cx):
    return base[j, 0] + (2.0 / 3.0 * time_step * scal[j, 0]) * (cx[0, 0] * halo[1 - j]), base[j, 1]


def turn(scal, weights, halo, base, cx, cy, cz, dg, goals, adj, after_far, final_own, final_far, term, msg, partial):
    final_own[0], final_own[1] = finals(0, scal, halo, base, cx)
    final_far[0], final_far[1] = finals(1, scal, halo, base, cx)
    first = [weights[0] * final_own[k] + weights[1] * final_far[k] for k in range(2)]
    for j, (final, after) in enumerate(((final_own, (adj[0], adj[1])), (final_far, (after_far[0], after_far[1])))):
        a = rows_of(scal, j)
        u = []
        for k in range(2):
            t = after[k] + goals[k] * weights[j] * (1.0 + 2.0 * variance_gain * (final[k] - first[k]))
            term[j, k] = t
            u.append(2.0 / 3.0 * t)
        msg[j, 0] = a[0] * (cx[0, 0] * u[0])
        spread = a[0] * (cx[0, 1] * u[1]) + in_plane_back(u[0], a, cy, cz, 0) - dg[j, 0] * u[0]
        value = u[0] + time_step * spread
        partial[j] = value
        msg[j, 1] = a[0] * (cx[0, 0] * value)


class Laid:
    def __init__(self, refs):
        self.left = [(ref, start) for ref in refs for start in range(0, ref.shape[0], 8)]

    def put(self, value):
        for start in range(0, value.shape[0], 8):
            ref, at = self.left.pop(0)
            ref[at : at + 8] = value[start : start + 8]


def get(refs, count, rows):
    whole = jnp.concatenate([ref[...] for ref in refs], 0)
    return [whole[rows * k : rows * k + rows] for k in range(count)] + [whole[rows * count :]]


def cut(rows, pieces):
    tiles = rows // 8
    return [8 * (tiles // pieces + (k < tiles % pieces)) for k in range(pieces)]


def turn_inner(scal, weights, final_own, final_far, terms, cx, cy, cz, dg, goals, part, cost, *pins):
    laid = Laid(pins)
    for j in range(2):
        a = rows_of(scal, j)
        u = [2.0 / 3.0 * terms[j, k] for k in range(2)]
        laid.put(a[0] * (cx[1, 1] * u[1]))
        spread = a[0] * (cx[1, 0] * u[0]) + in_plane_back(u[1], a, cy, cz, 1) - dg[j, 1] * u[1]
        value = u[1] + time_step * spread
        part[j] = value
        laid.put(a[0] * (cx[1, 1] * value))
    total = 0.0
    for k in range(2):
        own, far = weights[0] * final_own[k], weights[1] * final_far[k]
        first = own + far
        second = own * final_own[k] + far * final_far[k]
        total = total + goals[k] * (first + variance_gain * (second - first * first))
    rows = total.shape[0]
    total = sum(total[8 * r : 8 * r + 8] for r in range(rows // 8))
    cost[...] = total
    laid.put(total)


def back_second(scal, msgs, partials, part, halo, near, cx, cy, cz, dg, cost_own, *rest):
    base, a2, total = rest[-3:]
    count, rows = (len(rest) - 3) // 2, msgs.shape[2]
    mine, theirs = get(rest[:count], 4, rows), get(rest[count:-3], 4, rows)
    cost = cost_own[...] + theirs[4]
    total[...] = sum(cost[:, 128 * k : 128 * k + 128] for k in range(cost.shape[1] // 128))
    for j in range(2):
        a = rows_of(scal, j)
        pin, pin2 = theirs[2 - 2 * j], theirs[3 - 2 * j]
        pin2 = 0.25 * (pin2 + (time_step * a[0]) * (near[...] * mine[2 * j]))
        a2_i = part[j] + time_step * pin
        a2[j] = a2_i
        u_o, u_i = 0.25 * partials[j], 0.25 * a2_i
        back = (0.25 * time_step * a[0]) * (halo[2] * msgs[j, 0])
        spread = a[0] * (cx[0, 1] * u_i) + in_plane_back(u_o, a, cy, cz, 0) - dg[j, 0] * u_o + back
        base[j, 0] = u_o + time_step * spread
        spread = a[0] * (cx[1, 0] * u_o) + in_plane_back(u_i, a, cy, cz, 1) - dg[j, 1] * u_i + pin2
        base[j, 1] = u_i + time_step * spread


def second_back_edge(scal, halo, base, cx, cy, cz, dg, a1, msg):
    for j in range(2):
        a = rows_of(scal, j)
        step = (0.25 * time_step) * halo[1 - j, 0]
        spread = in_plane_back(step, a, cy, cz, 0) - dg[j, 0] * step + 0.25 * halo[1 - j, 1]
        value = base[j, 0] + step + time_step * spread
        a1[j] = value
        msg[j] = a[0] * (cx[0, 0] * value)


def close(core, scal, terms, partials, halo, a1, a2, base, cx, cy, cz, dg, ctl, cost, cost_far, keep, part, give, total, *send):
    total[...] = cost[...] + cost_far[...]
    laid = Laid(send)
    sources = [0.0, 0.0]
    for j in range(2):
        a = rows_of(scal, j)
        first = halo[1 - j, 0]
        x = [a1[j], base[j, 1] + (0.25 * time_step * time_step * a[0]) * (cx[1, 0] * first)]
        a2_o = partials[j] + time_step * first
        for k, second in enumerate((a2_o, a2[j])):
            sources[k] = sources[k] + a[4] * (2.0 / 3.0 * terms[j, k] + 0.25 * second + x[k])
        spread = a[0] * (cx[0, 1] * x[1]) + in_plane_back(x[0], a, cy, cz, 0) - dg[j, 0] * x[0]
        outer = terms[j, 0] / 3.0 + 0.75 * a2_o + (x[0] + time_step * spread)
        spread = a[0] * (cx[1, 0] * x[0]) + in_plane_back(x[1], a, cy, cz, 1) - dg[j, 1] * x[1]
        inner = terms[j, 1] / 3.0 + 0.75 * a2[j] + (x[1] + time_step * spread)
        pin = a[0] * (cx[1, 1] * x[1])
        part[j] = outer
        if j == 0:
            part[2], part[3] = inner, pin
        else:
            laid.put(inner)
            laid.put(pin)
    half = ctl.shape[2] // 2
    zero = core[0] == 0
    for k in range(2):
        gradient = time_step * sources[k] + penalty * ctl[k]
        low, high = gradient[:, :half], gradient[:, half:]
        keep[k] = jnp.where(zero, low, high)
        give[k] = jnp.where(zero, high, low)


def last_edge(halo, part, cost, cost_far, outer, give, total):
    total[...] = cost[...] + cost_far[...]
    give[...] = part[1] + time_step * halo[0]
    outer[...] = part[0] + time_step * halo[1]


def write_inner(core, part, keep, taken, *rest):
    theirs, (out, gradient) = get(rest[:-2], 2, part.shape[1]), rest[-2:]
    me = core[0]
    out[0, 1 + me] = part[2] + time_step * theirs[1]
    out[0, 2 - me] = theirs[0] + time_step * part[3]
    gradient[3 * me] = keep[0]
    gradient[1 + me] = keep[1]
    gradient[3 - 3 * me] = taken[0]
    gradient[2 - me] = taken[1]


def write_outer(far, core, value, _, out, sem):
    at = 3 * core[0]
    copy = pltpu.make_async_copy(value, out.at[0, 3 - at if far else at], sem)
    copy.start()
    copy.wait()


def finish(cells, cost, objective):
    objective[0] = jnp.sum(cost[...]) / cells


def on_core(body, outs, scalars, arrays, hbm_out=(), smem_out=(), after=(), cost=0, name=None):
    hbm_out = tuple(hbm_out) + tuple(smem_out)
    out_shape = [
        jax.ShapeDtypeStruct(s, jnp.float32) if i in hbm_out else pltpu.VMEM(s, jnp.float32)
        for i, s in enumerate(outs)
    ]
    held = [pltpu.with_memory_space_constraint(x, pltpu.SMEM) for x in scalars]
    held += [pltpu.with_memory_space_constraint(x, pltpu.VMEM) for x in arrays]
    count, waits = len(held), len(after)

    def run(*refs):
        body(*refs[:count], *refs[count + waits :])

    return pl.pallas_call(
        run,
        out_shape=out_shape,
        in_specs=[pl.BlockSpec(memory_space=pltpu.SMEM)] * len(scalars)
        + [pl.BlockSpec(memory_space=pltpu.VMEM)] * len(arrays)
        + [pl.BlockSpec(memory_space=pl.ANY)] * waits,
        out_specs=[
            pl.BlockSpec(memory_space=pltpu.SMEM if i in smem_out else pltpu.VMEM) for i in range(len(outs))
        ],
        compiler_params=pltpu.CompilerParams(vmem_limit_bytes=VMEM_LIMIT),
        cost_estimate=cost_of(cost) if cost else None,
        name=name or body.__name__,
    )(*held, *after)


def shards(
    concentration,
    adjoint_next,
    speed,
    direction_mask,
    decay_rate,
    control,
    goal_weight,
    node_index,
    weight_num,
    step_index,
):
    sections = lax.axis_size("space")
    ranks = sections * lax.axis_size("node")
    within = [(i, i ^ 1) for i in range(ranks)]
    across = [p for i in range(1, ranks - 1, 2) for p in ((i, i + 1), (i + 1, i))]

    def swap(x, what):
        with jax.named_scope("swap_" + what):
            return lax.ppermute(x, AXES, within)

    def pass_on(x, what):
        with jax.named_scope("pass_" + what):
            return lax.ppermute(x, AXES, across)

    _, layers, rows, columns = concentration.shape
    me = lax.axis_index("node").astype(jnp.int32)
    core = jnp.reshape(me, (1,))
    far = swap(concentration, "state")
    plane = (rows, columns)
    pair, four_planes = (2,) + plane, (4,) + plane
    four = (2,) + pair
    sides = (2, rows, columns // 2)
    held = lambda x, space: pltpu.with_memory_space_constraint(x, space)
    (first,) = on_core(begin, [(8, 128)], [], [], cost=LONG)
    (packed,) = on_core(
        pack, [(3,) + plane], [core], [concentration, far, speed, direction_mask], after=[first]
    )
    halo = pass_on(packed, "state")
    numbers = pl.pallas_call(
        gather_numbers,
        out_shape=pltpu.VMEM((8, 128), jnp.float32),
        in_specs=[pl.BlockSpec(memory_space=pltpu.SMEM)] * 3 + [pl.BlockSpec(memory_space=pl.ANY)],
        out_specs=pl.BlockSpec(memory_space=pltpu.VMEM),
        name="gather_numbers",
    )(node_index, weight_num, step_index, packed)
    far_numbers = swap(numbers, "numbers")

    shapes = [four, four, four, four, pair]
    scal, cx, cy, cz, dg, ctl = pl.pallas_call(
        prepare,
        out_shape=[pltpu.SMEM((2, 8), jnp.float32)] + [pltpu.VMEM(s, jnp.float32) for s in shapes],
        in_specs=[pl.BlockSpec(memory_space=pltpu.SMEM)]
        + [pl.BlockSpec(memory_space=pltpu.VMEM)] * 6,
        out_specs=[pl.BlockSpec(memory_space=pltpu.SMEM)] + [pl.BlockSpec(memory_space=pltpu.VMEM)] * len(shapes),
        compiler_params=pltpu.CompilerParams(vmem_limit_bytes=VMEM_LIMIT),
        name="prepare",
    )(
        core,
        *[held(x, pltpu.VMEM) for x in (numbers, far_numbers, speed, direction_mask, decay_rate, control)],
    )
    fields = [cx, cy, cz, dg]
    both = [core, scal]
    states = [concentration, far]
    base, base_q, s1_in = on_core(first_stage, [pair] * 3, both, states + fields + [ctl])
    far_base = pass_on(base, "stage1")
    msg, s1_out = on_core(
        first_edge, [pair, pair], [scal], [halo, base, base_q] + fields, cost=LONG
    )
    halo2 = pass_on(msg, "stage2")
    weights, goals, adj, adj_out = pl.pallas_call(
        prepare_back,
        out_shape=[pltpu.SMEM((2,), jnp.float32)]
        + [pltpu.VMEM(s, jnp.float32) for s in (pair, pair, pair)],
        in_specs=[pl.BlockSpec(memory_space=pltpu.SMEM)]
        + [pl.BlockSpec(memory_space=pltpu.VMEM)] * 4
        + [pl.BlockSpec(memory_space=pl.ANY)],
        out_specs=[pl.BlockSpec(memory_space=pltpu.SMEM)] + [pl.BlockSpec(memory_space=pltpu.VMEM)] * 3,
        compiler_params=pltpu.CompilerParams(vmem_limit_bytes=VMEM_LIMIT),
        name="prepare_back",
    )(
        core,
        held(goal_weight, pltpu.HBM),
        *[held(x, pltpu.VMEM) for x in (numbers, far_numbers)],
        held(adjoint_next, pltpu.HBM),
        msg,
    )
    s1_next, near = pl.pallas_call(
        prepare_next,
        out_shape=[pltpu.VMEM(pair, jnp.float32), pltpu.VMEM(plane, jnp.float32)],
        in_specs=[pl.BlockSpec(memory_space=pltpu.SMEM)] * 2
        + [pl.BlockSpec(memory_space=pltpu.VMEM)] * 6
        + [pl.BlockSpec(memory_space=pl.ANY)],
        out_specs=[pl.BlockSpec(memory_space=pltpu.VMEM)] * 2,
        scratch_shapes=[pltpu.VMEM((2, 1) + plane, jnp.float32)] * 4,
        compiler_params=pltpu.CompilerParams(vmem_limit_bytes=VMEM_LIMIT),
        name="prepare_next",
    )(
        core,
        held(scal, pltpu.SMEM),
        *[held(x, pltpu.VMEM) for x in (speed, direction_mask, decay_rate, control)],
        *[held(x, pltpu.VMEM) for x in states],
        msg,
    )

    after = swap(adj_out, "after")

    (far_step,) = on_core(far_part, [pair], both, states + [halo, far_base, cx], cost=LONG)
    s2 = list(on_core(second_inner, [plane] * 2, both, states + [s1_out, s1_in, s1_next] + fields + [ctl]))
    s2_next = [swap(s2[1], "s2_far"), swap(s2[0], "s2_own")]
    (base,) = on_core(third_stage, [four], both, states + [msg, s1_out] + s2 + s2_next + [halo, far_step] + fields + [ctl])
    final_own, final_far, terms, msg3, partials = on_core(
        turn,
        [pair, pair, four, four, pair],
        [scal, weights],
        [halo2, base] + fields + [goals, adj, after],
    )
    halo3 = pass_on(msg3, "back2")
    part, cost, *pins = on_core(
        turn_inner,
        [pair, (8, columns)] + [(r, columns) for r in cut(4 * rows + 8, 3)],
        [scal, weights],
        [final_own, final_far, terms] + fields + [goals],
    )
    theirs = [swap(x, "pin") for x in pins]
    base, a2, cost = on_core(
        back_second,
        [four, pair, (8, 128)],
        [scal],
        [msg3, partials, part, halo, near] + fields + [cost] + pins + theirs,
    )
    whole = sections & (sections - 1) == 0
    steps = [1 << k for k in range(sections.bit_length() - 1)] if whole else []
    steps = steps[1:] + steps[:1]

    def from_pair(x, k):
        with jax.named_scope("goal_sum"):
            if k >= len(steps):
                return jnp.zeros_like(x)
            return lax.ppermute(x, "space", [(i, i ^ steps[k]) for i in range(sections)])

    cost = cost + from_pair(cost, 0)
    a1, msg4 = on_core(second_back_edge, [pair, pair], [scal], [halo3, base] + fields, after=[cost])
    halo4 = pass_on(msg4, "back1")
    keep, part, give, cost, *out = on_core(
        close,
        [sides, four_planes, sides, (8, 128)] + [(r, columns) for r in cut(2 * rows, 2)],
        both,
        [terms, partials, halo3, a1, a2, base] + fields + [ctl, cost, from_pair(cost, 1)],
        cost=2 * LONG,
    )
    parts = [swap(x, "adjoint") for x in out]
    taken = swap(give, "gradient")
    adjoint, gradient = on_core(
        write_inner,
        [(1, layers, rows, columns), (layers, rows, columns // 2)],
        [core],
        [part, keep, taken] + parts,
        hbm_out=(0, 1),
    )
    for k in range(2, len(steps) - 1):
        cost = cost + from_pair(cost, k)
    outer, give, cost = on_core(
        last_edge,
        [plane, plane, (8, 128)],
        [],
        [halo4, part, cost, from_pair(cost, max(2, len(steps) - 1))],
        after=[held(adjoint, pltpu.HBM)],
        cost=LONG,
    )
    if not whole:
        cost = lax.psum(cost, "space")
    cells = sections * layers * rows * columns
    (objective,) = on_core(functools.partial(finish, cells), [(1,)], [], [cost], smem_out=(0,), name="finish")
    for far, value in ((False, outer), (True, swap(give, "outer"))):
        adjoint = pl.pallas_call(
            functools.partial(write_outer, far),
            out_shape=jax.ShapeDtypeStruct(adjoint.shape, jnp.float32),
            in_specs=[
                pl.BlockSpec(memory_space=pltpu.SMEM),
                pl.BlockSpec(memory_space=pltpu.VMEM),
                pl.BlockSpec(memory_space=pl.ANY),
            ],
            out_specs=pl.BlockSpec(memory_space=pl.ANY),
            scratch_shapes=[pltpu.SemaphoreType.DMA],
            input_output_aliases={2: 0},
            compiler_params=pltpu.CompilerParams(vmem_limit_bytes=VMEM_LIMIT),
            name="write_outer",
        )(held(core, pltpu.SMEM), held(value, pltpu.VMEM), held(adjoint, pltpu.HBM))
    return (adjoint, gradient, objective)


def solution(mesh):
    return jax.shard_map(
        shards,
        mesh=mesh,
        in_specs=(
            P("node", ("groups", "space"), None, None),
            P("node", ("groups", "space"), None, None),
            P(None, ("groups", "space"), None, None),
            P(None, ("groups", "space"), None, None),
            P(("groups", "space"), None, None),
            P(("groups", "space"), None, None),
            P(("groups", "space"), None, None),
            P("node", None),
            P("node"),
            P("groups"),
        ),
        out_specs=(
            P("node", ("groups", "space"), None, None),
            P(("groups", "space"), None, "node"),
            P("groups"),
        ),
        check_vma=False,
    )
```

```python
import functools
import math

import jax
import jax.numpy as jnp
from jax import lax
from jax.experimental import pallas as pl
from jax.experimental.pallas import tpu as pltpu
from jax.sharding import PartitionSpec as P

time_step = 0.6
variance_gain = 0.5
penalty = 0.1
weight_denominator = 16.0

VMEM_LIMIT = 8 * 1024 * 1024
AXES = ("space", "node")
LONG = 8


def cost_of(us):
    return pl.CostEstimate(flops=us * 1_000_000_000, bytes_accessed=us * 3_000_000, transcendentals=0)


def roll(value, steps, axis):
    return pltpu.roll(value, steps % value.shape[axis], axis)


def in_plane(value, a, cy, cz, k):
    return a[1] * (cy[0, k] * roll(value, 1, 0) + cy[1, k] * roll(value, -1, 0)) + a[2] * (
        cz[0, k] * roll(value, 1, 1) + cz[1, k] * roll(value, -1, 1)
    )


def in_plane_back(value, a, cy, cz, k):
    return a[1] * (roll(cy[0, k] * value, -1, 0) + roll(cy[1, k] * value, 1, 0)) + a[2] * (
        roll(cz[0, k] * value, -1, 1) + roll(cz[1, k] * value, 1, 1)
    )


def rows_of(scal, j):
    return [scal[j, k] for k in range(5)]


def pick(values, index):
    result = jnp.float32(values[-1])
    for k, value in enumerate(values[:-1]):
        result = jnp.where(index == k, jnp.float32(value), result)
    return result


def node_scales(tiles, scal):
    levels = [-math.cos(math.pi * k / 8.0) for k in range(9)]
    step = tiles[0][0, 9].astype(jnp.int32)
    half = step & 31
    wave = pick([math.sin(2.0 * math.pi * k / 64.0) for k in range(17)], jnp.minimum(half, 32 - half))
    phase = 1.0 + jnp.where(step < 32, 0.5, -0.5) * wave
    for j, tile in enumerate(tiles):
        p = {k: pick(levels, tile[0, k]) for k in (0, 1, 2, 4, 6, 7)}
        scal[j, 0] = 1.0 + 0.3 * p[0]
        scal[j, 1] = 1.0 + 0.3 * p[1]
        scal[j, 2] = (1.0 + 0.3 * p[2]) * (1.0 + 0.2 * p[7])
        scal[j, 3] = pick([math.exp(0.5 * p) for p in levels], tile[0, 3]) * pick(
            [math.exp(0.25 * p) for p in levels], tile[0, 5]
        )
        scal[j, 4] = (1.0 + 0.3 * p[4] + 0.2 * p[6]) * phase


def expand(bits, columns):
    blocks = bits.shape[1]
    spread = (
        lax.broadcasted_iota(jnp.int32, (blocks, columns), 1) // (columns // blocks)
        == lax.broadcasted_iota(jnp.int32, (blocks, columns), 0)
    ).astype(jnp.bfloat16)
    return jnp.dot(bits.astype(jnp.float32).astype(jnp.bfloat16), spread, preferred_element_type=jnp.float32)


def toward_outer(up, me):
    flip = (me == 1).astype(jnp.float32)
    return up + flip - 2.0 * flip * up


def begin(out):
    out[...] = jnp.zeros_like(out)


def gather_numbers(index, weight, step, _, numbers):
    lane = lax.broadcasted_iota(jnp.int32, numbers.shape, 1)
    value = jnp.zeros(numbers.shape, jnp.int32)
    for k, number in enumerate([index[0, k] for k in range(index.shape[1])] + [weight[0], step[0]]):
        value = jnp.where(lane == k, number, value)
    numbers[...] = value.astype(jnp.float32)


def pack(core, own, far, speed, mask, out):
    at = 3 * core[0]
    out[0] = own[0, at]
    out[1] = far[0, at]
    out[2] = speed[0, at].astype(jnp.float32) * toward_outer(expand(mask[0, at], speed.shape[3]), core[0])


def fields_of(k, at, me, speeds, masks, cx, cy, cz):
    rows, columns = speeds.shape[2:]
    row = lax.broadcasted_iota(jnp.int32, (rows, columns), 0)
    column = lax.broadcasted_iota(jnp.int32, (rows, columns), 1)
    up = [expand(masks[d, at], columns) for d in range(3)]
    s = [speeds[d, at].astype(jnp.float32) for d in range(3)]
    outer = s[0] * toward_outer(up[0], me)
    cx[0, k] = outer
    cx[1, k] = s[0] - outer
    lower = s[1] * up[1]
    cy[0, k] = jnp.where(row == 0, 0.0, lower)
    cy[1, k] = jnp.where(row == rows - 1, 0.0, s[1] - lower)
    lower = s[2] * up[2]
    cz[0, k] = jnp.where(column == 0, 0.0, lower)
    cz[1, k] = jnp.where(column == columns - 1, 0.0, s[2] - lower)


def own_of(k, at, rates, speeds, scal, dg):
    s = [speeds[d, at].astype(jnp.float32) for d in range(3)] + [rates[at].astype(jnp.float32)]
    for j in range(2):
        dg[j, k] = sum(scal[j, d] * s[d] for d in range(4))


def prepare(core, own_numbers, far_numbers, speed, mask, decay, control, scal, cx, cy, cz, dg, ctl):
    me = core[0]
    for k, at in enumerate((3 * me, 1 + me)):
        fields_of(k, at, me, speed, mask, cx, cy, cz)
        ctl[k] = control[at]
    node_scales((own_numbers[...], far_numbers[...]), scal)
    for k, at in enumerate((3 * me, 1 + me)):
        own_of(k, at, decay, speed, scal, dg)


def prepare_next(core, scal, speed, mask, decay, control, own, far, _, s1_next, near, cx, cy, cz, dg):
    me = core[0]
    at = 2 - me
    fields_of(0, at, me, speed, mask, cx, cy, cz)
    own_of(0, at, decay, speed, scal, dg)
    near[...] = cx[0, 0]
    for j, c in enumerate((own, far)):
        a = rows_of(scal, j)
        value = c[0, at]
        l = a[0] * (cx[0, 0] * c[0, 1 + me] + cx[1, 0] * c[0, 3 - 3 * me]) + in_plane(value, a, cy, cz, 0) - dg[j, 0] * value
        s1_next[j] = value + time_step * (l + a[4] * control[at])


def prepare_back(core, goal, own_numbers, far_numbers, adjoint, _, weights, goals, adj, adj_out):
    me = core[0]
    weights[0] = own_numbers[...][0, 8] * (1.0 / weight_denominator)
    weights[1] = far_numbers[...][0, 8] * (1.0 / weight_denominator)
    for k, at in enumerate((3 * me, 1 + me)):
        goals[k] = goal[at].astype(jnp.float32)
        adj[k] = adjoint[0, at].astype(jnp.float32)
    adj_out[0] = adjoint[0, 3 - 3 * me].astype(jnp.float32)
    adj_out[1] = adjoint[0, 2 - me].astype(jnp.float32)


def first_stage(core, scal, own, far, cx, cy, cz, dg, ctl, base, base_q, s1_in):
    me = core[0]
    for j, c in enumerate((own, far)):
        a = rows_of(scal, j)
        c_o, c_i = c[0, 3 * me], c[0, 1 + me]
        push = [a[4] * ctl[k] for k in range(2)]
        l_i = a[0] * (cx[0, 1] * c_o + cx[1, 1] * c[0, 2 - me]) + in_plane(c_i, a, cy, cz, 1) - dg[j, 1] * c_i
        s1_i = c_i + time_step * (l_i + push[1])
        s1_in[j] = s1_i
        l_o = a[0] * (cx[1, 0] * c_i) + in_plane(c_o, a, cy, cz, 0) - dg[j, 0] * c_o
        base[j] = c_o + time_step * (l_o + push[0])
        base_q[j] = 0.75 * c_o + (0.25 * time_step) * (a[0] * (cx[1, 0] * s1_i) + push[0])


def first_edge(scal, halo, base, base_q, cx, cy, cz, dg, msg, s1_out):
    for j in range(2):
        a = rows_of(scal, j)
        s1_o = base[j] + (time_step * a[0]) * (cx[0, 0] * halo[1 - j])
        s1_out[j] = s1_o
        msg[j] = base_q[j] + 0.25 * (s1_o + time_step * (in_plane(s1_o, a, cy, cz, 0) - dg[j, 0] * s1_o))


def second_inner(core, scal, own, far, s1_out, s1_in, s1_next, cx, cy, cz, dg, ctl, s2_own, s2_far):
    for j, (c, out) in enumerate(((own, s2_own), (far, s2_far))):
        a = rows_of(scal, j)
        s1_i = s1_in[j]
        l_i = a[0] * (cx[0, 1] * s1_out[j] + cx[1, 1] * s1_next[j]) + in_plane(s1_i, a, cy, cz, 1) - dg[j, 1] * s1_i
        out[...] = 0.75 * c[0, 1 + core[0]] + 0.25 * (s1_i + time_step * (l_i + a[4] * ctl[1]))


def far_part(core, scal, own, far, halo, far_base, cx, step):
    for j, c in enumerate((own, far)):
        s1_h = far_base[1 - j] + (time_step * scal[j, 0]) * (halo[2] * c[0, 3 * core[0]])
        step[j] = (0.25 * time_step * scal[j, 0]) * (cx[0, 0] * s1_h)


def third_stage(core, scal, own, far, msg, s1_out, s2_own, s2_far, next_own, next_far, halo, step, cx, cy, cz, dg, ctl, base):
    me = core[0]
    parts = ((own, s2_own, next_own), (far, s2_far, next_far))
    for j, (c, s2, s2_next) in enumerate(parts):
        a = rows_of(scal, j)
        c_o, s2_i = c[0, 3 * me], s2[...]
        s2_o = msg[j] + step[j]
        back = (0.25 * time_step * a[0]) * (halo[2] * s1_out[j])
        l_o = a[0] * (cx[0, 0] * back + cx[1, 0] * s2_i) + in_plane(s2_o, a, cy, cz, 0) - dg[j, 0] * s2_o
        l_i = a[0] * (cx[0, 1] * s2_o + cx[1, 1] * s2_next[...]) + in_plane(s2_i, a, cy, cz, 1) - dg[j, 1] * s2_i
        base[j, 0] = c_o / 3.0 + 2.0 / 3.0 * (s2_o + time_step * (l_o + a[4] * ctl[0]))
        base[j, 1] = c[0, 1 + me] / 3.0 + 2.0 / 3.0 * (s2_i + time_step * (l_i + a[4] * ctl[1]))


def finals(j, scal, halo, base, cx):
    return base[j, 0] + (2.0 / 3.0 * time_step * scal[j, 0]) * (cx[0, 0] * halo[1 - j]), base[j, 1]


def turn(scal, weights, halo, base, cx, cy, cz, dg, goals, adj, after_far, final_own, final_far, term, msg, partial):
    final_own[0], final_own[1] = finals(0, scal, halo, base, cx)
    final_far[0], final_far[1] = finals(1, scal, halo, base, cx)
    first = [weights[0] * final_own[k] + weights[1] * final_far[k] for k in range(2)]
    for j, (final, after) in enumerate(((final_own, (adj[0], adj[1])), (final_far, (after_far[0], after_far[1])))):
        a = rows_of(scal, j)
        u = []
        for k in range(2):
            t = after[k] + goals[k] * weights[j] * (1.0 + 2.0 * variance_gain * (final[k] - first[k]))
            term[j, k] = t
            u.append(2.0 / 3.0 * t)
        msg[j, 0] = a[0] * (cx[0, 0] * u[0])
        spread = a[0] * (cx[0, 1] * u[1]) + in_plane_back(u[0], a, cy, cz, 0) - dg[j, 0] * u[0]
        value = u[0] + time_step * spread
        partial[j] = value
        msg[j, 1] = a[0] * (cx[0, 0] * value)


class Laid:
    def __init__(self, refs):
        self.left = [(ref, start) for ref in refs for start in range(0, ref.shape[0], 8)]

    def put(self, value):
        for start in range(0, value.shape[0], 8):
            ref, at = self.left.pop(0)
            ref[at : at + 8] = value[start : start + 8]


def get(refs, count, rows):
    whole = jnp.concatenate([ref[...] for ref in refs], 0)
    return [whole[rows * k : rows * k + rows] for k in range(count)] + [whole[rows * count :]]


def cut(rows, pieces):
    tiles = rows // 8
    return [8 * (tiles // pieces + (k < tiles % pieces)) for k in range(pieces)]


def turn_inner(scal, weights, final_own, final_far, terms, cx, cy, cz, dg, goals, part, cost, *pins):
    laid = Laid(pins)
    for j in range(2):
        a = rows_of(scal, j)
        u = [2.0 / 3.0 * terms[j, k] for k in range(2)]
        laid.put(a[0] * (cx[1, 1] * u[1]))
        spread = a[0] * (cx[1, 0] * u[0]) + in_plane_back(u[1], a, cy, cz, 1) - dg[j, 1] * u[1]
        value = u[1] + time_step * spread
        part[j] = value
        laid.put(a[0] * (cx[1, 1] * value))
    total = 0.0
    for k in range(2):
        own, far = weights[0] * final_own[k], weights[1] * final_far[k]
        first = own + far
        second = own * final_own[k] + far * final_far[k]
        total = total + goals[k] * (first + variance_gain * (second - first * first))
    rows, columns = total.shape
    total = sum(total[8 * r : 8 * r + 8] for r in range(rows // 8))
    cost[...] = sum(total[:, 128 * k : 128 * k + 128] for k in range(columns // 128))


def back_second(scal, msgs, partials, part, halo, near, cx, cy, cz, dg, cost, cost_far, *rest):
    base, a2, total = rest[-3:]
    count, rows = (len(rest) - 3) // 2, msgs.shape[2]
    mine, theirs = get(rest[:count], 4, rows), get(rest[count:-3], 4, rows)
    total[...] = cost[...] + cost_far[...]
    for j in range(2):
        a = rows_of(scal, j)
        pin, pin2 = theirs[2 - 2 * j], theirs[3 - 2 * j]
        pin2 = 0.25 * (pin2 + (time_step * a[0]) * (near[...] * mine[2 * j]))
        a2_i = part[j] + time_step * pin
        a2[j] = a2_i
        u_o, u_i = 0.25 * partials[j], 0.25 * a2_i
        back = (0.25 * time_step * a[0]) * (halo[2] * msgs[j, 0])
        spread = a[0] * (cx[0, 1] * u_i) + in_plane_back(u_o, a, cy, cz, 0) - dg[j, 0] * u_o + back
        base[j, 0] = u_o + time_step * spread
        spread = a[0] * (cx[1, 0] * u_o) + in_plane_back(u_i, a, cy, cz, 1) - dg[j, 1] * u_i + pin2
        base[j, 1] = u_i + time_step * spread


def second_back_edge(scal, halo, base, cx, cy, cz, dg, a1, msg):
    for j in range(2):
        a = rows_of(scal, j)
        step = (0.25 * time_step) * halo[1 - j, 0]
        spread = in_plane_back(step, a, cy, cz, 0) - dg[j, 0] * step + 0.25 * halo[1 - j, 1]
        value = base[j, 0] + step + time_step * spread
        a1[j] = value
        msg[j] = a[0] * (cx[0, 0] * value)


def close(core, scal, terms, partials, halo, a1, a2, base, cx, cy, cz, dg, ctl, cost, cost_far, keep, part, give, total, *send):
    total[...] = cost[...] + cost_far[...]
    laid = Laid(send)
    sources = [0.0, 0.0]
    for j in range(2):
        a = rows_of(scal, j)
        first = halo[1 - j, 0]
        x = [a1[j], base[j, 1] + (0.25 * time_step * time_step * a[0]) * (cx[1, 0] * first)]
        a2_o = partials[j] + time_step * first
        for k, second in enumerate((a2_o, a2[j])):
            sources[k] = sources[k] + a[4] * (2.0 / 3.0 * terms[j, k] + 0.25 * second + x[k])
        spread = a[0] * (cx[0, 1] * x[1]) + in_plane_back(x[0], a, cy, cz, 0) - dg[j, 0] * x[0]
        outer = terms[j, 0] / 3.0 + 0.75 * a2_o + (x[0] + time_step * spread)
        spread = a[0] * (cx[1, 0] * x[0]) + in_plane_back(x[1], a, cy, cz, 1) - dg[j, 1] * x[1]
        inner = terms[j, 1] / 3.0 + 0.75 * a2[j] + (x[1] + time_step * spread)
        pin = a[0] * (cx[1, 1] * x[1])
        part[j] = outer
        if j == 0:
            part[2], part[3] = inner, pin
        else:
            laid.put(inner)
            laid.put(pin)
    half = ctl.shape[2] // 2
    zero = core[0] == 0
    for k in range(2):
        gradient = time_step * sources[k] + penalty * ctl[k]
        low, high = gradient[:, :half], gradient[:, half:]
        keep[k] = jnp.where(zero, low, high)
        give[k] = jnp.where(zero, high, low)


def last_edge(halo, part, cost, cost_far, outer, give):
    rows = outer.shape[0]
    outer[...] = part[0] + time_step * halo[1]
    give[:rows] = part[1] + time_step * halo[0]
    give[rows:] = jnp.zeros((8, outer.shape[1]), jnp.float32)
    give[rows:, :128] = cost[...] + cost_far[...]


def write_inner(core, part, keep, taken, *rest):
    theirs, (out, gradient) = get(rest[:-2], 2, part.shape[1]), rest[-2:]
    me = core[0]
    out[0, 1 + me] = part[2] + time_step * theirs[1]
    out[0, 2 - me] = theirs[0] + time_step * part[3]
    gradient[3 * me] = keep[0]
    gradient[1 + me] = keep[1]
    gradient[3 - 3 * me] = taken[0]
    gradient[2 - me] = taken[1]


def write_outer(core, value, _, out, sem):
    copy = pltpu.make_async_copy(value, out.at[0, 3 * core[0]], sem)
    copy.start()
    copy.wait()


def finish(cells, core, mine, taken, _, out, objective, number, sems):
    rows = mine.shape[0] - 8
    copy = pltpu.make_async_copy(taken.at[:rows], out.at[0, 3 - 3 * core[0]], sems.at[0])
    copy.start()
    number[0] = jnp.sum(mine[rows:, :128] + taken[rows:, :128]) / cells
    result = pltpu.make_async_copy(number, objective, sems.at[1])
    result.start()
    copy.wait()
    result.wait()


def on_core(body, outs, scalars, arrays, hbm_out=(), smem_out=(), after=(), cost=0, name=None):
    hbm_out = tuple(hbm_out) + tuple(smem_out)
    out_shape = [
        jax.ShapeDtypeStruct(s, jnp.float32) if i in hbm_out else pltpu.VMEM(s, jnp.float32)
        for i, s in enumerate(outs)
    ]
    held = [pltpu.with_memory_space_constraint(x, pltpu.SMEM) for x in scalars]
    held += [pltpu.with_memory_space_constraint(x, pltpu.VMEM) for x in arrays]
    count, waits = len(held), len(after)

    def run(*refs):
        body(*refs[:count], *refs[count + waits :])

    return pl.pallas_call(
        run,
        out_shape=out_shape,
        in_specs=[pl.BlockSpec(memory_space=pltpu.SMEM)] * len(scalars)
        + [pl.BlockSpec(memory_space=pltpu.VMEM)] * len(arrays)
        + [pl.BlockSpec(memory_space=pl.ANY)] * waits,
        out_specs=[
            pl.BlockSpec(memory_space=pltpu.SMEM if i in smem_out else pltpu.VMEM) for i in range(len(outs))
        ],
        compiler_params=pltpu.CompilerParams(vmem_limit_bytes=VMEM_LIMIT),
        cost_estimate=cost_of(cost) if cost else None,
        name=name or body.__name__,
    )(*held, *after)


def shards(
    concentration,
    adjoint_next,
    speed,
    direction_mask,
    decay_rate,
    control,
    goal_weight,
    node_index,
    weight_num,
    step_index,
):
    sections = lax.axis_size("space")
    ranks = sections * lax.axis_size("node")
    within = [(i, i ^ 1) for i in range(ranks)]
    across = [p for i in range(1, ranks - 1, 2) for p in ((i, i + 1), (i + 1, i))]

    def swap(x, what):
        with jax.named_scope("swap_" + what):
            return lax.ppermute(x, AXES, within)

    def pass_on(x, what):
        with jax.named_scope("pass_" + what):
            return lax.ppermute(x, AXES, across)

    _, layers, rows, columns = concentration.shape
    me = lax.axis_index("node").astype(jnp.int32)
    core = jnp.reshape(me, (1,))
    far = swap(concentration, "state")
    plane = (rows, columns)
    pair, four_planes = (2,) + plane, (4,) + plane
    four = (2,) + pair
    sides = (2, rows, columns // 2)
    held = lambda x, space: pltpu.with_memory_space_constraint(x, space)
    (first,) = on_core(begin, [(8, 128)], [], [], cost=LONG)
    (packed,) = on_core(
        pack, [(3,) + plane], [core], [concentration, far, speed, direction_mask], after=[first]
    )
    halo = pass_on(packed, "state")
    numbers = pl.pallas_call(
        gather_numbers,
        out_shape=pltpu.VMEM((8, 128), jnp.float32),
        in_specs=[pl.BlockSpec(memory_space=pltpu.SMEM)] * 3 + [pl.BlockSpec(memory_space=pl.ANY)],
        out_specs=pl.BlockSpec(memory_space=pltpu.VMEM),
        name="gather_numbers",
    )(node_index, weight_num, step_index, packed)
    far_numbers = swap(numbers, "numbers")

    shapes = [four, four, four, four, pair]
    scal, cx, cy, cz, dg, ctl = pl.pallas_call(
        prepare,
        out_shape=[pltpu.SMEM((2, 8), jnp.float32)] + [pltpu.VMEM(s, jnp.float32) for s in shapes],
        in_specs=[pl.BlockSpec(memory_space=pltpu.SMEM)]
        + [pl.BlockSpec(memory_space=pltpu.VMEM)] * 6,
        out_specs=[pl.BlockSpec(memory_space=pltpu.SMEM)] + [pl.BlockSpec(memory_space=pltpu.VMEM)] * len(shapes),
        compiler_params=pltpu.CompilerParams(vmem_limit_bytes=VMEM_LIMIT),
        name="prepare",
    )(
        core,
        *[held(x, pltpu.VMEM) for x in (numbers, far_numbers, speed, direction_mask, decay_rate, control)],
    )
    fields = [cx, cy, cz, dg]
    both = [core, scal]
    states = [concentration, far]
    base, base_q, s1_in = on_core(first_stage, [pair] * 3, both, states + fields + [ctl])
    far_base = pass_on(base, "stage1")
    msg, s1_out = on_core(
        first_edge, [pair, pair], [scal], [halo, base, base_q] + fields, cost=LONG
    )
    halo2 = pass_on(msg, "stage2")
    weights, goals, adj, adj_out = pl.pallas_call(
        prepare_back,
        out_shape=[pltpu.SMEM((2,), jnp.float32)]
        + [pltpu.VMEM(s, jnp.float32) for s in (pair, pair, pair)],
        in_specs=[pl.BlockSpec(memory_space=pltpu.SMEM)]
        + [pl.BlockSpec(memory_space=pltpu.VMEM)] * 4
        + [pl.BlockSpec(memory_space=pl.ANY)],
        out_specs=[pl.BlockSpec(memory_space=pltpu.SMEM)] + [pl.BlockSpec(memory_space=pltpu.VMEM)] * 3,
        compiler_params=pltpu.CompilerParams(vmem_limit_bytes=VMEM_LIMIT),
        name="prepare_back",
    )(
        core,
        held(goal_weight, pltpu.HBM),
        *[held(x, pltpu.VMEM) for x in (numbers, far_numbers)],
        held(adjoint_next, pltpu.HBM),
        msg,
    )
    s1_next, near = pl.pallas_call(
        prepare_next,
        out_shape=[pltpu.VMEM(pair, jnp.float32), pltpu.VMEM(plane, jnp.float32)],
        in_specs=[pl.BlockSpec(memory_space=pltpu.SMEM)] * 2
        + [pl.BlockSpec(memory_space=pltpu.VMEM)] * 6
        + [pl.BlockSpec(memory_space=pl.ANY)],
        out_specs=[pl.BlockSpec(memory_space=pltpu.VMEM)] * 2,
        scratch_shapes=[pltpu.VMEM((2, 1) + plane, jnp.float32)] * 4,
        compiler_params=pltpu.CompilerParams(vmem_limit_bytes=VMEM_LIMIT),
        name="prepare_next",
    )(
        core,
        held(scal, pltpu.SMEM),
        *[held(x, pltpu.VMEM) for x in (speed, direction_mask, decay_rate, control)],
        *[held(x, pltpu.VMEM) for x in states],
        msg,
    )

    after = swap(adj_out, "after")

    (far_step,) = on_core(far_part, [pair], both, states + [halo, far_base, cx], cost=LONG)
    s2 = list(on_core(second_inner, [plane] * 2, both, states + [s1_out, s1_in, s1_next] + fields + [ctl]))
    s2_next = [swap(s2[1], "s2_far"), swap(s2[0], "s2_own")]
    (base,) = on_core(third_stage, [four], both, states + [msg, s1_out] + s2 + s2_next + [halo, far_step] + fields + [ctl])
    final_own, final_far, terms, msg3, partials = on_core(
        turn,
        [pair, pair, four, four, pair],
        [scal, weights],
        [halo2, base] + fields + [goals, adj, after],
    )
    halo3 = pass_on(msg3, "back2")
    part, cost, *pins = on_core(
        turn_inner,
        [pair, (8, 128)] + [(r, columns) for r in cut(4 * rows, 3)],
        [scal, weights],
        [final_own, final_far, terms] + fields + [goals],
    )
    whole = sections & (sections - 1) == 0
    steps = [1 << k for k in range(sections.bit_length() - 1)] if whole else []
    steps = steps[1:] + steps[:1]

    def from_pair(x, k):
        with jax.named_scope("goal_sum"):
            if k >= len(steps):
                return jnp.zeros_like(x)
            flip = 3 if steps[k] == 1 else 2 * steps[k]
            return lax.ppermute(x, AXES, [(i, i ^ flip) for i in range(ranks)])

    theirs = [swap(x, "pin") for x in pins]
    base, a2, cost = on_core(
        back_second,
        [four, pair, (8, 128)],
        [scal],
        [msg3, partials, part, halo, near] + fields + [cost, from_pair(cost, 0)] + pins + theirs,
    )
    a1, msg4 = on_core(second_back_edge, [pair, pair], [scal], [halo3, base] + fields, after=[cost])
    halo4 = pass_on(msg4, "back1")
    keep, part, give, cost, *out = on_core(
        close,
        [sides, four_planes, sides, (8, 128)] + [(r, columns) for r in cut(2 * rows, 2)],
        both,
        [terms, partials, halo3, a1, a2, base] + fields + [ctl, cost, from_pair(cost, 1)],
        cost=2 * LONG,
    )
    parts = [swap(x, "adjoint") for x in out]
    taken = swap(give, "gradient")
    adjoint, gradient = on_core(
        write_inner,
        [(1, layers, rows, columns), (layers, rows, columns // 2)],
        [core],
        [part, keep, taken] + parts,
        hbm_out=(0, 1),
    )
    for k in range(2, len(steps) - 1):
        cost = cost + from_pair(cost, k)
    cost_far = from_pair(cost, max(2, len(steps) - 1))
    if not whole:
        cost = lax.psum(cost, "space")
    outer, give = on_core(
        last_edge,
        [plane, (rows + 8, columns)],
        [],
        [halo4, part, cost, cost_far],
        after=[held(adjoint, pltpu.HBM)],
        cost=LONG,
    )
    anywhere, in_smem = pl.BlockSpec(memory_space=pl.ANY), pl.BlockSpec(memory_space=pltpu.SMEM)
    adjoint = pl.pallas_call(
        write_outer,
        out_shape=jax.ShapeDtypeStruct(adjoint.shape, jnp.float32),
        in_specs=[in_smem, pl.BlockSpec(memory_space=pltpu.VMEM), anywhere],
        out_specs=anywhere,
        scratch_shapes=[pltpu.SemaphoreType.DMA],
        input_output_aliases={2: 0},
        compiler_params=pltpu.CompilerParams(vmem_limit_bytes=VMEM_LIMIT),
        name="write_outer",
    )(held(core, pltpu.SMEM), held(outer, pltpu.VMEM), held(adjoint, pltpu.HBM))
    adjoint, objective = pl.pallas_call(
        functools.partial(finish, sections * layers * rows * columns),
        out_shape=[jax.ShapeDtypeStruct(adjoint.shape, jnp.float32), jax.ShapeDtypeStruct((1,), jnp.float32)],
        in_specs=[in_smem] + [pl.BlockSpec(memory_space=pltpu.VMEM)] * 2 + [anywhere],
        out_specs=[anywhere] * 2,
        scratch_shapes=[pltpu.SMEM((1,), jnp.float32), pltpu.SemaphoreType.DMA((2,))],
        input_output_aliases={3: 0},
        compiler_params=pltpu.CompilerParams(vmem_limit_bytes=VMEM_LIMIT),
        name="finish",
    )(
        held(core, pltpu.SMEM),
        *[held(x, pltpu.VMEM) for x in (give, swap(give, "outer"))],
        held(adjoint, pltpu.HBM),
    )
    return (adjoint, gradient, objective)


def solution(mesh):
    return jax.shard_map(
        shards,
        mesh=mesh,
        in_specs=(
            P("node", ("groups", "space"), None, None),
            P("node", ("groups", "space"), None, None),
            P(None, ("groups", "space"), None, None),
            P(None, ("groups", "space"), None, None),
            P(("groups", "space"), None, None),
            P(("groups", "space"), None, None),
            P(("groups", "space"), None, None),
            P("node", None),
            P("node"),
            P("groups"),
        ),
        out_specs=(
            P("node", ("groups", "space"), None, None),
            P(("groups", "space"), None, "node"),
            P("groups"),
        ),
        check_vma=False,
    )
```

```python
import functools
import math

import jax
import jax.numpy as jnp
from jax import lax
from jax.experimental import pallas as pl
from jax.experimental.pallas import tpu as pltpu
from jax.sharding import PartitionSpec as P

time_step = 0.6
variance_gain = 0.5
penalty = 0.1
weight_denominator = 16.0

VMEM_LIMIT = 8 * 1024 * 1024
AXES = ("space", "node")
LONG = 8


def cost_of(us):
    return pl.CostEstimate(flops=us * 1_000_000_000, bytes_accessed=us * 3_000_000, transcendentals=0)


def roll(value, steps, axis):
    return pltpu.roll(value, steps % value.shape[axis], axis)


def in_plane(value, a, cy, cz, k):
    return a[1] * (cy[0, k] * roll(value, 1, 0) + cy[1, k] * roll(value, -1, 0)) + a[2] * (
        cz[0, k] * roll(value, 1, 1) + cz[1, k] * roll(value, -1, 1)
    )


def in_plane_back(value, a, cy, cz, k):
    return a[1] * (roll(cy[0, k] * value, -1, 0) + roll(cy[1, k] * value, 1, 0)) + a[2] * (
        roll(cz[0, k] * value, -1, 1) + roll(cz[1, k] * value, 1, 1)
    )


def rows_of(scal, j):
    return [scal[j, k] for k in range(5)]


def pick(values, index):
    result = jnp.float32(values[-1])
    for k, value in enumerate(values[:-1]):
        result = jnp.where(index == k, jnp.float32(value), result)
    return result


def node_scales(tiles, scal):
    levels = [-math.cos(math.pi * k / 8.0) for k in range(9)]
    step = tiles[0][0, 9].astype(jnp.int32)
    half = step & 31
    wave = pick([math.sin(2.0 * math.pi * k / 64.0) for k in range(17)], jnp.minimum(half, 32 - half))
    phase = 1.0 + jnp.where(step < 32, 0.5, -0.5) * wave
    for j, tile in enumerate(tiles):
        p = {k: pick(levels, tile[0, k]) for k in (0, 1, 2, 4, 6, 7)}
        scal[j, 0] = 1.0 + 0.3 * p[0]
        scal[j, 1] = 1.0 + 0.3 * p[1]
        scal[j, 2] = (1.0 + 0.3 * p[2]) * (1.0 + 0.2 * p[7])
        scal[j, 3] = pick([math.exp(0.5 * p) for p in levels], tile[0, 3]) * pick(
            [math.exp(0.25 * p) for p in levels], tile[0, 5]
        )
        scal[j, 4] = (1.0 + 0.3 * p[4] + 0.2 * p[6]) * phase


def expand(bits, columns):
    blocks = bits.shape[1]
    spread = (
        lax.broadcasted_iota(jnp.int32, (blocks, columns), 1) // (columns // blocks)
        == lax.broadcasted_iota(jnp.int32, (blocks, columns), 0)
    ).astype(jnp.bfloat16)
    return jnp.dot(bits.astype(jnp.float32).astype(jnp.bfloat16), spread, preferred_element_type=jnp.float32)


def toward_outer(up, me):
    flip = (me == 1).astype(jnp.float32)
    return up + flip - 2.0 * flip * up


def begin(out):
    out[...] = jnp.zeros_like(out)


def gather_numbers(index, weight, step, _, numbers):
    lane = lax.broadcasted_iota(jnp.int32, numbers.shape, 1)
    value = jnp.zeros(numbers.shape, jnp.int32)
    for k, number in enumerate([index[0, k] for k in range(index.shape[1])] + [weight[0], step[0]]):
        value = jnp.where(lane == k, number, value)
    numbers[...] = value.astype(jnp.float32)


def pack(core, own, far, speed, mask, out):
    at = 3 * core[0]
    out[0] = own[0, at]
    out[1] = far[0, at]
    out[2] = speed[0, at].astype(jnp.float32) * toward_outer(expand(mask[0, at], speed.shape[3]), core[0])


def fields_of(k, at, me, speeds, masks, cx, cy, cz):
    rows, columns = speeds.shape[2:]
    row = lax.broadcasted_iota(jnp.int32, (rows, columns), 0)
    column = lax.broadcasted_iota(jnp.int32, (rows, columns), 1)
    up = [expand(masks[d, at], columns) for d in range(3)]
    s = [speeds[d, at].astype(jnp.float32) for d in range(3)]
    outer = s[0] * toward_outer(up[0], me)
    cx[0, k] = outer
    cx[1, k] = s[0] - outer
    lower = s[1] * up[1]
    cy[0, k] = jnp.where(row == 0, 0.0, lower)
    cy[1, k] = jnp.where(row == rows - 1, 0.0, s[1] - lower)
    lower = s[2] * up[2]
    cz[0, k] = jnp.where(column == 0, 0.0, lower)
    cz[1, k] = jnp.where(column == columns - 1, 0.0, s[2] - lower)


def own_of(k, at, rates, speeds, scal, dg):
    s = [speeds[d, at].astype(jnp.float32) for d in range(3)] + [rates[at].astype(jnp.float32)]
    for j in range(2):
        dg[j, k] = sum(scal[j, d] * s[d] for d in range(4))


def prepare(core, own_numbers, far_numbers, speed, mask, decay, control, scal, cx, cy, cz, dg, ctl):
    me = core[0]
    for k, at in enumerate((3 * me, 1 + me)):
        fields_of(k, at, me, speed, mask, cx, cy, cz)
        ctl[k] = control[at]
    node_scales((own_numbers[...], far_numbers[...]), scal)
    for k, at in enumerate((3 * me, 1 + me)):
        own_of(k, at, decay, speed, scal, dg)


def prepare_next(core, scal, speed, mask, decay, control, own, far, _, s1_next, near, cx, cy, cz, dg):
    me = core[0]
    at = 2 - me
    fields_of(0, at, me, speed, mask, cx, cy, cz)
    own_of(0, at, decay, speed, scal, dg)
    near[...] = cx[0, 0]
    for j, c in enumerate((own, far)):
        a = rows_of(scal, j)
        value = c[0, at]
        l = a[0] * (cx[0, 0] * c[0, 1 + me] + cx[1, 0] * c[0, 3 - 3 * me]) + in_plane(value, a, cy, cz, 0) - dg[j, 0] * value
        s1_next[j] = value + time_step * (l + a[4] * control[at])


def prepare_back(core, goal, own_numbers, far_numbers, adjoint, _, weights, goals, adj, adj_out):
    me = core[0]
    weights[0] = own_numbers[...][0, 8] * (1.0 / weight_denominator)
    weights[1] = far_numbers[...][0, 8] * (1.0 / weight_denominator)
    for k, at in enumerate((3 * me, 1 + me)):
        goals[k] = goal[at].astype(jnp.float32)
        adj[k] = adjoint[0, at].astype(jnp.float32)
    adj_out[0] = adjoint[0, 3 - 3 * me].astype(jnp.float32)
    adj_out[1] = adjoint[0, 2 - me].astype(jnp.float32)


def first_stage(core, scal, own, far, cx, cy, cz, dg, ctl, base, base_q, s1_in):
    me = core[0]
    for j, c in enumerate((own, far)):
        a = rows_of(scal, j)
        c_o, c_i = c[0, 3 * me], c[0, 1 + me]
        push = [a[4] * ctl[k] for k in range(2)]
        l_i = a[0] * (cx[0, 1] * c_o + cx[1, 1] * c[0, 2 - me]) + in_plane(c_i, a, cy, cz, 1) - dg[j, 1] * c_i
        s1_i = c_i + time_step * (l_i + push[1])
        s1_in[j] = s1_i
        l_o = a[0] * (cx[1, 0] * c_i) + in_plane(c_o, a, cy, cz, 0) - dg[j, 0] * c_o
        base[j] = c_o + time_step * (l_o + push[0])
        base_q[j] = 0.75 * c_o + (0.25 * time_step) * (a[0] * (cx[1, 0] * s1_i) + push[0])


def first_edge(scal, halo, base, base_q, cx, cy, cz, dg, msg, s1_out):
    for j in range(2):
        a = rows_of(scal, j)
        s1_o = base[j] + (time_step * a[0]) * (cx[0, 0] * halo[1 - j])
        s1_out[j] = s1_o
        msg[j] = base_q[j] + 0.25 * (s1_o + time_step * (in_plane(s1_o, a, cy, cz, 0) - dg[j, 0] * s1_o))


def second_inner(core, scal, own, far, s1_out, s1_in, s1_next, cx, cy, cz, dg, ctl, s2_own, s2_far):
    for j, (c, out) in enumerate(((own, s2_own), (far, s2_far))):
        a = rows_of(scal, j)
        s1_i = s1_in[j]
        l_i = a[0] * (cx[0, 1] * s1_out[j] + cx[1, 1] * s1_next[j]) + in_plane(s1_i, a, cy, cz, 1) - dg[j, 1] * s1_i
        out[...] = 0.75 * c[0, 1 + core[0]] + 0.25 * (s1_i + time_step * (l_i + a[4] * ctl[1]))


def far_part(core, scal, own, far, halo, far_base, cx, step):
    for j, c in enumerate((own, far)):
        s1_h = far_base[1 - j] + (time_step * scal[j, 0]) * (halo[2] * c[0, 3 * core[0]])
        step[j] = (0.25 * time_step * scal[j, 0]) * (cx[0, 0] * s1_h)


def third_stage(core, scal, own, far, msg, s1_out, s2_own, s2_far, next_own, next_far, halo, step, cx, cy, cz, dg, ctl, base):
    me = core[0]
    parts = ((own, s2_own, next_own), (far, s2_far, next_far))
    for j, (c, s2, s2_next) in enumerate(parts):
        a = rows_of(scal, j)
        c_o, s2_i = c[0, 3 * me], s2[...]
        s2_o = msg[j] + step[j]
        back = (0.25 * time_step * a[0]) * (halo[2] * s1_out[j])
        l_o = a[0] * (cx[0, 0] * back + cx[1, 0] * s2_i) + in_plane(s2_o, a, cy, cz, 0) - dg[j, 0] * s2_o
        l_i = a[0] * (cx[0, 1] * s2_o + cx[1, 1] * s2_next[...]) + in_plane(s2_i, a, cy, cz, 1) - dg[j, 1] * s2_i
        base[j, 0] = c_o / 3.0 + 2.0 / 3.0 * (s2_o + time_step * (l_o + a[4] * ctl[0]))
        base[j, 1] = c[0, 1 + me] / 3.0 + 2.0 / 3.0 * (s2_i + time_step * (l_i + a[4] * ctl[1]))


def finals(j, scal, halo, base, cx):
    return base[j, 0] + (2.0 / 3.0 * time_step * scal[j, 0]) * (cx[0, 0] * halo[1 - j]), base[j, 1]


def turn(scal, weights, halo, base, cx, cy, cz, dg, goals, adj, after_far, final_own, final_far, term, msg, partial):
    final_own[0], final_own[1] = finals(0, scal, halo, base, cx)
    final_far[0], final_far[1] = finals(1, scal, halo, base, cx)
    first = [weights[0] * final_own[k] + weights[1] * final_far[k] for k in range(2)]
    for j, (final, after) in enumerate(((final_own, (adj[0], adj[1])), (final_far, (after_far[0], after_far[1])))):
        a = rows_of(scal, j)
        u = []
        for k in range(2):
            t = after[k] + goals[k] * weights[j] * (1.0 + 2.0 * variance_gain * (final[k] - first[k]))
            term[j, k] = t
            u.append(2.0 / 3.0 * t)
        msg[j, 0] = a[0] * (cx[0, 0] * u[0])
        spread = a[0] * (cx[0, 1] * u[1]) + in_plane_back(u[0], a, cy, cz, 0) - dg[j, 0] * u[0]
        value = u[0] + time_step * spread
        partial[j] = value
        msg[j, 1] = a[0] * (cx[0, 0] * value)


class Laid:
    def __init__(self, refs):
        self.left = [(ref, start) for ref in refs for start in range(0, ref.shape[0], 8)]

    def put(self, value):
        for start in range(0, value.shape[0], 8):
            ref, at = self.left.pop(0)
            ref[at : at + 8] = value[start : start + 8]


def get(refs, count, rows):
    whole = jnp.concatenate([ref[...] for ref in refs], 0)
    return [whole[rows * k : rows * k + rows] for k in range(count)] + [whole[rows * count :]]


def cut(rows, pieces):
    tiles = rows // 8
    return [8 * (tiles // pieces + (k < tiles % pieces)) for k in range(pieces)]


def turn_inner(scal, terms, cx, cy, cz, dg, part, *pins):
    laid = Laid(pins)
    for j in range(2):
        a = rows_of(scal, j)
        u = [2.0 / 3.0 * terms[j, k] for k in range(2)]
        laid.put(a[0] * (cx[1, 1] * u[1]))
        spread = a[0] * (cx[1, 0] * u[0]) + in_plane_back(u[1], a, cy, cz, 1) - dg[j, 1] * u[1]
        value = u[1] + time_step * spread
        part[j] = value
        laid.put(a[0] * (cx[1, 1] * value))


def goal_sum(weights, final_own, final_far, goals, _, cost):
    total = 0.0
    for k in range(2):
        own, far = weights[0] * final_own[k], weights[1] * final_far[k]
        first = own + far
        second = own * final_own[k] + far * final_far[k]
        total = total + goals[k] * (first + variance_gain * (second - first * first))
    rows, columns = total.shape
    total = sum(total[8 * r : 8 * r + 8] for r in range(rows // 8))
    cost[...] = sum(total[:, 128 * k : 128 * k + 128] for k in range(columns // 128))


def back_second(scal, msgs, partials, part, halo, near, cx, cy, cz, dg, *rest):
    base, a2 = rest[-2:]
    count, rows = (len(rest) - 2) // 2, msgs.shape[2]
    mine, theirs = get(rest[:count], 4, rows), get(rest[count:-2], 4, rows)
    for j in range(2):
        a = rows_of(scal, j)
        pin, pin2 = theirs[2 - 2 * j], theirs[3 - 2 * j]
        pin2 = 0.25 * (pin2 + (time_step * a[0]) * (near[...] * mine[2 * j]))
        a2_i = part[j] + time_step * pin
        a2[j] = a2_i
        u_o, u_i = 0.25 * partials[j], 0.25 * a2_i
        back = (0.25 * time_step * a[0]) * (halo[2] * msgs[j, 0])
        spread = a[0] * (cx[0, 1] * u_i) + in_plane_back(u_o, a, cy, cz, 0) - dg[j, 0] * u_o + back
        base[j, 0] = u_o + time_step * spread
        spread = a[0] * (cx[1, 0] * u_o) + in_plane_back(u_i, a, cy, cz, 1) - dg[j, 1] * u_i + pin2
        base[j, 1] = u_i + time_step * spread


def second_back_edge(scal, halo, base, cx, cy, cz, dg, a1, msg):
    for j in range(2):
        a = rows_of(scal, j)
        step = (0.25 * time_step) * halo[1 - j, 0]
        spread = in_plane_back(step, a, cy, cz, 0) - dg[j, 0] * step + 0.25 * halo[1 - j, 1]
        value = base[j, 0] + step + time_step * spread
        a1[j] = value
        msg[j] = a[0] * (cx[0, 0] * value)


def close(core, scal, terms, partials, halo, a1, a2, base, cx, cy, cz, dg, ctl, cost, cost_far, keep, part, give, total, *send):
    total[...] = cost[...] + cost_far[...]
    laid = Laid(send)
    sources = [0.0, 0.0]
    for j in range(2):
        a = rows_of(scal, j)
        first = halo[1 - j, 0]
        x = [a1[j], base[j, 1] + (0.25 * time_step * time_step * a[0]) * (cx[1, 0] * first)]
        a2_o = partials[j] + time_step * first
        for k, second in enumerate((a2_o, a2[j])):
            sources[k] = sources[k] + a[4] * (2.0 / 3.0 * terms[j, k] + 0.25 * second + x[k])
        spread = a[0] * (cx[0, 1] * x[1]) + in_plane_back(x[0], a, cy, cz, 0) - dg[j, 0] * x[0]
        outer = terms[j, 0] / 3.0 + 0.75 * a2_o + (x[0] + time_step * spread)
        spread = a[0] * (cx[1, 0] * x[0]) + in_plane_back(x[1], a, cy, cz, 1) - dg[j, 1] * x[1]
        inner = terms[j, 1] / 3.0 + 0.75 * a2[j] + (x[1] + time_step * spread)
        pin = a[0] * (cx[1, 1] * x[1])
        part[j] = outer
        if j == 0:
            part[2], part[3] = inner, pin
        else:
            laid.put(inner)
            laid.put(pin)
    half = ctl.shape[2] // 2
    zero = core[0] == 0
    for k in range(2):
        gradient = time_step * sources[k] + penalty * ctl[k]
        low, high = gradient[:, :half], gradient[:, half:]
        keep[k] = jnp.where(zero, low, high)
        give[k] = jnp.where(zero, high, low)


def combine(cost, cost_far, total):
    total[...] = cost[...] + cost_far[...]


def last_edge(halo, part, cost, cost_far, outer, give):
    rows = outer.shape[0]
    outer[...] = part[0] + time_step * halo[1]
    give[:rows] = part[1] + time_step * halo[0]
    give[rows:] = jnp.zeros((8, outer.shape[1]), jnp.float32)
    give[rows:, :128] = cost[...] + cost_far[...]


def write_inner(core, part, keep, taken, *rest):
    theirs, (out, gradient) = get(rest[:-2], 2, part.shape[1]), rest[-2:]
    me = core[0]
    out[0, 1 + me] = part[2] + time_step * theirs[1]
    out[0, 2 - me] = theirs[0] + time_step * part[3]
    gradient[3 * me] = keep[0]
    gradient[1 + me] = keep[1]
    gradient[3 - 3 * me] = taken[0]
    gradient[2 - me] = taken[1]


def write_outer(core, value, _, out, sem):
    copy = pltpu.make_async_copy(value, out.at[0, 3 * core[0]], sem)
    copy.start()
    copy.wait()


def finish(cells, core, mine, taken, _, out, objective, number, sems):
    rows = mine.shape[0] - 8
    copy = pltpu.make_async_copy(taken.at[:rows], out.at[0, 3 - 3 * core[0]], sems.at[0])
    copy.start()
    number[0] = jnp.sum(mine[rows:, :128] + taken[rows:, :128]) / cells
    result = pltpu.make_async_copy(number, objective, sems.at[1])
    result.start()
    copy.wait()
    result.wait()


def on_core(body, outs, scalars, arrays, hbm_out=(), smem_out=(), after=(), cost=0, name=None):
    hbm_out = tuple(hbm_out) + tuple(smem_out)
    out_shape = [
        jax.ShapeDtypeStruct(s, jnp.float32) if i in hbm_out else pltpu.VMEM(s, jnp.float32)
        for i, s in enumerate(outs)
    ]
    held = [pltpu.with_memory_space_constraint(x, pltpu.SMEM) for x in scalars]
    held += [pltpu.with_memory_space_constraint(x, pltpu.VMEM) for x in arrays]
    count, waits = len(held), len(after)

    def run(*refs):
        body(*refs[:count], *refs[count + waits :])

    return pl.pallas_call(
        run,
        out_shape=out_shape,
        in_specs=[pl.BlockSpec(memory_space=pltpu.SMEM)] * len(scalars)
        + [pl.BlockSpec(memory_space=pltpu.VMEM)] * len(arrays)
        + [pl.BlockSpec(memory_space=pl.ANY)] * waits,
        out_specs=[
            pl.BlockSpec(memory_space=pltpu.SMEM if i in smem_out else pltpu.VMEM) for i in range(len(outs))
        ],
        compiler_params=pltpu.CompilerParams(vmem_limit_bytes=VMEM_LIMIT),
        cost_estimate=cost_of(cost) if cost else None,
        name=name or body.__name__,
    )(*held, *after)


def shards(
    concentration,
    adjoint_next,
    speed,
    direction_mask,
    decay_rate,
    control,
    goal_weight,
    node_index,
    weight_num,
    step_index,
):
    sections = lax.axis_size("space")
    ranks = sections * lax.axis_size("node")
    within = [(i, i ^ 1) for i in range(ranks)]
    across = [p for i in range(1, ranks - 1, 2) for p in ((i, i + 1), (i + 1, i))]

    def swap(x, what):
        with jax.named_scope("swap_" + what):
            return lax.ppermute(x, AXES, within)

    def pass_on(x, what):
        with jax.named_scope("pass_" + what):
            return lax.ppermute(x, AXES, across)

    _, layers, rows, columns = concentration.shape
    me = lax.axis_index("node").astype(jnp.int32)
    core = jnp.reshape(me, (1,))
    far = swap(concentration, "state")
    plane = (rows, columns)
    pair, four_planes = (2,) + plane, (4,) + plane
    four = (2,) + pair
    sides = (2, rows, columns // 2)
    held = lambda x, space: pltpu.with_memory_space_constraint(x, space)
    (first,) = on_core(begin, [(8, 128)], [], [], cost=LONG)
    (packed,) = on_core(
        pack, [(3,) + plane], [core], [concentration, far, speed, direction_mask], after=[first]
    )
    halo = pass_on(packed, "state")
    numbers = pl.pallas_call(
        gather_numbers,
        out_shape=pltpu.VMEM((8, 128), jnp.float32),
        in_specs=[pl.BlockSpec(memory_space=pltpu.SMEM)] * 3 + [pl.BlockSpec(memory_space=pl.ANY)],
        out_specs=pl.BlockSpec(memory_space=pltpu.VMEM),
        name="gather_numbers",
    )(node_index, weight_num, step_index, packed)
    far_numbers = swap(numbers, "numbers")

    shapes = [four, four, four, four, pair]
    scal, cx, cy, cz, dg, ctl = pl.pallas_call(
        prepare,
        out_shape=[pltpu.SMEM((2, 8), jnp.float32)] + [pltpu.VMEM(s, jnp.float32) for s in shapes],
        in_specs=[pl.BlockSpec(memory_space=pltpu.SMEM)]
        + [pl.BlockSpec(memory_space=pltpu.VMEM)] * 6,
        out_specs=[pl.BlockSpec(memory_space=pltpu.SMEM)] + [pl.BlockSpec(memory_space=pltpu.VMEM)] * len(shapes),
        compiler_params=pltpu.CompilerParams(vmem_limit_bytes=VMEM_LIMIT),
        name="prepare",
    )(
        core,
        *[held(x, pltpu.VMEM) for x in (numbers, far_numbers, speed, direction_mask, decay_rate, control)],
    )
    fields = [cx, cy, cz, dg]
    both = [core, scal]
    states = [concentration, far]
    base, base_q, s1_in = on_core(first_stage, [pair] * 3, both, states + fields + [ctl])
    far_base = pass_on(base, "stage1")
    msg, s1_out = on_core(
        first_edge, [pair, pair], [scal], [halo, base, base_q] + fields, cost=LONG
    )
    halo2 = pass_on(msg, "stage2")
    weights, goals, adj, adj_out = pl.pallas_call(
        prepare_back,
        out_shape=[pltpu.SMEM((2,), jnp.float32)]
        + [pltpu.VMEM(s, jnp.float32) for s in (pair, pair, pair)],
        in_specs=[pl.BlockSpec(memory_space=pltpu.SMEM)]
        + [pl.BlockSpec(memory_space=pltpu.VMEM)] * 4
        + [pl.BlockSpec(memory_space=pl.ANY)],
        out_specs=[pl.BlockSpec(memory_space=pltpu.SMEM)] + [pl.BlockSpec(memory_space=pltpu.VMEM)] * 3,
        compiler_params=pltpu.CompilerParams(vmem_limit_bytes=VMEM_LIMIT),
        name="prepare_back",
    )(
        core,
        held(goal_weight, pltpu.HBM),
        *[held(x, pltpu.VMEM) for x in (numbers, far_numbers)],
        held(adjoint_next, pltpu.HBM),
        msg,
    )
    s1_next, near = pl.pallas_call(
        prepare_next,
        out_shape=[pltpu.VMEM(pair, jnp.float32), pltpu.VMEM(plane, jnp.float32)],
        in_specs=[pl.BlockSpec(memory_space=pltpu.SMEM)] * 2
        + [pl.BlockSpec(memory_space=pltpu.VMEM)] * 6
        + [pl.BlockSpec(memory_space=pl.ANY)],
        out_specs=[pl.BlockSpec(memory_space=pltpu.VMEM)] * 2,
        scratch_shapes=[pltpu.VMEM((2, 1) + plane, jnp.float32)] * 4,
        compiler_params=pltpu.CompilerParams(vmem_limit_bytes=VMEM_LIMIT),
        name="prepare_next",
    )(
        core,
        held(scal, pltpu.SMEM),
        *[held(x, pltpu.VMEM) for x in (speed, direction_mask, decay_rate, control)],
        *[held(x, pltpu.VMEM) for x in states],
        msg,
    )

    after = swap(adj_out, "after")

    (far_step,) = on_core(far_part, [pair], both, states + [halo, far_base, cx], cost=LONG)
    s2 = list(on_core(second_inner, [plane] * 2, both, states + [s1_out, s1_in, s1_next] + fields + [ctl]))
    s2_next = [swap(s2[1], "s2_far"), swap(s2[0], "s2_own")]
    (base,) = on_core(third_stage, [four], both, states + [msg, s1_out] + s2 + s2_next + [halo, far_step] + fields + [ctl])
    final_own, final_far, terms, msg3, partials = on_core(
        turn,
        [pair, pair, four, four, pair],
        [scal, weights],
        [halo2, base] + fields + [goals, adj, after],
    )
    halo3 = pass_on(msg3, "back2")
    part, *pins = on_core(
        turn_inner, [pair] + [(r, columns) for r in cut(4 * rows, 3)], [scal], [terms] + fields
    )
    (cost,) = on_core(goal_sum, [(8, 128)], [weights], [final_own, final_far, goals, part])
    whole = sections & (sections - 1) == 0
    steps = [1 << k for k in range(sections.bit_length() - 1)] if whole else []
    steps = steps[1:] + steps[:1]

    def from_pair(x, k):
        with jax.named_scope("goal_sum"):
            if k >= len(steps):
                return jnp.zeros_like(x)
            flip = 3 if steps[k] == 1 else 2 * steps[k]
            return lax.ppermute(x, AXES, [(i, i ^ flip) for i in range(ranks)])

    theirs = [swap(x, "pin") for x in pins]
    base, a2 = on_core(
        back_second,
        [four, pair],
        [scal],
        [msg3, partials, part, halo, near] + fields + pins + theirs,
    )
    (cost,) = on_core(combine, [(8, 128)], [], [cost, from_pair(cost, 0)], after=[a2])
    a1, msg4 = on_core(second_back_edge, [pair, pair], [scal], [halo3, base] + fields, after=[cost])
    halo4 = pass_on(msg4, "back1")
    keep, part, give, cost, *out = on_core(
        close,
        [sides, four_planes, sides, (8, 128)] + [(r, columns) for r in cut(2 * rows, 2)],
        both,
        [terms, partials, halo3, a1, a2, base] + fields + [ctl, cost, from_pair(cost, 1)],
        cost=2 * LONG,
    )
    parts = [swap(x, "adjoint") for x in out]
    taken = swap(give, "gradient")
    adjoint, gradient = on_core(
        write_inner,
        [(1, layers, rows, columns), (layers, rows, columns // 2)],
        [core],
        [part, keep, taken] + parts,
        hbm_out=(0, 1),
    )
    for k in range(2, len(steps) - 1):
        cost = cost + from_pair(cost, k)
    cost_far = from_pair(cost, max(2, len(steps) - 1))
    if not whole:
        cost = lax.psum(cost, "space")
    outer, give = on_core(
        last_edge,
        [plane, (rows + 8, columns)],
        [],
        [halo4, part, cost, cost_far],
        after=[held(adjoint, pltpu.HBM)],
        cost=LONG,
    )
    anywhere, in_smem = pl.BlockSpec(memory_space=pl.ANY), pl.BlockSpec(memory_space=pltpu.SMEM)
    adjoint = pl.pallas_call(
        write_outer,
        out_shape=jax.ShapeDtypeStruct(adjoint.shape, jnp.float32),
        in_specs=[in_smem, pl.BlockSpec(memory_space=pltpu.VMEM), anywhere],
        out_specs=anywhere,
        scratch_shapes=[pltpu.SemaphoreType.DMA],
        input_output_aliases={2: 0},
        compiler_params=pltpu.CompilerParams(vmem_limit_bytes=VMEM_LIMIT),
        name="write_outer",
    )(held(core, pltpu.SMEM), held(outer, pltpu.VMEM), held(adjoint, pltpu.HBM))
    adjoint, objective = pl.pallas_call(
        functools.partial(finish, sections * layers * rows * columns),
        out_shape=[jax.ShapeDtypeStruct(adjoint.shape, jnp.float32), jax.ShapeDtypeStruct((1,), jnp.float32)],
        in_specs=[in_smem] + [pl.BlockSpec(memory_space=pltpu.VMEM)] * 2 + [anywhere],
        out_specs=[anywhere] * 2,
        scratch_shapes=[pltpu.SMEM((1,), jnp.float32), pltpu.SemaphoreType.DMA((2,))],
        input_output_aliases={3: 0},
        compiler_params=pltpu.CompilerParams(vmem_limit_bytes=VMEM_LIMIT),
        name="finish",
    )(
        held(core, pltpu.SMEM),
        *[held(x, pltpu.VMEM) for x in (give, swap(give, "outer"))],
        held(adjoint, pltpu.HBM),
    )
    return (adjoint, gradient, objective)


def solution(mesh):
    return jax.shard_map(
        shards,
        mesh=mesh,
        in_specs=(
            P("node", ("groups", "space"), None, None),
            P("node", ("groups", "space"), None, None),
            P(None, ("groups", "space"), None, None),
            P(None, ("groups", "space"), None, None),
            P(("groups", "space"), None, None),
            P(("groups", "space"), None, None),
            P(("groups", "space"), None, None),
            P("node", None),
            P("node"),
            P("groups"),
        ),
        out_specs=(
            P("node", ("groups", "space"), None, None),
            P(("groups", "space"), None, "node"),
            P("groups"),
        ),
        check_vma=False,
    )
```

```python
import functools
import math

import jax
import jax.numpy as jnp
from jax import lax
from jax.experimental import pallas as pl
from jax.experimental.pallas import tpu as pltpu
from jax.sharding import PartitionSpec as P

time_step = 0.6
variance_gain = 0.5
penalty = 0.1
weight_denominator = 16.0

VMEM_LIMIT = 8 * 1024 * 1024
AXES = ("space", "node")
LONG = 8


def cost_of(us):
    return pl.CostEstimate(flops=us * 1_000_000_000, bytes_accessed=us * 3_000_000, transcendentals=0)


def roll(value, steps, axis):
    return pltpu.roll(value, steps % value.shape[axis], axis)


def in_plane(value, a, cy, cz, k):
    return a[1] * (cy[0, k] * roll(value, 1, 0) + cy[1, k] * roll(value, -1, 0)) + a[2] * (
        cz[0, k] * roll(value, 1, 1) + cz[1, k] * roll(value, -1, 1)
    )


def in_plane_back(value, a, cy, cz, k):
    return a[1] * (roll(cy[0, k] * value, -1, 0) + roll(cy[1, k] * value, 1, 0)) + a[2] * (
        roll(cz[0, k] * value, -1, 1) + roll(cz[1, k] * value, 1, 1)
    )


def rows_of(scal, j):
    return [scal[j, k] for k in range(5)]


def pick(values, index):
    result = jnp.float32(values[-1])
    for k, value in enumerate(values[:-1]):
        result = jnp.where(index == k, jnp.float32(value), result)
    return result


def node_scales(tiles, scal):
    levels = [-math.cos(math.pi * k / 8.0) for k in range(9)]
    step = tiles[0][0, 8].astype(jnp.int32)
    half = step & 31
    wave = pick([math.sin(2.0 * math.pi * k / 64.0) for k in range(17)], jnp.minimum(half, 32 - half))
    phase = 1.0 + jnp.where(step < 32, 0.5, -0.5) * wave
    for j, tile in enumerate(tiles):
        p = {k: pick(levels, tile[0, k]) for k in (0, 1, 2, 4, 6, 7)}
        scal[j, 0] = 1.0 + 0.3 * p[0]
        scal[j, 1] = 1.0 + 0.3 * p[1]
        scal[j, 2] = (1.0 + 0.3 * p[2]) * (1.0 + 0.2 * p[7])
        scal[j, 3] = pick([math.exp(0.5 * p) for p in levels], tile[0, 3]) * pick(
            [math.exp(0.25 * p) for p in levels], tile[0, 5]
        )
        scal[j, 4] = (1.0 + 0.3 * p[4] + 0.2 * p[6]) * phase


def expand(bits, columns):
    blocks = bits.shape[1]
    spread = (
        lax.broadcasted_iota(jnp.int32, (blocks, columns), 1) // (columns // blocks)
        == lax.broadcasted_iota(jnp.int32, (blocks, columns), 0)
    ).astype(jnp.bfloat16)
    return jnp.dot(bits.astype(jnp.float32).astype(jnp.bfloat16), spread, preferred_element_type=jnp.float32)


def toward_outer(up, me):
    flip = (me == 1).astype(jnp.float32)
    return up + flip - 2.0 * flip * up


def begin(out):
    out[...] = jnp.zeros_like(out)


def gather_numbers(index, step, _, numbers):
    lane = lax.broadcasted_iota(jnp.int32, numbers.shape, 1)
    value = jnp.zeros(numbers.shape, jnp.int32)
    for k, number in enumerate([index[0, k] for k in range(index.shape[1])] + [step[0]]):
        value = jnp.where(lane == k, number, value)
    numbers[...] = value.astype(jnp.float32)


def pack(core, own, far, speed, mask, out):
    at = 3 * core[0]
    out[0] = own[0, at]
    out[1] = far[0, at]
    out[2] = speed[0, at].astype(jnp.float32) * toward_outer(expand(mask[0, at], speed.shape[3]), core[0])


def fields_of(k, at, me, speeds, masks, cx, cy, cz):
    rows, columns = speeds.shape[2:]
    row = lax.broadcasted_iota(jnp.int32, (rows, columns), 0)
    column = lax.broadcasted_iota(jnp.int32, (rows, columns), 1)
    up = [expand(masks[d, at], columns) for d in range(3)]
    s = [speeds[d, at].astype(jnp.float32) for d in range(3)]
    outer = s[0] * toward_outer(up[0], me)
    cx[0, k] = outer
    cx[1, k] = s[0] - outer
    lower = s[1] * up[1]
    cy[0, k] = jnp.where(row == 0, 0.0, lower)
    cy[1, k] = jnp.where(row == rows - 1, 0.0, s[1] - lower)
    lower = s[2] * up[2]
    cz[0, k] = jnp.where(column == 0, 0.0, lower)
    cz[1, k] = jnp.where(column == columns - 1, 0.0, s[2] - lower)


def own_of(k, at, rates, speeds, scal, dg):
    s = [speeds[d, at].astype(jnp.float32) for d in range(3)] + [rates[at].astype(jnp.float32)]
    for j in range(2):
        dg[j, k] = sum(scal[j, d] * s[d] for d in range(4))


def prepare(core, own_numbers, far_numbers, speed, mask, decay, control, scal, cx, cy, cz, dg, ctl):
    me = core[0]
    for k, at in enumerate((3 * me, 1 + me)):
        fields_of(k, at, me, speed, mask, cx, cy, cz)
        ctl[k] = control[at]
    node_scales((own_numbers[...], far_numbers[...]), scal)
    for k, at in enumerate((3 * me, 1 + me)):
        own_of(k, at, decay, speed, scal, dg)


def prepare_next(core, scal, speed, mask, decay, control, own, far, _, s1_next, near, cx, cy, cz, dg):
    me = core[0]
    at = 2 - me
    fields_of(0, at, me, speed, mask, cx, cy, cz)
    own_of(0, at, decay, speed, scal, dg)
    near[...] = cx[0, 0]
    for j, c in enumerate((own, far)):
        a = rows_of(scal, j)
        value = c[0, at]
        l = a[0] * (cx[0, 0] * c[0, 1 + me] + cx[1, 0] * c[0, 3 - 3 * me]) + in_plane(value, a, cy, cz, 0) - dg[j, 0] * value
        s1_next[j] = value + time_step * (l + a[4] * control[at])


def prepare_back(core, own_weight, far_weight, goal, adjoint, _, weights, goals, adj, adj_out):
    me = core[0]
    weights[0] = own_weight[0].astype(jnp.float32) * (1.0 / weight_denominator)
    weights[1] = far_weight[0].astype(jnp.float32) * (1.0 / weight_denominator)
    for k, at in enumerate((3 * me, 1 + me)):
        goals[k] = goal[at].astype(jnp.float32)
        adj[k] = adjoint[0, at].astype(jnp.float32)
    adj_out[0] = adjoint[0, 3 - 3 * me].astype(jnp.float32)
    adj_out[1] = adjoint[0, 2 - me].astype(jnp.float32)


def first_stage(core, scal, own, far, cx, cy, cz, dg, ctl, base, base_q, s1_in):
    me = core[0]
    for j, c in enumerate((own, far)):
        a = rows_of(scal, j)
        c_o, c_i = c[0, 3 * me], c[0, 1 + me]
        push = [a[4] * ctl[k] for k in range(2)]
        l_i = a[0] * (cx[0, 1] * c_o + cx[1, 1] * c[0, 2 - me]) + in_plane(c_i, a, cy, cz, 1) - dg[j, 1] * c_i
        s1_i = c_i + time_step * (l_i + push[1])
        s1_in[j] = s1_i
        l_o = a[0] * (cx[1, 0] * c_i) + in_plane(c_o, a, cy, cz, 0) - dg[j, 0] * c_o
        base[j] = c_o + time_step * (l_o + push[0])
        base_q[j] = 0.75 * c_o + (0.25 * time_step) * (a[0] * (cx[1, 0] * s1_i) + push[0])


def first_edge(scal, halo, base, base_q, cx, cy, cz, dg, msg, s1_out):
    for j in range(2):
        a = rows_of(scal, j)
        s1_o = base[j] + (time_step * a[0]) * (cx[0, 0] * halo[1 - j])
        s1_out[j] = s1_o
        msg[j] = base_q[j] + 0.25 * (s1_o + time_step * (in_plane(s1_o, a, cy, cz, 0) - dg[j, 0] * s1_o))


def second_inner(core, scal, own, far, s1_out, s1_in, s1_next, cx, cy, cz, dg, ctl, s2_own, s2_far):
    for j, (c, out) in enumerate(((own, s2_own), (far, s2_far))):
        a = rows_of(scal, j)
        s1_i = s1_in[j]
        l_i = a[0] * (cx[0, 1] * s1_out[j] + cx[1, 1] * s1_next[j]) + in_plane(s1_i, a, cy, cz, 1) - dg[j, 1] * s1_i
        out[...] = 0.75 * c[0, 1 + core[0]] + 0.25 * (s1_i + time_step * (l_i + a[4] * ctl[1]))


def far_part(core, scal, own, far, halo, far_base, cx, step):
    for j, c in enumerate((own, far)):
        s1_h = far_base[1 - j] + (time_step * scal[j, 0]) * (halo[2] * c[0, 3 * core[0]])
        step[j] = (0.25 * time_step * scal[j, 0]) * (cx[0, 0] * s1_h)


def third_stage(core, scal, own, far, msg, s1_out, s2_own, s2_far, next_own, next_far, halo, step, cx, cy, cz, dg, ctl, base):
    me = core[0]
    parts = ((own, s2_own, next_own), (far, s2_far, next_far))
    for j, (c, s2, s2_next) in enumerate(parts):
        a = rows_of(scal, j)
        c_o, s2_i = c[0, 3 * me], s2[...]
        s2_o = msg[j] + step[j]
        back = (0.25 * time_step * a[0]) * (halo[2] * s1_out[j])
        l_o = a[0] * (cx[0, 0] * back + cx[1, 0] * s2_i) + in_plane(s2_o, a, cy, cz, 0) - dg[j, 0] * s2_o
        l_i = a[0] * (cx[0, 1] * s2_o + cx[1, 1] * s2_next[...]) + in_plane(s2_i, a, cy, cz, 1) - dg[j, 1] * s2_i
        base[j, 0] = c_o / 3.0 + 2.0 / 3.0 * (s2_o + time_step * (l_o + a[4] * ctl[0]))
        base[j, 1] = c[0, 1 + me] / 3.0 + 2.0 / 3.0 * (s2_i + time_step * (l_i + a[4] * ctl[1]))


def finals(j, scal, halo, base, cx):
    return base[j, 0] + (2.0 / 3.0 * time_step * scal[j, 0]) * (cx[0, 0] * halo[1 - j]), base[j, 1]


def turn(scal, weights, halo, base, cx, cy, cz, dg, goals, adj, after_far, final_own, final_far, term, msg, partial):
    final_own[0], final_own[1] = finals(0, scal, halo, base, cx)
    final_far[0], final_far[1] = finals(1, scal, halo, base, cx)
    first = [weights[0] * final_own[k] + weights[1] * final_far[k] for k in range(2)]
    for j, (final, after) in enumerate(((final_own, (adj[0], adj[1])), (final_far, (after_far[0], after_far[1])))):
        a = rows_of(scal, j)
        u = []
        for k in range(2):
            t = after[k] + goals[k] * weights[j] * (1.0 + 2.0 * variance_gain * (final[k] - first[k]))
            term[j, k] = t
            u.append(2.0 / 3.0 * t)
        msg[j, 0] = a[0] * (cx[0, 0] * u[0])
        spread = a[0] * (cx[0, 1] * u[1]) + in_plane_back(u[0], a, cy, cz, 0) - dg[j, 0] * u[0]
        value = u[0] + time_step * spread
        partial[j] = value
        msg[j, 1] = a[0] * (cx[0, 0] * value)


class Laid:
    def __init__(self, refs):
        self.left = [(ref, start) for ref in refs for start in range(0, ref.shape[0], 8)]

    def put(self, value):
        for start in range(0, value.shape[0], 8):
            ref, at = self.left.pop(0)
            ref[at : at + 8] = value[start : start + 8]


def get(refs, count, rows):
    whole = jnp.concatenate([ref[...] for ref in refs], 0)
    return [whole[rows * k : rows * k + rows] for k in range(count)] + [whole[rows * count :]]


def cut(rows, pieces):
    tiles = rows // 8
    return [8 * (tiles // pieces + (k < tiles % pieces)) for k in range(pieces)]


def turn_inner(scal, terms, cx, cy, cz, dg, part, *pins):
    laid = Laid(pins)
    for j in range(2):
        a = rows_of(scal, j)
        u = [2.0 / 3.0 * terms[j, k] for k in range(2)]
        laid.put(a[0] * (cx[1, 1] * u[1]))
        spread = a[0] * (cx[1, 0] * u[0]) + in_plane_back(u[1], a, cy, cz, 1) - dg[j, 1] * u[1]
        value = u[1] + time_step * spread
        part[j] = value
        laid.put(a[0] * (cx[1, 1] * value))


def goal_sum(weights, final_own, final_far, goals, _, cost):
    total = 0.0
    for k in range(2):
        own, far = weights[0] * final_own[k], weights[1] * final_far[k]
        first = own + far
        second = own * final_own[k] + far * final_far[k]
        total = total + goals[k] * (first + variance_gain * (second - first * first))
    rows, columns = total.shape
    total = sum(total[8 * r : 8 * r + 8] for r in range(rows // 8))
    cost[...] = sum(total[:, 128 * k : 128 * k + 128] for k in range(columns // 128))


def back_second(scal, msgs, partials, part, halo, near, cx, cy, cz, dg, *rest):
    base, a2 = rest[-2:]
    count, rows = (len(rest) - 2) // 2, msgs.shape[2]
    mine, theirs = get(rest[:count], 4, rows), get(rest[count:-2], 4, rows)
    for j in range(2):
        a = rows_of(scal, j)
        pin, pin2 = theirs[2 - 2 * j], theirs[3 - 2 * j]
        pin2 = 0.25 * (pin2 + (time_step * a[0]) * (near[...] * mine[2 * j]))
        a2_i = part[j] + time_step * pin
        a2[j] = a2_i
        u_o, u_i = 0.25 * partials[j], 0.25 * a2_i
        back = (0.25 * time_step * a[0]) * (halo[2] * msgs[j, 0])
        spread = a[0] * (cx[0, 1] * u_i) + in_plane_back(u_o, a, cy, cz, 0) - dg[j, 0] * u_o + back
        base[j, 0] = u_o + time_step * spread
        spread = a[0] * (cx[1, 0] * u_o) + in_plane_back(u_i, a, cy, cz, 1) - dg[j, 1] * u_i + pin2
        base[j, 1] = u_i + time_step * spread


def second_back_edge(scal, halo, base, cx, cy, cz, dg, a1, msg):
    for j in range(2):
        a = rows_of(scal, j)
        step = (0.25 * time_step) * halo[1 - j, 0]
        spread = in_plane_back(step, a, cy, cz, 0) - dg[j, 0] * step + 0.25 * halo[1 - j, 1]
        value = base[j, 0] + step + time_step * spread
        a1[j] = value
        msg[j] = a[0] * (cx[0, 0] * value)


def close(core, scal, terms, partials, halo, a1, a2, base, cx, cy, cz, dg, ctl, cost, cost_far, keep, part, give, total, *send):
    total[...] = cost[...] + cost_far[...]
    laid = Laid(send)
    sources = [0.0, 0.0]
    for j in range(2):
        a = rows_of(scal, j)
        first = halo[1 - j, 0]
        x = [a1[j], base[j, 1] + (0.25 * time_step * time_step * a[0]) * (cx[1, 0] * first)]
        a2_o = partials[j] + time_step * first
        for k, second in enumerate((a2_o, a2[j])):
            sources[k] = sources[k] + a[4] * (2.0 / 3.0 * terms[j, k] + 0.25 * second + x[k])
        spread = a[0] * (cx[0, 1] * x[1]) + in_plane_back(x[0], a, cy, cz, 0) - dg[j, 0] * x[0]
        outer = terms[j, 0] / 3.0 + 0.75 * a2_o + (x[0] + time_step * spread)
        spread = a[0] * (cx[1, 0] * x[0]) + in_plane_back(x[1], a, cy, cz, 1) - dg[j, 1] * x[1]
        inner = terms[j, 1] / 3.0 + 0.75 * a2[j] + (x[1] + time_step * spread)
        pin = a[0] * (cx[1, 1] * x[1])
        part[j] = outer
        if j == 0:
            part[2], part[3] = inner, pin
        else:
            laid.put(inner)
            laid.put(pin)
    half = ctl.shape[2] // 2
    zero = core[0] == 0
    for k in range(2):
        gradient = time_step * sources[k] + penalty * ctl[k]
        low, high = gradient[:, :half], gradient[:, half:]
        keep[k] = jnp.where(zero, low, high)
        give[k] = jnp.where(zero, high, low)


def combine(cost, cost_far, total):
    total[...] = cost[...] + cost_far[...]


def last_edge(halo, part, cost, cost_far, outer, give):
    rows = outer.shape[0]
    outer[...] = part[0] + time_step * halo[1]
    give[:rows] = part[1] + time_step * halo[0]
    give[rows:] = jnp.zeros((8, outer.shape[1]), jnp.float32)
    give[rows:, :128] = cost[...] + cost_far[...]


def write_inner(core, part, keep, taken, *rest):
    theirs, (out, gradient) = get(rest[:-2], 2, part.shape[1]), rest[-2:]
    me = core[0]
    out[0, 1 + me] = part[2] + time_step * theirs[1]
    out[0, 2 - me] = theirs[0] + time_step * part[3]
    gradient[3 * me] = keep[0]
    gradient[1 + me] = keep[1]
    gradient[3 - 3 * me] = taken[0]
    gradient[2 - me] = taken[1]


def write_outer(core, value, _, out, sem):
    copy = pltpu.make_async_copy(value, out.at[0, 3 * core[0]], sem)
    copy.start()
    copy.wait()


def finish(cells, core, mine, taken, _, out, objective, number, sems):
    rows = mine.shape[0] - 8
    copy = pltpu.make_async_copy(taken.at[:rows], out.at[0, 3 - 3 * core[0]], sems.at[0])
    copy.start()
    number[0] = jnp.sum(mine[rows:, :128] + taken[rows:, :128]) / cells
    result = pltpu.make_async_copy(number, objective, sems.at[1])
    result.start()
    copy.wait()
    result.wait()


def on_core(body, outs, scalars, arrays, hbm_out=(), smem_out=(), after=(), cost=0, name=None):
    hbm_out = tuple(hbm_out) + tuple(smem_out)
    out_shape = [
        jax.ShapeDtypeStruct(s, jnp.float32) if i in hbm_out else pltpu.VMEM(s, jnp.float32)
        for i, s in enumerate(outs)
    ]
    held = [pltpu.with_memory_space_constraint(x, pltpu.SMEM) for x in scalars]
    held += [pltpu.with_memory_space_constraint(x, pltpu.VMEM) for x in arrays]
    count, waits = len(held), len(after)

    def run(*refs):
        body(*refs[:count], *refs[count + waits :])

    return pl.pallas_call(
        run,
        out_shape=out_shape,
        in_specs=[pl.BlockSpec(memory_space=pltpu.SMEM)] * len(scalars)
        + [pl.BlockSpec(memory_space=pltpu.VMEM)] * len(arrays)
        + [pl.BlockSpec(memory_space=pl.ANY)] * waits,
        out_specs=[
            pl.BlockSpec(memory_space=pltpu.SMEM if i in smem_out else pltpu.VMEM) for i in range(len(outs))
        ],
        compiler_params=pltpu.CompilerParams(vmem_limit_bytes=VMEM_LIMIT),
        cost_estimate=cost_of(cost) if cost else None,
        name=name or body.__name__,
    )(*held, *after)


def shards(
    concentration,
    adjoint_next,
    speed,
    direction_mask,
    decay_rate,
    control,
    goal_weight,
    node_index,
    weight_num,
    step_index,
):
    sections = lax.axis_size("space")
    ranks = sections * lax.axis_size("node")
    within = [(i, i ^ 1) for i in range(ranks)]
    across = [p for i in range(1, ranks - 1, 2) for p in ((i, i + 1), (i + 1, i))]

    def swap(x, what):
        with jax.named_scope("swap_" + what):
            return lax.ppermute(x, AXES, within)

    def pass_on(x, what):
        with jax.named_scope("pass_" + what):
            return lax.ppermute(x, AXES, across)

    _, layers, rows, columns = concentration.shape
    me = lax.axis_index("node").astype(jnp.int32)
    core = jnp.reshape(me, (1,))
    far = swap(concentration, "state")
    plane = (rows, columns)
    pair, four_planes = (2,) + plane, (4,) + plane
    four = (2,) + pair
    sides = (2, rows, columns // 2)
    held = lambda x, space: pltpu.with_memory_space_constraint(x, space)
    (first,) = on_core(begin, [(8, 128)], [], [], cost=LONG)
    (packed,) = on_core(
        pack, [(3,) + plane], [core], [concentration, far, speed, direction_mask], after=[first]
    )
    halo = pass_on(packed, "state")
    numbers = pl.pallas_call(
        gather_numbers,
        out_shape=pltpu.VMEM((8, 128), jnp.float32),
        in_specs=[pl.BlockSpec(memory_space=pltpu.SMEM)] * 2 + [pl.BlockSpec(memory_space=pl.ANY)],
        out_specs=pl.BlockSpec(memory_space=pltpu.VMEM),
        name="gather_numbers",
    )(node_index, step_index, packed)
    far_numbers = swap(numbers, "numbers")

    shapes = [four, four, four, four, pair]
    scal, cx, cy, cz, dg, ctl = pl.pallas_call(
        prepare,
        out_shape=[pltpu.SMEM((2, 8), jnp.float32)] + [pltpu.VMEM(s, jnp.float32) for s in shapes],
        in_specs=[pl.BlockSpec(memory_space=pltpu.SMEM)]
        + [pl.BlockSpec(memory_space=pltpu.VMEM)] * 6,
        out_specs=[pl.BlockSpec(memory_space=pltpu.SMEM)] + [pl.BlockSpec(memory_space=pltpu.VMEM)] * len(shapes),
        compiler_params=pltpu.CompilerParams(vmem_limit_bytes=VMEM_LIMIT),
        name="prepare",
    )(
        core,
        *[held(x, pltpu.VMEM) for x in (numbers, far_numbers, speed, direction_mask, decay_rate, control)],
    )
    fields = [cx, cy, cz, dg]
    both = [core, scal]
    states = [concentration, far]
    base, base_q, s1_in = on_core(first_stage, [pair] * 3, both, states + fields + [ctl])
    far_base = pass_on(base, "stage1")
    msg, s1_out = on_core(
        first_edge, [pair, pair], [scal], [halo, base, base_q] + fields, cost=LONG
    )
    halo2 = pass_on(msg, "stage2")
    weights, goals, adj, adj_out = pl.pallas_call(
        prepare_back,
        out_shape=[pltpu.SMEM((2,), jnp.float32)]
        + [pltpu.VMEM(s, jnp.float32) for s in (pair, pair, pair)],
        in_specs=[pl.BlockSpec(memory_space=pltpu.SMEM)] * 3
        + [pl.BlockSpec(memory_space=pltpu.VMEM)] * 2
        + [pl.BlockSpec(memory_space=pl.ANY)],
        out_specs=[pl.BlockSpec(memory_space=pltpu.SMEM)] + [pl.BlockSpec(memory_space=pltpu.VMEM)] * 3,
        compiler_params=pltpu.CompilerParams(vmem_limit_bytes=VMEM_LIMIT),
        name="prepare_back",
    )(
        core,
        weight_num,
        swap(weight_num, "weight_num"),
        held(goal_weight, pltpu.HBM),
        held(adjoint_next, pltpu.HBM),
        msg,
    )
    s1_next, near = pl.pallas_call(
        prepare_next,
        out_shape=[pltpu.VMEM(pair, jnp.float32), pltpu.VMEM(plane, jnp.float32)],
        in_specs=[pl.BlockSpec(memory_space=pltpu.SMEM)] * 2
        + [pl.BlockSpec(memory_space=pltpu.VMEM)] * 6
        + [pl.BlockSpec(memory_space=pl.ANY)],
        out_specs=[pl.BlockSpec(memory_space=pltpu.VMEM)] * 2,
        scratch_shapes=[pltpu.VMEM((2, 1) + plane, jnp.float32)] * 4,
        compiler_params=pltpu.CompilerParams(vmem_limit_bytes=VMEM_LIMIT),
        name="prepare_next",
    )(
        core,
        held(scal, pltpu.SMEM),
        *[held(x, pltpu.VMEM) for x in (speed, direction_mask, decay_rate, control)],
        *[held(x, pltpu.VMEM) for x in states],
        msg,
    )

    after = swap(adj_out, "after")

    (far_step,) = on_core(far_part, [pair], both, states + [halo, far_base, cx], cost=LONG)
    s2 = list(on_core(second_inner, [plane] * 2, both, states + [s1_out, s1_in, s1_next] + fields + [ctl]))
    s2_next = [swap(s2[1], "s2_far"), swap(s2[0], "s2_own")]
    (base,) = on_core(third_stage, [four], both, states + [msg, s1_out] + s2 + s2_next + [halo, far_step] + fields + [ctl])
    final_own, final_far, terms, msg3, partials = on_core(
        turn,
        [pair, pair, four, four, pair],
        [scal, weights],
        [halo2, base] + fields + [goals, adj, after],
    )
    halo3 = pass_on(msg3, "back2")
    part, *pins = on_core(
        turn_inner, [pair] + [(r, columns) for r in cut(4 * rows, 3)], [scal], [terms] + fields
    )
    (cost,) = on_core(goal_sum, [(8, 128)], [weights], [final_own, final_far, goals, part])
    whole = sections & (sections - 1) == 0
    steps = [1 << k for k in range(sections.bit_length() - 1)] if whole else []
    steps = steps[1:] + steps[:1]

    def from_pair(x, k):
        with jax.named_scope("goal_sum"):
            if k >= len(steps):
                return jnp.zeros_like(x)
            flip = 3 if steps[k] == 1 else 2 * steps[k]
            return lax.ppermute(x, AXES, [(i, i ^ flip) for i in range(ranks)])

    theirs = [swap(x, "pin") for x in pins]
    base, a2 = on_core(
        back_second,
        [four, pair],
        [scal],
        [msg3, partials, part, halo, near] + fields + pins + theirs,
    )
    (cost,) = on_core(combine, [(8, 128)], [], [cost, from_pair(cost, 0)], after=[a2])
    a1, msg4 = on_core(second_back_edge, [pair, pair], [scal], [halo3, base] + fields, after=[cost])
    halo4 = pass_on(msg4, "back1")
    keep, part, give, cost, *out = on_core(
        close,
        [sides, four_planes, sides, (8, 128)] + [(r, columns) for r in cut(2 * rows, 2)],
        both,
        [terms, partials, halo3, a1, a2, base] + fields + [ctl, cost, from_pair(cost, 1)],
        cost=2 * LONG,
    )
    parts = [swap(x, "adjoint") for x in out]
    taken = swap(give, "gradient")
    adjoint, gradient = on_core(
        write_inner,
        [(1, layers, rows, columns), (layers, rows, columns // 2)],
        [core],
        [part, keep, taken] + parts,
        hbm_out=(0, 1),
    )
    for k in range(2, len(steps) - 1):
        cost = cost + from_pair(cost, k)
    cost_far = from_pair(cost, max(2, len(steps) - 1))
    if not whole:
        cost = lax.psum(cost, "space")
    outer, give = on_core(
        last_edge,
        [plane, (rows + 8, columns)],
        [],
        [halo4, part, cost, cost_far],
        after=[held(adjoint, pltpu.HBM)],
        cost=LONG,
    )
    anywhere, in_smem = pl.BlockSpec(memory_space=pl.ANY), pl.BlockSpec(memory_space=pltpu.SMEM)
    adjoint = pl.pallas_call(
        write_outer,
        out_shape=jax.ShapeDtypeStruct(adjoint.shape, jnp.float32),
        in_specs=[in_smem, pl.BlockSpec(memory_space=pltpu.VMEM), anywhere],
        out_specs=anywhere,
        scratch_shapes=[pltpu.SemaphoreType.DMA],
        input_output_aliases={2: 0},
        compiler_params=pltpu.CompilerParams(vmem_limit_bytes=VMEM_LIMIT),
        name="write_outer",
    )(held(core, pltpu.SMEM), held(outer, pltpu.VMEM), held(adjoint, pltpu.HBM))
    adjoint, objective = pl.pallas_call(
        functools.partial(finish, sections * layers * rows * columns),
        out_shape=[jax.ShapeDtypeStruct(adjoint.shape, jnp.float32), jax.ShapeDtypeStruct((1,), jnp.float32)],
        in_specs=[in_smem] + [pl.BlockSpec(memory_space=pltpu.VMEM)] * 2 + [anywhere],
        out_specs=[anywhere] * 2,
        scratch_shapes=[pltpu.SMEM((1,), jnp.float32), pltpu.SemaphoreType.DMA((2,))],
        input_output_aliases={3: 0},
        compiler_params=pltpu.CompilerParams(vmem_limit_bytes=VMEM_LIMIT),
        name="finish",
    )(
        held(core, pltpu.SMEM),
        *[held(x, pltpu.VMEM) for x in (give, swap(give, "outer"))],
        held(adjoint, pltpu.HBM),
    )
    return (adjoint, gradient, objective)


def solution(mesh):
    return jax.shard_map(
        shards,
        mesh=mesh,
        in_specs=(
            P("node", ("groups", "space"), None, None),
            P("node", ("groups", "space"), None, None),
            P(None, ("groups", "space"), None, None),
            P(None, ("groups", "space"), None, None),
            P(("groups", "space"), None, None),
            P(("groups", "space"), None, None),
            P(("groups", "space"), None, None),
            P("node", None),
            P("node"),
            P("groups"),
        ),
        out_specs=(
            P("node", ("groups", "space"), None, None),
            P(("groups", "space"), None, "node"),
            P("groups"),
        ),
        check_vma=False,
    )
```
